32 devices in a mesh: groups: 2 (over y), dp: 4 (over z), mp: 2 (over x), rep: 2 (over core).
Axes of the slice: x: 2, y: 2, z: 4, core: 2. Of those that a mesh axis runs over, the one named last changes fastest.
Arguments:
- query_ids: int32 [16384], P(('groups', 'dp', 'rep')), parts along dimension 0, may hold values from 0 to 128255
- query_delta: bfloat16 [16384, 4096], P(('groups', 'dp', 'rep'), 'mp'), parts along dimension 0, may hold values from -6 to 6
- doc_lengths: int32 [16, 128], P(('groups', 'dp', 'rep')), parts along dimension 0, may hold values from 1 to 32, 1024 in all within a row
- vocab_factor: bfloat16 [128256, 64], P('mp'), may hold values from -6 to 6
- output_factor: bfloat16 [4096, 64], P('mp'), may hold values from -0.09375 to 0.09375
- train_grads: bfloat16 [4096, 4096], P(('groups', 'dp'), 'mp'), parts along dimension 0, as said below
Outputs:
- scores: bfloat16 [4096, 4, 2, 128], P(('groups', 'dp', 'mp'), None, 'rep'), parts along dimension 0
The draws below stay inside these ranges and needn't reach their ends.
There are 2 independent parts, one for each index of `groups`. The reference program is written for one: setup_inputs(seed, part) draws one part's arguments, and reference() takes and returns one part's arrays. A program takes and returns all parts, laid end to end along the dimension named above; an argument that names none is the same for every part. Nothing has to cross between parts.
Inputs may be any that keep to these rules, and one draw needn't show every extreme that they name: `doc_lengths`: in each row the lengths sum to 1024. `train_grads`: coordinates ordered as 64 model-width-side indices by 64 vocabulary-side indices.
All inputs are finite; a program needn't handle non-finite values.
Results may differ from the reference program's by a relative error of at most 0.012.
The reference program's roundings to bfloat16 on the way count: a program that leaves them out, or rounds other values in their place, can miss the bound.
Values may be sent and summed in bfloat16 or wider, within the bound.
No kernel may reach another device: no remote copies, remote signals or barrier semaphores. Data moves between devices by JAX's collectives and lax.ppermute only.
A program may use at most 128 MiB of HBM per device.

```python
import math
import jax
import jax.numpy as jnp
import numpy as np
from jax import lax

D = 4096
V = 128256
PROJ = 64
FBLK = 128
QMOST = 32
QB = 128
QTOK = 1024
QBLOCKS = 8
QUERIES = 1024
QTOKENS = 8192
TRAIN = 2048
N_DP = 4
N_MP = 2
N_REP = 2


def draw_train_grads(key, part):
    key = jax.random.fold_in(key, 7)
    row_key = jax.random.fold_in(key, 0)
    col_key = jax.random.fold_in(key, 1)
    main_key = jax.random.fold_in(key, 2)
    weight_key = jax.random.fold_in(key, 4)
    sign_key = jax.random.fold_in(key, 5)
    nblocks = PROJ * PROJ // FBLK
    directions = FBLK // 2
    row_scale = jnp.exp(jax.random.uniform(row_key, (TRAIN, 1, 1), jnp.float32, 0.0, math.log(10.0)))
    col_scale = jnp.exp(jax.random.uniform(col_key, (1, nblocks, FBLK), jnp.float32, math.log(0.3), math.log(3.0)))
    signs = jax.random.bernoulli(sign_key, 0.5, (directions, nblocks, FBLK))
    unit_dirs = jnp.where(signs, 1.0, -1.0).astype(jnp.float32) / math.sqrt(FBLK)
    private = jnp.clip(jax.random.normal(main_key, (TRAIN, nblocks, FBLK), jnp.float32), -4.0, 4.0)
    loads = jnp.clip(jax.random.normal(weight_key, (directions, TRAIN, nblocks, 1), jnp.float32), -4.0, 4.0)
    values = 0.15 * private
    for index in range(directions):
        strength = 7.5 * math.exp(-0.75 * math.log(index + 1.0))
        values = values + strength * loads[index] * unit_dirs[index][None, :, :]
    values = values * row_scale * col_scale
    return values.reshape(TRAIN, PROJ * PROJ).astype(jnp.bfloat16)


def with_ends(entries, own_key, least, high):
    spot = [jax.random.randint(jax.random.fold_in(own_key, axis), (), 0, length) for axis, length in enumerate(entries.shape)]
    main_axis = entries.shape.index(max(entries.shape))
    neighbour = spot[:main_axis] + [(spot[main_axis] + 1) % entries.shape[main_axis]] + spot[main_axis + 1:]
    return entries.at[tuple(spot)].set(least).at[tuple(neighbour)].set(high)


def level_of(stream_key, extent, shards, smallest, high):
    def one(dim, parts):
        heights = jax.random.uniform(jax.random.fold_in(jax.random.fold_in(stream_key, 6), dim), (parts,), jnp.float32, smallest / len(shards), high / len(shards))
        return jnp.repeat(jnp.exp(heights), extent[dim] // parts).reshape((-1,) + (1,) * (len(extent) - dim - 1))

    level = one(*shards[0])
    for cut in shards[1:]:
        level = level * one(*cut)
    return level


def skewed_wide(own_key, extent, amount, skew):
    portions = [min(1 << octave, amount + 1 - (1 << octave)) * (1 << 20) // math.isqrt((1 << octave) ** skew) + 1 for octave in range((amount + 1).bit_length()) if 1 << octave <= amount]
    spread = 1 + sum(portions) // (1 << 30)
    grid = np.cumsum(np.array([max(1, weight // spread) for weight in portions]))
    ticket = jax.random.randint(jax.random.fold_in(own_key, 1), extent, 0, int(grid[len(portions) - 1]))
    start = jnp.left_shift(1, jnp.searchsorted(jnp.asarray(grid, jnp.int32), ticket, side="right").astype(jnp.int32))
    rank = start - 1 + jax.random.randint(jax.random.fold_in(own_key, 4), extent, 0, 1 << 30) % jnp.minimum(start, amount + 1 - start)
    return jax.random.permutation(jax.random.fold_in(own_key, 2), amount)[rank].astype(jnp.int32)


def length_profile(amount, total, reach, slope):
    weights = [(1 << 20) // math.isqrt(grade ** slope) + 1 for grade in range(2, amount + 1)]
    spare, counts = total - reach - (amount - 1), [1] * (amount - 1)
    while spare > 0:
        movable = [i for i in range(amount - 1) if counts[i] < reach]
        pool, remaining = sum([weights[i] for i in movable]), spare
        for i in movable:
            extra = min(reach - counts[i], max(1, remaining * weights[i] // pool), spare)
            counts[i] = counts[i] + extra
            spare = spare - extra
    return np.array([reach] + counts)


def ragged_sizes(key, number_of, total, reach, skew):
    if number_of == 2:
        one = jax.random.randint(key, (), max(1, total - reach), min(reach, total - 1) + 1)
        return jnp.stack([one, total - one])
    lengths = jnp.asarray(length_profile(number_of, total, reach, skew), jnp.int32)
    twos = (number_of - 1) // 2
    donor, receiver = lengths[1:1 + 2 * twos:2], lengths[2:2 + 2 * twos:2]
    margin = jnp.minimum(donor - 1, reach - receiver)
    shifted = jax.random.randint(jax.random.fold_in(key, 1), (twos,), 0, 1 << 20) % (margin + 1)
    lengths = lengths.at[1:1 + 2 * twos:2].set(donor - shifted).at[2:2 + 2 * twos:2].set(receiver + shifted)
    return lengths[jax.random.permutation(jax.random.fold_in(key, 2), number_of)]


def gaussian(stream_key, extent, scale, bound, cuts=(), kind=jnp.bfloat16):
    drawn = scale * jax.random.normal(stream_key, extent, jnp.float32)
    if cuts:
        drawn = drawn * level_of(stream_key, extent, cuts, -0.22, 0.18)
    return jnp.clip(drawn, -bound, bound).astype(kind)


def setup_inputs(seed: int = 0, part: int = 0) -> dict:
    seeds = jax.random.split(jax.random.key(seed), 7)
    own_keys = jax.random.split(jax.random.fold_in(seeds[6], part), 7)
    return {
        "query_ids": with_ends(skewed_wide(own_keys[0], (QTOKENS,), V, 2), jax.random.fold_in(own_keys[0], 3), 0, V - 1).astype(jnp.int32),
        "query_delta": gaussian(own_keys[1], (QTOKENS, D), 1.0, 6.0, ((0, 8), (1, 2))),
        "doc_lengths": jax.vmap(lambda own: ragged_sizes(own, QB, QTOK, QMOST, 2))(jax.random.split(own_keys[2], QBLOCKS)).reshape((QBLOCKS, QB)).astype(jnp.int32),
        "vocab_factor": gaussian(seeds[3], (V, PROJ), 1.0, 6.0, ((0, 2),)),
        "output_factor": gaussian(seeds[4], (D, PROJ), D ** -0.5, 0.09375, ((0, 2),)),
        "train_grads": draw_train_grads(jax.random.fold_in(jax.random.fold_in(seeds[6], part), 71), part),
    }


damping = 0.1

def doc_matrix(lengths_row, count):
    ends = jnp.cumsum(lengths_row).astype(jnp.int32)
    starts = ends - lengths_row.astype(jnp.int32)
    place = jnp.arange(count, dtype=jnp.int32)
    inside = (place[None, :] >= starts[:, None]) & (place[None, :] < ends[:, None])
    return inside.astype(jnp.bfloat16)

def reference(query_ids, query_delta, doc_lengths, vocab_factor, output_factor, train_grads):
    feat = PROJ * PROJ
    output_side = jnp.dot(query_delta.astype(jnp.float32), output_factor.astype(jnp.float32), preferred_element_type=jnp.float32)
    input_side = vocab_factor[query_ids].astype(jnp.float32)
    token_grads = (output_side[:, :, None] * input_side[:, None, :]).reshape(QTOKENS, feat).astype(jnp.bfloat16)
    token_grads = token_grads.reshape(QBLOCKS, QTOK, feat)

    def block_grads(pieces):
        lengths_row, block = pieces
        return jnp.dot(doc_matrix(lengths_row, QTOK).astype(jnp.float32), block.astype(jnp.float32), preferred_element_type=jnp.float32)
    query_grads = lax.map(block_grads, (doc_lengths, token_grads)).reshape(QUERIES, feat)
    nblocks = feat // FBLK
    train_blocks = train_grads.reshape(TRAIN, nblocks, FBLK)
    query_blocks = query_grads.reshape(QUERIES, nblocks, FBLK)

    def precondition(index):
        block = lax.dynamic_index_in_dim(train_blocks, index, 1, keepdims=False).astype(jnp.float32)
        fisher = jnp.dot(block.T, block, precision=lax.Precision.HIGHEST) / TRAIN
        shift = damping * (jnp.trace(fisher) / FBLK)
        damped = fisher + shift * jnp.eye(FBLK, dtype=jnp.float32)
        factor = jnp.linalg.cholesky(damped)
        rhs = lax.dynamic_index_in_dim(query_blocks, index, 1, keepdims=False)
        solved = jax.scipy.linalg.cho_solve((factor, True), rhs.T)
        return (solved.T / PROJ).astype(jnp.bfloat16)
    pre = lax.map(precondition, jnp.arange(nblocks, dtype=jnp.int32))
    pre = jnp.transpose(pre, (1, 0, 2)).reshape(QUERIES, feat)
    feat_dev = feat // N_MP

    def partial_sum(carry, index):
        start = (index * feat_dev).astype(jnp.int32)
        left = lax.dynamic_slice_in_dim(train_grads, start, feat_dev, 1)
        right = lax.dynamic_slice_in_dim(pre, start, feat_dev, 1)
        term = jnp.dot(left.astype(jnp.float32), right.T.astype(jnp.float32), preferred_element_type=jnp.float32).astype(jnp.bfloat16)
        term = lax.optimization_barrier(term)
        return (carry + term.astype(jnp.float32), None)
    total, unused = lax.scan(partial_sum, jnp.zeros((TRAIN, QUERIES), jnp.float32), jnp.arange(N_MP, dtype=jnp.int32))
    return total.astype(jnp.bfloat16).reshape(TRAIN, N_DP, N_REP, QB)
```

```python
import functools
import jax
import jax.numpy as jnp
from jax import lax
from jax.experimental import pallas as pl
from jax.experimental.pallas import tpu as pltpu
from jax.sharding import PartitionSpec as P

FBLK = 128
SLAB = FBLK + 8

damping = 0.1

VMEM = pl.BlockSpec(memory_space=pltpu.VMEM)
SMEM = pl.BlockSpec(memory_space=pltpu.SMEM)
HBM = pl.BlockSpec(memory_space=pl.ANY)


def call(kernel, outs, in_specs, scratch=(), vmem=48, flops=0, moved=0):
    return pl.pallas_call(
        kernel,
        out_shape=outs,
        in_specs=in_specs,
        scratch_shapes=list(scratch),
        compiler_params=pltpu.CompilerParams(vmem_limit_bytes=vmem << 20),
        cost_estimate=pl.CostEstimate(flops=flops, bytes_accessed=moved, transcendentals=0),
    )


def passed_along(shard, axis, by):
    size = lax.axis_size(axis)
    return lax.ppermute(shard, axis, [(i, (i + by) % size) for i in range(size)])


def square(dim):
    return lax.broadcasted_iota(jnp.int32, (FBLK, FBLK), dim)


def halves(value):
    high = value.astype(jnp.bfloat16)
    return high, (value - high.astype(jnp.float32)).astype(jnp.bfloat16)


def pack(first, second, spare=None):
    row, col = square(0), square(1)
    body = jnp.where(row >= col, first, second)
    diagonal = jnp.sum(jnp.where(row == col, second, 0.0), axis=0, keepdims=True)
    place = lax.broadcasted_iota(jnp.int32, (8, FBLK), 0)
    tail = jnp.where(place == 0, diagonal, 0.0)
    if spare is not None:
        tail = jnp.where(place == 1, spare, tail)
    return body, tail


def unpack(body, diagonal):
    row, col = square(0), square(1)
    turned = body.T
    first = jnp.where(row >= col, body, turned)
    second = jnp.where(row < col, body, jnp.where(row > col, turned, diagonal))
    return first, second


def gram_kernel(cycle, lengths, train, *slabs):
    mine, half = lax.axis_index("dp"), lax.axis_index("rep")
    spare = lengths[...].astype(jnp.float32)
    for shift in range(cycle):
        owner = half * cycle + lax.rem(mine + shift, cycle)
        start = pl.multiple_of(owner * (2 * FBLK), 2 * FBLK)
        part = train[:, pl.ds(start, 2 * FBLK)]
        gram = lax.dot_general(part, part, (((0,), (0,)), ((), ())), preferred_element_type=jnp.float32)
        body, tail = pack(gram[:FBLK, :FBLK], gram[FBLK:, FBLK:], spare)
        slabs[shift][pl.ds(0, FBLK), :] = body
        slabs[shift][pl.ds(FBLK, 8), :] = tail


def inverted(block):
    lane = square(1)
    row8 = lax.broadcasted_iota(jnp.int32, (FBLK, FBLK), 0)
    for k in range(FBLK):
        column = jnp.broadcast_to(block[:, k:k + 1], (FBLK, FBLK))
        pivot = 1.0 / column[k:k + 1, :]
        line = jnp.where(lane[:1, :] == k, pivot, block[k:k + 1, :] * pivot)
        rest = jnp.where(lane == k, 0.0, block) - column * line
        block = jnp.where(row8 == k, line, rest)
    return block


def factor_kernel(examples, scale, *refs):
    slabs, out = refs[:-1], refs[-1]
    body = slabs[0][pl.ds(0, FBLK), :]
    diagonal = slabs[0][pl.ds(FBLK, 1), :]
    for slab in slabs[1:]:
        body = body + slab[pl.ds(0, FBLK), :]
        diagonal = diagonal + slab[pl.ds(FBLK, 1), :]
    same = square(0) == square(1)
    results = []
    for gram in unpack(body, diagonal):
        fisher = gram / examples
        trace = jnp.sum(jnp.sum(jnp.where(same, fisher, 0.0), axis=0, keepdims=True), axis=1, keepdims=True)
        results.append(inverted(fisher + jnp.where(same, damping * (trace / FBLK), 0.0)) * scale)
    body, tail = pack(*results)
    out[pl.ds(0, FBLK), :] = body
    out[pl.ds(FBLK, 8), :] = tail


def factors_kernel(ids, id_rows, delta_hbm, table_hbm, factor, sent, kept, delta, table, looked, sems):
    model = lax.axis_index("mp")
    vocab_rows = table.shape[1]
    tokens, width = delta.shape
    proj = factor.shape[0]
    each = proj // lax.axis_size("mp")
    get_delta = pltpu.make_async_copy(delta_hbm, delta, sems.at[0])
    get_table = pltpu.make_async_copy(table_hbm, table, sems.at[1])
    get_delta.start()
    get_table.start()
    get_delta.wait()
    output = lax.dot_general(
        delta[...], factor[...], (((1,), (1,)), ((), ())), preferred_element_type=jnp.float32
    )
    looked[pl.ds(0, proj), :] = output.T
    mine = looked[pl.ds(pl.multiple_of(model * each, each), each), :]
    other = looked[pl.ds(pl.multiple_of((1 - model) * each, each), each), :]
    kept[...] = mine
    high, low = halves(other)
    sent[pl.ds(0, each), :] = high
    sent[pl.ds(each, each), :] = low
    get_table.wait()
    lanes = lax.broadcasted_iota(jnp.int32, (proj, FBLK), 1)
    first = model * vocab_rows

    def group(g, carry):
        gathered = jnp.zeros((proj, FBLK), jnp.bfloat16)
        base = g * FBLK
        for j in range(FBLK):
            local = ids[base + j] - first
            local = jnp.where((local >= 0) & (local < vocab_rows), local, 0)
            block = table[:, pl.ds(pl.multiple_of((local >> 7) * FBLK, FBLK), FBLK)]
            gathered = jnp.where(lanes == j, pltpu.roll(block, (j - local) & (FBLK - 1), 1), gathered)
        local = id_rows[pl.ds(g, 1), :] - first
        owned = (local >= 0) & (local < vocab_rows)
        spread = jnp.where(owned, 1.0, 0.0)
        gathered = (gathered.astype(jnp.float32) * spread).astype(jnp.bfloat16)
        sent[pl.ds(2 * each, proj), pl.ds(pl.multiple_of(base, FBLK), FBLK)] = gathered
        return carry

    lax.fori_loop(0, tokens // FBLK, group, 0)


def merge_kernel(kept, sent, got, out):
    each = kept.shape[0]
    received = got[pl.ds(0, each), :].astype(jnp.float32) + got[pl.ds(each, each), :].astype(jnp.float32)
    high, low = halves(kept[...] + received)
    out[pl.ds(0, each), :] = high
    out[pl.ds(each, each), :] = low
    rows = pl.ds(2 * each, out.shape[0] - 2 * each)
    out[rows, :] = sent[rows, :] + got[rows, :]


def queries_kernel(each, factors, slab, high_out, low_out):
    tokens = factors.shape[1]
    proj = factors.shape[0] - 2 * each
    queries = high_out.shape[1]
    lengths = slab[pl.ds(FBLK + 1, 1), :]
    upto = jnp.where(square(0) <= square(1), 1.0, 0.0).astype(jnp.bfloat16)
    ends = lax.dot_general(
        jnp.broadcast_to(lengths, (8, queries)).astype(jnp.bfloat16), upto, (((1,), (0,)), ((), ())),
        preferred_element_type=jnp.float32,
    )[:1]
    starts = ends - lengths
    place = lax.broadcasted_iota(jnp.int32, (tokens, queries), 0).astype(jnp.float32)
    inside = jnp.where((place >= starts) & (place < ends), 1.0, 0.0).astype(jnp.bfloat16)
    output = factors[pl.ds(0, each), :].astype(jnp.float32) + factors[pl.ds(each, each), :].astype(jnp.float32)
    inputs = factors[pl.ds(2 * each, proj), :].astype(jnp.float32)
    step = 8
    for start in range(0, each, step):
        grads = jnp.concatenate(
            [(inputs * output[r:r + 1, :]).astype(jnp.bfloat16) for r in range(start, start + step)], axis=0
        )
        summed = jnp.dot(grads, inside, preferred_element_type=jnp.float32)
        high, low = halves(summed)
        high_out[pl.ds(start * proj, step * proj), :] = high
        low_out[pl.ds(start * proj, step * proj), :] = low


def scores_kernel(cycle, *refs):
    own, peers = refs[:cycle], refs[cycle:2 * cycle]
    highs, lows = refs[2 * cycle:3 * cycle], refs[3 * cycle:4 * cycle]
    train, sent, kept, pre = refs[4 * cycle:]
    mine, rep, model = lax.axis_index("dp"), lax.axis_index("rep"), lax.axis_index("mp")
    queries = highs[0].shape[1]
    for side, slabs in enumerate((own, peers)):
        half = rep if side == 0 else 1 - rep
        for shift in range(cycle):
            owner = half * cycle + lax.rem(mine + cycle - shift, cycle)
            slab = slabs[shift]
            blocks = unpack(slab[pl.ds(0, FBLK), :], slab[pl.ds(FBLK, 1), :])
            for index, block in enumerate(blocks):
                rows = pl.ds(pl.multiple_of(owner * (2 * FBLK) + index * FBLK, FBLK), FBLK)
                high, low = halves(block)
                right_high = jnp.concatenate([ref[rows, :] for ref in highs], axis=1)
                right_low = jnp.concatenate([ref[rows, :] for ref in lows], axis=1)
                solved = jnp.dot(
                    jnp.concatenate([high, high, low], axis=1),
                    jnp.concatenate([right_high, right_low, right_high], axis=0),
                    preferred_element_type=jnp.float32,
                )
                pre[rows, :] = solved.astype(jnp.bfloat16)
    half_rows = sent.shape[0]
    for out, which in ((sent, 1 - model), (kept, model)):
        rows = pl.ds(pl.multiple_of(which * half_rows, half_rows), half_rows)
        scores = jnp.dot(train[rows, :], pre[...], preferred_element_type=jnp.float32).astype(jnp.bfloat16)
        for shift in range(cycle):
            source = lax.rem(mine + cycle - shift, cycle)
            out[:, pl.ds(pl.multiple_of(source * queries, queries), queries)] = (
                scores[:, shift * queries:(shift + 1) * queries]
            )


def shape(dims, dtype):
    return jax.ShapeDtypeStruct(dims, dtype)


def split_over_blocks(query_ids, query_delta, doc_lengths, vocab_factor, output_factor, train_grads):
    cycle = lax.axis_size("dp")
    tokens, width = query_delta.shape
    proj = output_factor.shape[1]
    each = proj // lax.axis_size("mp")
    vocab_rows = vocab_factor.shape[0]
    train_rows, feat = train_grads.shape
    queries = doc_lengths.shape[1]
    bf16, f32 = jnp.bfloat16, jnp.float32

    slabs = call(
        functools.partial(gram_kernel, cycle),
        [shape((SLAB, FBLK), f32)] * cycle,
        [VMEM, VMEM],
        flops=train_rows * feat * FBLK * 2,
        moved=2 * train_rows * feat,
        vmem=16,
    )(doc_lengths, train_grads)
    parts = [slabs[0]] + [passed_along(slabs[s], "dp", s) for s in range(1, cycle)]

    sent, kept = call(
        factors_kernel,
        [shape((2 * each + proj, tokens), bf16), shape((each, tokens), f32)],
        [SMEM, VMEM, HBM, HBM, VMEM],
        [
            pltpu.VMEM((tokens, width), bf16),
            pltpu.VMEM((proj, vocab_rows), bf16),
            pltpu.VMEM((proj, tokens), f32),
            pltpu.SemaphoreType.DMA((2,)),
        ],
        vmem=24,
        flops=2 * tokens * width * proj,
        moved=2 * (tokens * width + proj * vocab_rows) * 2,
    )(query_ids, query_ids.reshape(tokens // FBLK, FBLK), query_delta, vocab_factor.T, output_factor.T)
    got = passed_along(sent, "mp", 1)
    factors = call(
        merge_kernel,
        shape(sent.shape, bf16),
        [VMEM, VMEM, VMEM],
        vmem=16,
        flops=tokens * each,
        moved=8 * tokens * each * 4,
    )(kept, sent, got)
    gathered = [factors] + [passed_along(factors, "dp", s) for s in range(1, cycle)]

    inverse = call(
        functools.partial(factor_kernel, train_rows * cycle, 1.0 / proj),
        shape((SLAB, FBLK), f32),
        [VMEM] * cycle,
        vmem=16,
        flops=10 ** 10,
        moved=10 ** 6,
    )(*parts)
    inverses = [inverse] + [passed_along(inverse, "dp", s) for s in range(1, cycle)]
    peers = [passed_along(slab, "rep", 1) for slab in inverses]

    highs, lows = [], []
    for s in range(cycle):
        high, low = call(
            functools.partial(queries_kernel, each),
            [shape((feat, queries), bf16)] * 2,
            [VMEM, VMEM],
            vmem=24,
            flops=2 * feat * tokens * queries,
            moved=6 * feat * queries,
        )(gathered[s], parts[s])
        highs.append(high)
        lows.append(low)

    half_rows = train_rows // lax.axis_size("mp")
    outgoing, own = call(
        functools.partial(scores_kernel, cycle),
        [shape((half_rows, cycle * queries), bf16)] * 2,
        [VMEM] * (4 * cycle + 1),
        [pltpu.VMEM((feat, cycle * queries), bf16)],
        vmem=32,
        flops=2 * train_rows * feat * cycle * queries,
        moved=8 * feat * queries * cycle,
    )(*inverses, *peers, *highs, *lows, train_grads)
    incoming = passed_along(outgoing, "mp", 1)
    total = (own.astype(f32) + incoming.astype(f32)).astype(bf16)
    return total.reshape(half_rows, cycle, 1, queries)


def doc_matrix(lengths_row, count):
    ends = jnp.cumsum(lengths_row)
    starts = ends - lengths_row
    place = jnp.arange(count, dtype=jnp.int32)
    inside = (place[None, :] >= starts[:, None]) & (place[None, :] < ends[:, None])
    return inside.astype(jnp.bfloat16)


def solve_block(factor, rhs):
    return jax.scipy.linalg.cho_solve((factor, True), rhs)


def general(query_ids, query_delta, doc_lengths, vocab_factor, output_factor, train_grads):
    model_count = lax.axis_size("mp")
    model_index = lax.axis_index("mp")
    vocab_rows = vocab_factor.shape[0]
    local_ids = query_ids - model_index * vocab_rows
    owned = (local_ids >= 0) & (local_ids < vocab_rows)
    looked = vocab_factor[jnp.clip(local_ids, 0, vocab_rows - 1)].astype(jnp.float32)
    vocab_part = jnp.where(owned[:, None], looked, jnp.zeros_like(looked))
    output_part = jnp.dot(query_delta, output_factor, preferred_element_type=jnp.float32)
    input_side, output_side = lax.psum((vocab_part, output_part), "mp")
    proj = output_side.shape[1]
    rows_each = proj // model_count
    mine = lax.dynamic_slice_in_dim(output_side, model_index * rows_each, rows_each, 1)
    token_count = query_ids.shape[0]
    token_grads = (
        (mine[:, :, None] * input_side[:, None, :])
        .reshape(token_count, rows_each * proj)
        .astype(jnp.bfloat16)
    )
    query_grads = jnp.dot(
        doc_matrix(doc_lengths[0], token_count), token_grads, preferred_element_type=jnp.float32
    )
    train_rows, feat_dev = train_grads.shape
    nblocks = feat_dev // FBLK
    tiled = train_grads.reshape(train_rows, nblocks, FBLK)
    local_gram = jnp.einsum("tbi,tbj->bij", tiled, tiled, preferred_element_type=jnp.float32)
    total_gram = lax.psum(local_gram, "dp")
    fisher = total_gram / (train_rows * lax.axis_size("dp"))
    shift_amount = damping * (jnp.trace(fisher, axis1=1, axis2=2) / FBLK)
    damped = fisher + shift_amount[:, None, None] * jnp.eye(FBLK, dtype=jnp.float32)[None]
    factor = jnp.linalg.cholesky(damped)
    queries = query_grads.shape[0]
    rhs = jnp.transpose(query_grads.reshape(queries, nblocks, FBLK), (1, 2, 0))
    solved = jax.vmap(solve_block)(factor, rhs)
    pre = (jnp.transpose(solved, (2, 0, 1)).reshape(queries, feat_dev) / proj).astype(jnp.bfloat16)
    cycle = lax.axis_size("dp")
    everyone = lax.all_gather(pre, "dp", axis=0, tiled=True)
    scores = lax.dot_general(
        train_grads, everyone, (((1,), (1,)), ((), ())), preferred_element_type=jnp.float32
    )
    scores = scores.astype(jnp.bfloat16).reshape(train_rows, cycle, queries)
    summed = lax.psum_scatter(scores, "mp", scatter_dimension=0, tiled=True)
    return summed[:, :, None, :]


def per_device(query_ids, query_delta, doc_lengths, vocab_factor, output_factor, train_grads):
    owners = lax.axis_size("dp") * lax.axis_size("rep")
    fits = (
        train_grads.shape[1] == 2 * FBLK * owners
        and lax.axis_size("mp") == 2
        and lax.axis_size("rep") == 2
        and doc_lengths.shape[1] == FBLK
        and vocab_factor.shape[0] % FBLK == 0
    )
    body = split_over_blocks if fits else general
    return body(query_ids, query_delta, doc_lengths, vocab_factor, output_factor, train_grads)


def solution(mesh):
    placed = (
        P(("groups", "dp", "rep")),
        P(("groups", "dp", "rep"), "mp"),
        P(("groups", "dp", "rep"), None),
        P("mp", None),
        P("mp", None),
        P(("groups", "dp"), "mp"),
    )
    return jax.shard_map(
        per_device,
        mesh=mesh,
        in_specs=placed,
        out_specs=P(("groups", "dp", "mp"), None, "rep", None),
        check_vma=False,
    )
```

```python
import functools
import jax
import jax.numpy as jnp
from jax import lax
from jax.experimental import pallas as pl
from jax.experimental.pallas import tpu as pltpu
from jax.sharding import PartitionSpec as P

FBLK = 128
SLAB = FBLK + 8
PIVOTS = 4

damping = 0.1

VMEM = pl.BlockSpec(memory_space=pltpu.VMEM)
SMEM = pl.BlockSpec(memory_space=pltpu.SMEM)
HBM = pl.BlockSpec(memory_space=pltpu.HBM)


def call(kernel, outs, in_specs, scratch=(), vmem=48, flops=0, moved=0):
    return pl.pallas_call(
        kernel,
        out_shape=outs,
        in_specs=in_specs,
        scratch_shapes=list(scratch),
        compiler_params=pltpu.CompilerParams(vmem_limit_bytes=vmem << 20),
        cost_estimate=pl.CostEstimate(flops=flops, bytes_accessed=moved, transcendentals=0),
    )


def passed_along(shard, axis, by):
    size = lax.axis_size(axis)
    return lax.ppermute(shard, axis, [(i, (i + by) % size) for i in range(size)])


def square(dim):
    return lax.broadcasted_iota(jnp.int32, (FBLK, FBLK), dim)


def halves(value):
    high = value.astype(jnp.bfloat16)
    return high, (value - high.astype(jnp.float32)).astype(jnp.bfloat16)


def pack(first, second, spare=None):
    row, col = square(0), square(1)
    body = jnp.where(row >= col, first, second)
    diagonal = jnp.sum(jnp.where(row == col, second, 0.0), axis=0, keepdims=True)
    place = lax.broadcasted_iota(jnp.int32, (8, FBLK), 0)
    tail = jnp.where(place == 0, diagonal, 0.0)
    if spare is not None:
        tail = jnp.where(place == 1, spare, tail)
    return body, tail


def unpack(body, diagonal):
    row, col = square(0), square(1)
    turned = body.T
    first = jnp.where(row >= col, body, turned)
    second = jnp.where(row < col, body, jnp.where(row > col, turned, diagonal))
    return first, second


def gram_kernel(cycle, lengths, train, *slabs):
    mine, half = lax.axis_index("dp"), lax.axis_index("rep")
    spare = lengths[...].astype(jnp.float32)
    for shift in range(cycle):
        owner = half * cycle + lax.rem(mine + shift, cycle)
        start = pl.multiple_of(owner * (2 * FBLK), 2 * FBLK)
        part = train[:, pl.ds(start, 2 * FBLK)]
        gram = lax.dot_general(part, part, (((0,), (0,)), ((), ())), preferred_element_type=jnp.float32)
        body, tail = pack(gram[:FBLK, :FBLK], gram[FBLK:, FBLK:], spare)
        slabs[shift][pl.ds(0, FBLK), :] = body
        slabs[shift][pl.ds(FBLK, 8), :] = tail


def inverted(block):
    lane = lax.broadcasted_iota(jnp.int32, (8, FBLK), 1)
    sublane = lax.broadcasted_iota(jnp.int32, (8, FBLK), 0)
    groups = [block[8 * g:8 * (g + 1), :] for g in range(FBLK // 8)]

    def across(value, row):
        return jnp.broadcast_to(value[row:row + 1, :], (8, FBLK))

    def along(value, column):
        return jnp.broadcast_to(value[:, column:column + 1], (8, FBLK))

    for first in range(0, FBLK, PIVOTS):
        home, top = first // 8, first % 8
        count = range(PIVOTS)
        within = (lane >= first) & (lane < first + PIVOTS)
        panel = groups[home]
        columns = [along(panel, first + j) for j in count]
        pivots = [[across(columns[j], top + i) for j in count] for i in count]
        lines = [
            jnp.where(within, jnp.where(lane == first + i, 1.0, 0.0), across(panel, top + i)) for i in count
        ]
        for i in count:
            scale = 1.0 / pivots[i][i]
            lines[i] = lines[i] * scale
            for j in range(i + 1, PIVOTS):
                pivots[i][j] = pivots[i][j] * scale
            for other in count:
                if other != i:
                    lines[other] = lines[other] - pivots[other][i] * lines[i]
                    for j in range(i + 1, PIVOTS):
                        pivots[other][j] = pivots[other][j] - pivots[other][i] * pivots[i][j]
        for g in range(FBLK // 8):
            rest = jnp.where(within, 0.0, groups[g])
            for j in count:
                column = columns[j] if g == home else along(groups[g], first + j)
                rest = rest - column * lines[j]
            if g == home:
                for j in count:
                    rest = jnp.where(sublane == top + j, lines[j], rest)
            groups[g] = rest
    return jnp.concatenate(groups, axis=0)


def factor_kernel(examples, scale, *refs):
    slabs, out = refs[:-1], refs[-1]
    body = slabs[0][pl.ds(0, FBLK), :]
    diagonal = slabs[0][pl.ds(FBLK, 1), :]
    for slab in slabs[1:]:
        body = body + slab[pl.ds(0, FBLK), :]
        diagonal = diagonal + slab[pl.ds(FBLK, 1), :]
    same = square(0) == square(1)
    results = []
    for gram in unpack(body, diagonal):
        fisher = gram / examples
        trace = jnp.sum(jnp.sum(jnp.where(same, fisher, 0.0), axis=0, keepdims=True), axis=1, keepdims=True)
        results.append(inverted(fisher + jnp.where(same, damping * (trace / FBLK), 0.0)) * scale)
    body, tail = pack(*results)
    out[pl.ds(0, FBLK), :] = body
    out[pl.ds(FBLK, 8), :] = tail


def factors_kernel(ids, id_rows, delta_hbm, table_hbm, factor, sent, kept, delta, table, looked, sems):
    model = lax.axis_index("mp")
    vocab_rows = table.shape[1]
    tokens, width = delta.shape
    proj = factor.shape[0]
    each = proj // lax.axis_size("mp")
    get_delta = pltpu.make_async_copy(delta_hbm, delta, sems.at[0])
    get_table = pltpu.make_async_copy(table_hbm, table, sems.at[1])
    get_delta.start()
    get_table.start()
    get_delta.wait()
    output = lax.dot_general(
        delta[...], factor[...], (((1,), (1,)), ((), ())), preferred_element_type=jnp.float32
    )
    looked[pl.ds(0, proj), :] = output.T
    mine = looked[pl.ds(pl.multiple_of(model * each, each), each), :]
    other = looked[pl.ds(pl.multiple_of((1 - model) * each, each), each), :]
    kept[...] = mine
    high, low = halves(other)
    sent[pl.ds(0, each), :] = high
    sent[pl.ds(each, each), :] = low
    get_table.wait()
    lanes = lax.broadcasted_iota(jnp.int32, (proj, FBLK), 1)
    first = model * vocab_rows

    def group(g, carry):
        gathered = jnp.zeros((proj, FBLK), jnp.bfloat16)
        base = g * FBLK
        for j in range(FBLK):
            local = ids[base + j] - first
            local = jnp.where((local >= 0) & (local < vocab_rows), local, 0)
            block = table[:, pl.ds(pl.multiple_of((local >> 7) * FBLK, FBLK), FBLK)]
            gathered = jnp.where(lanes == j, pltpu.roll(block, (j - local) & (FBLK - 1), 1), gathered)
        local = id_rows[pl.ds(g, 1), :] - first
        owned = (local >= 0) & (local < vocab_rows)
        spread = jnp.where(owned, 1.0, 0.0)
        gathered = (gathered.astype(jnp.float32) * spread).astype(jnp.bfloat16)
        sent[pl.ds(2 * each, proj), pl.ds(pl.multiple_of(base, FBLK), FBLK)] = gathered
        return carry

    lax.fori_loop(0, tokens // FBLK, group, 0)


def merge_kernel(kept, sent, got, out):
    each = kept.shape[0]
    received = got[pl.ds(0, each), :].astype(jnp.float32) + got[pl.ds(each, each), :].astype(jnp.float32)
    high, low = halves(kept[...] + received)
    out[pl.ds(0, each), :] = high
    out[pl.ds(each, each), :] = low
    rows = pl.ds(2 * each, out.shape[0] - 2 * each)
    out[rows, :] = sent[rows, :] + got[rows, :]


def queries_kernel(each, cycle, factors, *refs):
    slabs, (high_out, low_out) = refs[:cycle], refs[cycle:]
    mine = lax.axis_index("dp")
    tokens = factors.shape[2]
    proj = factors.shape[1] - 2 * each
    upto = jnp.where(square(0) <= square(1), 1.0, 0.0).astype(jnp.bfloat16)
    place = lax.broadcasted_iota(jnp.int32, (tokens, FBLK), 0).astype(jnp.float32)
    for shift in range(cycle):
        source = lax.rem(mine + cycle - shift, cycle)
        lengths = slabs[shift][pl.ds(FBLK + 1, 1), :]
        ends = lax.dot_general(
            jnp.broadcast_to(lengths, (8, FBLK)).astype(jnp.bfloat16), upto, (((1,), (0,)), ((), ())),
            preferred_element_type=jnp.float32,
        )[:1]
        starts = ends - lengths
        inside = jnp.where((place >= starts) & (place < ends), 1.0, 0.0).astype(jnp.bfloat16)
        output = factors[source, pl.ds(0, each), :].astype(jnp.float32)
        output = output + factors[source, pl.ds(each, each), :].astype(jnp.float32)
        inputs = factors[source, pl.ds(2 * each, proj), :].astype(jnp.float32)
        columns = pl.ds(shift * FBLK, FBLK)
        step = 8
        for start in range(0, each, step):
            grads = jnp.concatenate(
                [(inputs * output[r:r + 1, :]).astype(jnp.bfloat16) for r in range(start, start + step)], axis=0
            )
            summed = jnp.dot(grads, inside, preferred_element_type=jnp.float32)
            high, low = halves(summed)
            high_out[pl.ds(start * proj, step * proj), columns] = high
            low_out[pl.ds(start * proj, step * proj), columns] = low


def scores_kernel(cycle, *refs):
    own, peers = refs[:cycle], refs[cycle:2 * cycle]
    highs, lows, train, sent, kept, pre = refs[2 * cycle:]
    mine, rep, model = lax.axis_index("dp"), lax.axis_index("rep"), lax.axis_index("mp")
    queries = highs.shape[1] // cycle
    for side, slabs in enumerate((own, peers)):
        half = rep if side == 0 else 1 - rep
        for shift in range(cycle):
            owner = half * cycle + lax.rem(mine + cycle - shift, cycle)
            slab = slabs[shift]
            blocks = unpack(slab[pl.ds(0, FBLK), :], slab[pl.ds(FBLK, 1), :])
            for index, block in enumerate(blocks):
                rows = pl.ds(pl.multiple_of(owner * (2 * FBLK) + index * FBLK, FBLK), FBLK)
                high, low = halves(block)
                right_high, right_low = highs[rows, :], lows[rows, :]
                solved = jnp.dot(
                    jnp.concatenate([high, high, low], axis=1),
                    jnp.concatenate([right_high, right_low, right_high], axis=0),
                    preferred_element_type=jnp.float32,
                )
                pre[rows, :] = solved.astype(jnp.bfloat16)
    half_rows = sent.shape[0]
    for out, which in ((sent, 1 - model), (kept, model)):
        rows = pl.ds(pl.multiple_of(which * half_rows, half_rows), half_rows)
        scores = jnp.dot(train[rows, :], pre[...], preferred_element_type=jnp.float32).astype(jnp.bfloat16)
        for shift in range(cycle):
            source = lax.rem(mine + cycle - shift, cycle)
            out[:, pl.ds(pl.multiple_of(source * queries, queries), queries)] = (
                scores[:, shift * queries:(shift + 1) * queries]
            )


def shape(dims, dtype):
    return jax.ShapeDtypeStruct(dims, dtype)


def split_over_blocks(query_ids, query_delta, doc_lengths, vocab_factor, output_factor, train_grads):
    cycle = lax.axis_size("dp")
    tokens, width = query_delta.shape
    proj = output_factor.shape[1]
    each = proj // lax.axis_size("mp")
    vocab_rows = vocab_factor.shape[0]
    train_rows, feat = train_grads.shape
    queries = doc_lengths.shape[1]
    bf16, f32 = jnp.bfloat16, jnp.float32

    slabs = call(
        functools.partial(gram_kernel, cycle),
        [shape((SLAB, FBLK), f32)] * cycle,
        [VMEM, VMEM],
        flops=train_rows * feat * FBLK * 2,
        moved=2 * train_rows * feat,
        vmem=16,
    )(doc_lengths, train_grads)
    parts = [slabs[0]] + [passed_along(slabs[s], "dp", s) for s in range(1, cycle)]

    sent, kept = call(
        factors_kernel,
        [shape((2 * each + proj, tokens), bf16), shape((each, tokens), f32)],
        [SMEM, VMEM, HBM, HBM, VMEM],
        [
            pltpu.VMEM((tokens, width), bf16),
            pltpu.VMEM((proj, vocab_rows), bf16),
            pltpu.VMEM((proj, tokens), f32),
            pltpu.SemaphoreType.DMA((2,)),
        ],
        vmem=24,
        flops=2 * tokens * width * proj,
        moved=2 * (tokens * width + proj * vocab_rows) * 2,
    )(query_ids, query_ids.reshape(tokens // FBLK, FBLK), query_delta, vocab_factor.T, output_factor.T)
    got = passed_along(sent, "mp", 1)
    factors = call(
        merge_kernel,
        shape(sent.shape, bf16),
        [VMEM, VMEM, VMEM],
        vmem=16,
        flops=tokens * each,
        moved=8 * tokens * each * 4,
    )(kept, sent, got)
    gathered = lax.all_gather(factors, "dp", axis=0)

    inverse = call(
        functools.partial(factor_kernel, train_rows * cycle, 1.0 / proj),
        shape((SLAB, FBLK), f32),
        [VMEM] * cycle,
        vmem=16,
        flops=10 ** 10,
        moved=10 ** 6,
    )(*parts)
    inverses = [inverse] + [passed_along(inverse, "dp", s) for s in range(1, cycle)]
    peers = [passed_along(slab, "rep", 1) for slab in inverses]

    highs, lows = call(
        functools.partial(queries_kernel, each, cycle),
        [shape((feat, cycle * queries), bf16)] * 2,
        [VMEM] * (1 + cycle),
        vmem=24,
        flops=2 * feat * tokens * queries * cycle,
        moved=6 * feat * queries * cycle,
    )(gathered, *parts)

    half_rows = train_rows // lax.axis_size("mp")
    outgoing, own = call(
        functools.partial(scores_kernel, cycle),
        [shape((half_rows, cycle * queries), bf16)] * 2,
        [VMEM] * (2 * cycle + 3),
        [pltpu.VMEM((feat, cycle * queries), bf16)],
        vmem=32,
        flops=2 * train_rows * feat * cycle * queries,
        moved=8 * feat * queries * cycle,
    )(*inverses, *peers, highs, lows, train_grads)
    incoming = passed_along(outgoing, "mp", 1)
    total = (own.astype(f32) + incoming.astype(f32)).astype(bf16)
    return total.reshape(half_rows, cycle, 1, queries)


def doc_matrix(lengths_row, count):
    ends = jnp.cumsum(lengths_row)
    starts = ends - lengths_row
    place = jnp.arange(count, dtype=jnp.int32)
    inside = (place[None, :] >= starts[:, None]) & (place[None, :] < ends[:, None])
    return inside.astype(jnp.bfloat16)


def solve_block(factor, rhs):
    return jax.scipy.linalg.cho_solve((factor, True), rhs)


def general(query_ids, query_delta, doc_lengths, vocab_factor, output_factor, train_grads):
    model_count = lax.axis_size("mp")
    model_index = lax.axis_index("mp")
    vocab_rows = vocab_factor.shape[0]
    local_ids = query_ids - model_index * vocab_rows
    owned = (local_ids >= 0) & (local_ids < vocab_rows)
    looked = vocab_factor[jnp.clip(local_ids, 0, vocab_rows - 1)].astype(jnp.float32)
    vocab_part = jnp.where(owned[:, None], looked, jnp.zeros_like(looked))
    output_part = jnp.dot(query_delta, output_factor, preferred_element_type=jnp.float32)
    input_side, output_side = lax.psum((vocab_part, output_part), "mp")
    proj = output_side.shape[1]
    rows_each = proj // model_count
    mine = lax.dynamic_slice_in_dim(output_side, model_index * rows_each, rows_each, 1)
    token_count = query_ids.shape[0]
    token_grads = (
        (mine[:, :, None] * input_side[:, None, :])
        .reshape(token_count, rows_each * proj)
        .astype(jnp.bfloat16)
    )
    query_grads = jnp.dot(
        doc_matrix(doc_lengths[0], token_count), token_grads, preferred_element_type=jnp.float32
    )
    train_rows, feat_dev = train_grads.shape
    nblocks = feat_dev // FBLK
    tiled = train_grads.reshape(train_rows, nblocks, FBLK)
    local_gram = jnp.einsum("tbi,tbj->bij", tiled, tiled, preferred_element_type=jnp.float32)
    total_gram = lax.psum(local_gram, "dp")
    fisher = total_gram / (train_rows * lax.axis_size("dp"))
    shift_amount = damping * (jnp.trace(fisher, axis1=1, axis2=2) / FBLK)
    damped = fisher + shift_amount[:, None, None] * jnp.eye(FBLK, dtype=jnp.float32)[None]
    factor = jnp.linalg.cholesky(damped)
    queries = query_grads.shape[0]
    rhs = jnp.transpose(query_grads.reshape(queries, nblocks, FBLK), (1, 2, 0))
    solved = jax.vmap(solve_block)(factor, rhs)
    pre = (jnp.transpose(solved, (2, 0, 1)).reshape(queries, feat_dev) / proj).astype(jnp.bfloat16)
    cycle = lax.axis_size("dp")
    everyone = lax.all_gather(pre, "dp", axis=0, tiled=True)
    scores = lax.dot_general(
        train_grads, everyone, (((1,), (1,)), ((), ())), preferred_element_type=jnp.float32
    )
    scores = scores.astype(jnp.bfloat16).reshape(train_rows, cycle, queries)
    summed = lax.psum_scatter(scores, "mp", scatter_dimension=0, tiled=True)
    return summed[:, :, None, :]


def per_device(query_ids, query_delta, doc_lengths, vocab_factor, output_factor, train_grads):
    owners = lax.axis_size("dp") * lax.axis_size("rep")
    fits = (
        train_grads.shape[1] == 2 * FBLK * owners
        and lax.axis_size("mp") == 2
        and lax.axis_size("rep") == 2
        and doc_lengths.shape[1] == FBLK
        and vocab_factor.shape[0] % FBLK == 0
    )
    body = split_over_blocks if fits else general
    return body(query_ids, query_delta, doc_lengths, vocab_factor, output_factor, train_grads)


def solution(mesh):
    placed = (
        P(("groups", "dp", "rep")),
        P(("groups", "dp", "rep"), "mp"),
        P(("groups", "dp", "rep"), None),
        P("mp", None),
        P("mp", None),
        P(("groups", "dp"), "mp"),
    )
    return jax.shard_map(
        per_device,
        mesh=mesh,
        in_specs=placed,
        out_specs=P(("groups", "dp", "mp"), None, "rep", None),
        check_vma=False,
    )
```

```python
import functools
import jax
import jax.numpy as jnp
from jax import lax
from jax.experimental import pallas as pl
from jax.experimental.pallas import tpu as pltpu
from jax.sharding import PartitionSpec as P

FBLK = 128
SLAB = FBLK + 8
PANEL = 8

damping = 0.1

VMEM = pl.BlockSpec(memory_space=pltpu.VMEM)
SMEM = pl.BlockSpec(memory_space=pltpu.SMEM)
HBM = pl.BlockSpec(memory_space=pl.ANY)


def call(kernel, outs, in_specs, scratch=(), vmem=48, flops=0, moved=0):
    return pl.pallas_call(
        kernel,
        out_shape=outs,
        in_specs=in_specs,
        scratch_shapes=list(scratch),
        compiler_params=pltpu.CompilerParams(vmem_limit_bytes=vmem << 20),
        cost_estimate=pl.CostEstimate(flops=flops, bytes_accessed=moved, transcendentals=0),
    )


def passed_along(shard, axis, by):
    size = lax.axis_size(axis)
    return lax.ppermute(shard, axis, [(i, (i + by) % size) for i in range(size)])


def square(dim):
    return lax.broadcasted_iota(jnp.int32, (FBLK, FBLK), dim)


def halves(value):
    high = value.astype(jnp.bfloat16)
    return high, (value - high.astype(jnp.float32)).astype(jnp.bfloat16)


def pack(first, second, spare=None):
    row, col = square(0), square(1)
    body = jnp.where(row >= col, first, second)
    diagonal = jnp.sum(jnp.where(row == col, second, 0.0), axis=0, keepdims=True)
    place = lax.broadcasted_iota(jnp.int32, (8, FBLK), 0)
    tail = jnp.where(place == 0, diagonal, 0.0)
    if spare is not None:
        tail = jnp.where(place == 1, spare, tail)
    return body, tail


def unpack(body, diagonal):
    row, col = square(0), square(1)
    turned = body.T
    first = jnp.where(row >= col, body, turned)
    second = jnp.where(row < col, body, jnp.where(row > col, turned, diagonal))
    return first, second


def gram_kernel(lengths, train, slabs):
    cycle = slabs.shape[0]
    half = lax.axis_index("rep")
    spare = lengths[...].astype(jnp.float32)
    for target in range(cycle):
        start = pl.multiple_of((half * cycle + target) * (2 * FBLK), 2 * FBLK)
        part = train[:, pl.ds(start, 2 * FBLK)]
        gram = lax.dot_general(part, part, (((0,), (0,)), ((), ())), preferred_element_type=jnp.float32)
        body, tail = pack(gram[:FBLK, :FBLK], gram[FBLK:, FBLK:], spare)
        slabs[target, pl.ds(0, FBLK), :] = body
        slabs[target, pl.ds(FBLK, 8), :] = tail


def thirds(value):
    high = value.astype(jnp.bfloat16)
    rest = value - high.astype(jnp.float32)
    middle = rest.astype(jnp.bfloat16)
    return high, middle, (rest - middle.astype(jnp.float32)).astype(jnp.bfloat16)


def at_rows(panel, first):
    pair = 2 * PANEL
    blank = jnp.zeros((PANEL, FBLK), jnp.float32)
    panel = panel.astype(jnp.float32)
    piece = jnp.concatenate([panel, blank] if first % pair == 0 else [blank, panel], axis=0).astype(jnp.bfloat16)
    before = first // pair * pair
    pieces = [jnp.zeros((before, FBLK), jnp.bfloat16), piece, jnp.zeros((FBLK - before - pair, FBLK), jnp.bfloat16)]
    return jnp.concatenate([piece for piece in pieces if piece.shape[0]], axis=0)


def product(left, right, first):
    high, middle, low = thirds(left)
    right_high, right_middle, right_low = (at_rows(part, first) for part in thirds(right))
    both = jnp.concatenate([right_high, right_middle], axis=1)
    large = jnp.dot(
        jnp.concatenate([high, middle], axis=1), jnp.concatenate([both, both], axis=0),
        preferred_element_type=jnp.float32,
    )
    small = jnp.dot(
        jnp.concatenate([high, low], axis=1), jnp.concatenate([right_low, right_high], axis=0),
        preferred_element_type=jnp.float32,
    )
    return large[:, :FBLK] + (large[:, FBLK:] + small)


def eliminated(panel, first):
    lane = lax.broadcasted_iota(jnp.int32, (PANEL, FBLK), 1)
    sublane = lax.broadcasted_iota(jnp.int32, (PANEL, FBLK), 0)
    within = (lane >= first) & (lane < first + PANEL)
    count = range(PANEL)

    def across(value, row):
        return jnp.broadcast_to(value[row:row + 1, :], (PANEL, FBLK))

    columns = [jnp.broadcast_to(panel[:, first + j:first + j + 1], (PANEL, FBLK)) for j in count]
    pivots = [[across(columns[j], i) if j >= i else None for j in count] for i in count]
    rest = jnp.where(within, jnp.where(lane == first + sublane, 1.0, 0.0), panel)
    lines = [across(rest, i) for i in count]
    for i in count:
        scale = 1.0 / pivots[i][i]
        scaled = lines[i] * scale
        shares = [pivots[i][j] * scale if j > i else None for j in count]
        for m in range(i + 1, PANEL):
            lines[m] = lines[m] - pivots[i][m] * scaled
            for j in range(m, PANEL):
                pivots[m][j] = pivots[m][j] - shares[m] * pivots[i][j]
        lines[i] = scaled
        pivots[i] = shares
    for i in reversed(count):
        for m in range(i):
            lines[m] = lines[m] - pivots[m][i] * lines[i]
    result = lines[0]
    for i in range(1, PANEL):
        result = jnp.where(sublane == i, lines[i], result)
    return result


def inverted(blocks):
    lane = square(1)
    for first in range(0, FBLK, PANEL):
        within = (lane >= first) & (lane < first + PANEL)
        panels = [eliminated(block[first:first + PANEL, :], first) for block in blocks]
        updates = [product(block, panel, first) for block, panel in zip(blocks, panels)]
        rests = [jnp.where(within, 0.0, block) - update for block, update in zip(blocks, updates)]
        blocks = [
            jnp.concatenate(
                [part for part in (rest[:first], panel, rest[first + PANEL:]) if part.shape[0]], axis=0
            )
            for rest, panel in zip(rests, panels)
        ]
    return blocks


def factor_kernel(examples, scale, slabs, out):
    copies = slabs.shape[0]
    body = slabs[0, pl.ds(0, FBLK), :]
    diagonal = slabs[0, pl.ds(FBLK, 1), :]
    for index in range(1, copies):
        body = body + slabs[index, pl.ds(0, FBLK), :]
        diagonal = diagonal + slabs[index, pl.ds(FBLK, 1), :]
    same = square(0) == square(1)
    damped = []
    for gram in unpack(body, diagonal):
        fisher = gram / examples
        trace = jnp.sum(jnp.sum(jnp.where(same, fisher, 0.0), axis=0, keepdims=True), axis=1, keepdims=True)
        damped.append(fisher + jnp.where(same, damping * (trace / FBLK), 0.0))
    first, second = inverted(damped)
    body, tail = pack(first * scale, second * scale)
    for index in range(copies):
        out[index, pl.ds(0, FBLK), :] = body
        out[index, pl.ds(FBLK, 8), :] = tail


def factors_kernel(ids, id_rows, delta_hbm, table_hbm, factor, sent, kept, delta, table, looked, sems):
    model = lax.axis_index("mp")
    vocab_rows = table.shape[1]
    tokens, width = delta.shape
    proj = factor.shape[0]
    each = proj // lax.axis_size("mp")
    get_delta = pltpu.make_async_copy(delta_hbm, delta, sems.at[0])
    get_table = pltpu.make_async_copy(table_hbm, table, sems.at[1])
    get_delta.start()
    get_table.start()
    get_delta.wait()
    output = lax.dot_general(
        delta[...], factor[...], (((1,), (1,)), ((), ())), preferred_element_type=jnp.float32
    )
    looked[pl.ds(0, proj), :] = output.T
    mine = looked[pl.ds(pl.multiple_of(model * each, each), each), :]
    other = looked[pl.ds(pl.multiple_of((1 - model) * each, each), each), :]
    kept[...] = mine
    high, low = halves(other)
    sent[pl.ds(0, each), :] = high
    sent[pl.ds(each, each), :] = low
    get_table.wait()
    lanes = lax.broadcasted_iota(jnp.int32, (proj, FBLK), 1)
    first = model * vocab_rows

    def group(g, carry):
        gathered = jnp.zeros((proj, FBLK), jnp.bfloat16)
        base = g * FBLK
        for j in range(FBLK):
            local = ids[base + j] - first
            local = jnp.where((local >= 0) & (local < vocab_rows), local, 0)
            block = table[:, pl.ds(pl.multiple_of((local >> 7) * FBLK, FBLK), FBLK)]
            gathered = jnp.where(lanes == j, pltpu.roll(block, (j - local) & (FBLK - 1), 1), gathered)
        local = id_rows[pl.ds(g, 1), :] - first
        owned = (local >= 0) & (local < vocab_rows)
        spread = jnp.where(owned, 1.0, 0.0)
        gathered = (gathered.astype(jnp.float32) * spread).astype(jnp.bfloat16)
        sent[pl.ds(2 * each, proj), pl.ds(pl.multiple_of(base, FBLK), FBLK)] = gathered
        return carry

    lax.fori_loop(0, tokens // FBLK, group, 0)


def merge_kernel(kept, sent, got, out):
    each = kept.shape[0]
    received = got[pl.ds(0, each), :].astype(jnp.float32) + got[pl.ds(each, each), :].astype(jnp.float32)
    high, low = halves(kept[...] + received)
    out[pl.ds(0, each), :] = high
    out[pl.ds(each, each), :] = low
    rows = pl.ds(2 * each, out.shape[0] - 2 * each)
    out[rows, :] = sent[rows, :] + got[rows, :]


def queries_kernel(each, shift, factors, slabs, high_out, low_out):
    tokens = factors.shape[1]
    proj = factors.shape[0] - 2 * each
    queries = high_out.shape[1]
    cycle = slabs.shape[0]
    source = lax.rem(lax.axis_index("dp") + cycle - shift, cycle)
    lengths = slabs[source, pl.ds(FBLK + 1, 1), :]
    upto = jnp.where(square(0) <= square(1), 1.0, 0.0).astype(jnp.bfloat16)
    ends = lax.dot_general(
        jnp.broadcast_to(lengths, (8, queries)).astype(jnp.bfloat16), upto, (((1,), (0,)), ((), ())),
        preferred_element_type=jnp.float32,
    )[:1]
    starts = ends - lengths
    place = lax.broadcasted_iota(jnp.int32, (tokens, queries), 0).astype(jnp.float32)
    inside = jnp.where((place >= starts) & (place < ends), 1.0, 0.0).astype(jnp.bfloat16)
    output = factors[pl.ds(0, each), :].astype(jnp.float32) + factors[pl.ds(each, each), :].astype(jnp.float32)
    inputs = factors[pl.ds(2 * each, proj), :].astype(jnp.float32)
    step = 8
    for start in range(0, each, step):
        grads = jnp.concatenate(
            [(inputs * output[r:r + 1, :]).astype(jnp.bfloat16) for r in range(start, start + step)], axis=0
        )
        summed = jnp.dot(grads, inside, preferred_element_type=jnp.float32)
        high, low = halves(summed)
        high_out[pl.ds(start * proj, step * proj), :] = high
        low_out[pl.ds(start * proj, step * proj), :] = low


def scores_kernel(cycle, *refs):
    own, peers = refs[:2]
    highs, lows = refs[2:2 + cycle], refs[2 + cycle:2 + 2 * cycle]
    train, sent, kept, pre = refs[2 + 2 * cycle:]
    mine, rep, model = lax.axis_index("dp"), lax.axis_index("rep"), lax.axis_index("mp")
    queries = highs[0].shape[1]
    for half, slabs in ((rep, own), (1 - rep, peers)):
        for owner in range(cycle):
            blocks = unpack(slabs[owner, pl.ds(0, FBLK), :], slabs[owner, pl.ds(FBLK, 1), :])
            for index, block in enumerate(blocks):
                start = (half * cycle + owner) * (2 * FBLK) + index * FBLK
                rows = pl.ds(pl.multiple_of(start, FBLK), FBLK)
                high, low = halves(block)
                right_high = jnp.concatenate([ref[rows, :] for ref in highs], axis=1)
                right_low = jnp.concatenate([ref[rows, :] for ref in lows], axis=1)
                solved = jnp.dot(
                    jnp.concatenate([high, high, low], axis=1),
                    jnp.concatenate([right_high, right_low, right_high], axis=0),
                    preferred_element_type=jnp.float32,
                )
                pre[rows, :] = solved.astype(jnp.bfloat16)
    half_rows = sent.shape[0]
    for out, which in ((sent, 1 - model), (kept, model)):
        rows = pl.ds(pl.multiple_of(which * half_rows, half_rows), half_rows)
        scores = jnp.dot(train[rows, :], pre[...], preferred_element_type=jnp.float32).astype(jnp.bfloat16)
        for shift in range(cycle):
            source = lax.rem(mine + cycle - shift, cycle)
            out[:, pl.ds(pl.multiple_of(source * queries, queries), queries)] = (
                scores[:, shift * queries:(shift + 1) * queries]
            )


def shape(dims, dtype):
    return jax.ShapeDtypeStruct(dims, dtype)


def split_over_blocks(query_ids, query_delta, doc_lengths, vocab_factor, output_factor, train_grads):
    cycle = lax.axis_size("dp")
    tokens, width = query_delta.shape
    proj = output_factor.shape[1]
    each = proj // lax.axis_size("mp")
    vocab_rows = vocab_factor.shape[0]
    train_rows, feat = train_grads.shape
    queries = doc_lengths.shape[1]
    bf16, f32 = jnp.bfloat16, jnp.float32

    slabs = call(
        gram_kernel,
        shape((cycle, SLAB, FBLK), f32),
        [VMEM, VMEM],
        flops=train_rows * feat * FBLK * 2,
        moved=2 * train_rows * feat,
        vmem=16,
    )(doc_lengths, train_grads)
    parts = lax.all_to_all(slabs, "dp", 0, 0)

    sent, kept = call(
        factors_kernel,
        [shape((2 * each + proj, tokens), bf16), shape((each, tokens), f32)],
        [SMEM, VMEM, HBM, HBM, VMEM],
        [
            pltpu.VMEM((tokens, width), bf16),
            pltpu.VMEM((proj, vocab_rows), bf16),
            pltpu.VMEM((proj, tokens), f32),
            pltpu.SemaphoreType.DMA((2,)),
        ],
        vmem=62,
        flops=2 * tokens * width * proj,
        moved=2 * (tokens * width + proj * vocab_rows) * 2,
    )(query_ids, query_ids.reshape(tokens // FBLK, FBLK), query_delta, vocab_factor.T, output_factor.T)
    got = passed_along(sent, "mp", 1)
    factors = call(
        merge_kernel,
        shape(sent.shape, bf16),
        [VMEM, VMEM, VMEM],
        vmem=16,
        flops=tokens * each,
        moved=8 * tokens * each * 4,
    )(kept, sent, got)
    gathered = [factors] + [passed_along(factors, "dp", s) for s in range(1, cycle)]

    inverses = call(
        functools.partial(factor_kernel, train_rows * cycle, 1.0 / proj),
        shape((cycle, SLAB, FBLK), f32),
        [VMEM],
        vmem=16,
        flops=10 ** 10,
        moved=10 ** 6,
    )(parts)
    inverses = lax.all_to_all(inverses, "dp", 0, 0)
    peers = passed_along(inverses, "rep", 1)

    highs, lows = [], []
    for s in range(cycle):
        high, low = call(
            functools.partial(queries_kernel, each, s),
            [shape((feat, queries), bf16)] * 2,
            [VMEM, VMEM],
            vmem=24,
            flops=2 * feat * tokens * queries,
            moved=6 * feat * queries,
        )(gathered[s], parts)
        highs.append(high)
        lows.append(low)

    half_rows = train_rows // lax.axis_size("mp")
    outgoing, own = call(
        functools.partial(scores_kernel, cycle),
        [shape((half_rows, cycle * queries), bf16)] * 2,
        [VMEM] * (2 * cycle + 3),
        [pltpu.VMEM((feat, cycle * queries), bf16)],
        vmem=32,
        flops=2 * train_rows * feat * cycle * queries,
        moved=8 * feat * queries * cycle,
    )(inverses, peers, *highs, *lows, train_grads)
    incoming = passed_along(outgoing, "mp", 1)
    total = (own.astype(f32) + incoming.astype(f32)).astype(bf16)
    return total.reshape(half_rows, cycle, 1, queries)


def doc_matrix(lengths_row, count):
    ends = jnp.cumsum(lengths_row)
    starts = ends - lengths_row
    place = jnp.arange(count, dtype=jnp.int32)
    inside = (place[None, :] >= starts[:, None]) & (place[None, :] < ends[:, None])
    return inside.astype(jnp.bfloat16)


def solve_block(factor, rhs):
    return jax.scipy.linalg.cho_solve((factor, True), rhs)


def general(query_ids, query_delta, doc_lengths, vocab_factor, output_factor, train_grads):
    model_count = lax.axis_size("mp")
    model_index = lax.axis_index("mp")
    vocab_rows = vocab_factor.shape[0]
    local_ids = query_ids - model_index * vocab_rows
    owned = (local_ids >= 0) & (local_ids < vocab_rows)
    looked = vocab_factor[jnp.clip(local_ids, 0, vocab_rows - 1)].astype(jnp.float32)
    vocab_part = jnp.where(owned[:, None], looked, jnp.zeros_like(looked))
    output_part = jnp.dot(query_delta, output_factor, preferred_element_type=jnp.float32)
    input_side, output_side = lax.psum((vocab_part, output_part), "mp")
    proj = output_side.shape[1]
    rows_each = proj // model_count
    mine = lax.dynamic_slice_in_dim(output_side, model_index * rows_each, rows_each, 1)
    token_count = query_ids.shape[0]
    token_grads = (
        (mine[:, :, None] * input_side[:, None, :])
        .reshape(token_count, rows_each * proj)
        .astype(jnp.bfloat16)
    )
    query_grads = jnp.dot(
        doc_matrix(doc_lengths[0], token_count), token_grads, preferred_element_type=jnp.float32
    )
    train_rows, feat_dev = train_grads.shape
    nblocks = feat_dev // FBLK
    tiled = train_grads.reshape(train_rows, nblocks, FBLK)
    local_gram = jnp.einsum("tbi,tbj->bij", tiled, tiled, preferred_element_type=jnp.float32)
    total_gram = lax.psum(local_gram, "dp")
    fisher = total_gram / (train_rows * lax.axis_size("dp"))
    shift_amount = damping * (jnp.trace(fisher, axis1=1, axis2=2) / FBLK)
    damped = fisher + shift_amount[:, None, None] * jnp.eye(FBLK, dtype=jnp.float32)[None]
    factor = jnp.linalg.cholesky(damped)
    queries = query_grads.shape[0]
    rhs = jnp.transpose(query_grads.reshape(queries, nblocks, FBLK), (1, 2, 0))
    solved = jax.vmap(solve_block)(factor, rhs)
    pre = (jnp.transpose(solved, (2, 0, 1)).reshape(queries, feat_dev) / proj).astype(jnp.bfloat16)
    cycle = lax.axis_size("dp")
    everyone = lax.all_gather(pre, "dp", axis=0, tiled=True)
    scores = lax.dot_general(
        train_grads, everyone, (((1,), (1,)), ((), ())), preferred_element_type=jnp.float32
    )
    scores = scores.astype(jnp.bfloat16).reshape(train_rows, cycle, queries)
    summed = lax.psum_scatter(scores, "mp", scatter_dimension=0, tiled=True)
    return summed[:, :, None, :]


def per_device(query_ids, query_delta, doc_lengths, vocab_factor, output_factor, train_grads):
    owners = lax.axis_size("dp") * lax.axis_size("rep")
    fits = (
        train_grads.shape[1] == 2 * FBLK * owners
        and lax.axis_size("mp") == 2
        and lax.axis_size("rep") == 2
        and doc_lengths.shape[1] == FBLK
        and vocab_factor.shape[0] % FBLK == 0
    )
    body = split_over_blocks if fits else general
    return body(query_ids, query_delta, doc_lengths, vocab_factor, output_factor, train_grads)


def solution(mesh):
    placed = (
        P(("groups", "dp", "rep")),
        P(("groups", "dp", "rep"), "mp"),
        P(("groups", "dp", "rep"), None),
        P("mp", None),
        P("mp", None),
        P(("groups", "dp"), "mp"),
    )
    return jax.shard_map(
        per_device,
        mesh=mesh,
        in_specs=placed,
        out_specs=P(("groups", "dp", "mp"), None, "rep", None),
        check_vma=False,
    )
```

```python
import functools
import jax
import jax.numpy as jnp
from jax import lax
from jax.experimental import pallas as pl
from jax.experimental.pallas import tpu as pltpu
from jax.sharding import PartitionSpec as P

FBLK = 128
SLAB = FBLK + 8
PANEL = 8
COPIES = 4

damping = 0.1

VMEM = pl.BlockSpec(memory_space=pltpu.VMEM)
SMEM = pl.BlockSpec(memory_space=pltpu.SMEM)
HBM = pl.BlockSpec(memory_space=pl.ANY)


def call(kernel, outs, in_specs, scratch=(), vmem=48, flops=0, moved=0):
    return pl.pallas_call(
        kernel,
        out_shape=outs,
        in_specs=in_specs,
        scratch_shapes=list(scratch),
        compiler_params=pltpu.CompilerParams(vmem_limit_bytes=vmem << 20),
        cost_estimate=pl.CostEstimate(flops=flops, bytes_accessed=moved, transcendentals=0),
    )


def passed_along(shard, axis, by):
    size = lax.axis_size(axis)
    return lax.ppermute(shard, axis, [(i, (i + by) % size) for i in range(size)])


def square(dim):
    return lax.broadcasted_iota(jnp.int32, (FBLK, FBLK), dim)


def halves(value):
    high = value.astype(jnp.bfloat16)
    return high, (value - high.astype(jnp.float32)).astype(jnp.bfloat16)


def pack(first, second, spare=None):
    row, col = square(0), square(1)
    body = jnp.where(row >= col, first, second)
    diagonal = jnp.sum(jnp.where(row == col, second, 0.0), axis=0, keepdims=True)
    place = lax.broadcasted_iota(jnp.int32, (8, FBLK), 0)
    tail = jnp.where(place == 0, diagonal, 0.0)
    if spare is not None:
        tail = jnp.where(place == 1, spare, tail)
    return body, tail


def unpack(body, diagonal):
    row, col = square(0), square(1)
    turned = body.T
    first = jnp.where(row >= col, body, turned)
    second = jnp.where(row < col, body, jnp.where(row > col, turned, diagonal))
    return first, second


def grams(lengths, train, slabs):
    cycle = len(slabs)
    mine, half = lax.axis_index("dp"), lax.axis_index("rep")
    spare = lengths[...].astype(jnp.float32)
    for shift, slab in enumerate(slabs):
        owner = half * cycle + lax.rem(mine + shift, cycle)
        start = pl.multiple_of(owner * (2 * FBLK), 2 * FBLK)
        part = train[:, pl.ds(start, 2 * FBLK)]
        gram = lax.dot_general(part, part, (((0,), (0,)), ((), ())), preferred_element_type=jnp.float32)
        body, tail = pack(gram[:FBLK, :FBLK], gram[FBLK:, FBLK:], spare)
        slab[pl.ds(0, FBLK), :] = body
        slab[pl.ds(FBLK, 8), :] = tail


def thirds(value):
    high = value.astype(jnp.bfloat16)
    rest = value - high.astype(jnp.float32)
    middle = rest.astype(jnp.bfloat16)
    return high, middle, (rest - middle.astype(jnp.float32)).astype(jnp.bfloat16)


def at_rows(panel, first):
    pair = 2 * PANEL
    blank = jnp.zeros((PANEL, FBLK), jnp.float32)
    panel = panel.astype(jnp.float32)
    piece = jnp.concatenate([panel, blank] if first % pair == 0 else [blank, panel], axis=0).astype(jnp.bfloat16)
    before = first // pair * pair
    pieces = [jnp.zeros((before, FBLK), jnp.bfloat16), piece, jnp.zeros((FBLK - before - pair, FBLK), jnp.bfloat16)]
    return jnp.concatenate([piece for piece in pieces if piece.shape[0]], axis=0)


def product(left, right, first):
    high, middle, low = thirds(left)
    right_high, right_middle, right_low = (at_rows(part, first) for part in thirds(right))
    both = jnp.concatenate([right_high, right_middle], axis=1)
    large = jnp.dot(
        jnp.concatenate([high, middle], axis=1), jnp.concatenate([both, both], axis=0),
        preferred_element_type=jnp.float32,
    )
    small = jnp.dot(
        jnp.concatenate([high, low], axis=1), jnp.concatenate([right_low, right_high], axis=0),
        preferred_element_type=jnp.float32,
    )
    return large[:, :FBLK] + (large[:, FBLK:] + small)


def eliminated(panel, first):
    lane = lax.broadcasted_iota(jnp.int32, (PANEL, FBLK), 1)
    sublane = lax.broadcasted_iota(jnp.int32, (PANEL, FBLK), 0)
    within = (lane >= first) & (lane < first + PANEL)
    count = range(PANEL)

    def across(value, row):
        return jnp.broadcast_to(value[row:row + 1, :], (PANEL, FBLK))

    columns = [jnp.broadcast_to(panel[:, first + j:first + j + 1], (PANEL, FBLK)) for j in count]
    pivots = [[across(columns[j], i) if j >= i else None for j in count] for i in count]
    rest = jnp.where(within, jnp.where(lane == first + sublane, 1.0, 0.0), panel)
    lines = [across(rest, i) for i in count]
    for i in count:
        scale = 1.0 / pivots[i][i]
        scaled = lines[i] * scale
        shares = [pivots[i][j] * scale if j > i else None for j in count]
        for m in range(i + 1, PANEL):
            lines[m] = lines[m] - pivots[i][m] * scaled
            for j in range(m, PANEL):
                pivots[m][j] = pivots[m][j] - shares[m] * pivots[i][j]
        lines[i] = scaled
        pivots[i] = shares
    for i in reversed(count):
        for m in range(i):
            lines[m] = lines[m] - pivots[m][i] * lines[i]
    result = lines[0]
    for i in range(1, PANEL):
        result = jnp.where(sublane == i, lines[i], result)
    return result


def inverted(blocks):
    lane = square(1)
    for first in range(0, FBLK, PANEL):
        within = (lane >= first) & (lane < first + PANEL)
        panels = [eliminated(block[first:first + PANEL, :], first) for block in blocks]
        updates = [product(block, panel, first) for block, panel in zip(blocks, panels)]
        rests = [jnp.where(within, 0.0, block) - update for block, update in zip(blocks, updates)]
        blocks = [
            jnp.concatenate(
                [part for part in (rest[:first], panel, rest[first + PANEL:]) if part.shape[0]], axis=0
            )
            for rest, panel in zip(rests, panels)
        ]
    return blocks


def factor_kernel(examples, scale, *refs):
    slabs, out = refs[:-2], refs[-1]
    body = slabs[0][pl.ds(0, FBLK), :]
    diagonal = slabs[0][pl.ds(FBLK, 1), :]
    for slab in slabs[1:]:
        body = body + slab[pl.ds(0, FBLK), :]
        diagonal = diagonal + slab[pl.ds(FBLK, 1), :]
    same = square(0) == square(1)
    damped = []
    for gram in unpack(body, diagonal):
        fisher = gram / examples
        trace = jnp.sum(jnp.sum(jnp.where(same, fisher, 0.0), axis=0, keepdims=True), axis=1, keepdims=True)
        damped.append(fisher + jnp.where(same, damping * (trace / FBLK), 0.0))
    first, second = inverted(damped)
    body, tail = pack(first * scale, second * scale)
    out[pl.ds(0, FBLK), :] = body
    out[pl.ds(FBLK, 8), :] = tail


def first_kernel(ids_hbm, id_rows_hbm, delta_hbm, table_hbm, factor_hbm, lengths_hbm, train_hbm, sent, kept, *refs):
    slabs, (ids, id_rows, delta, table, factor, lengths, train, looked, sems) = refs[:-9], refs[-9:]
    model = lax.axis_index("mp")
    proj, vocab_rows = table.shape
    tokens = delta.shape[0]
    each = proj // lax.axis_size("mp")
    small = [
        pltpu.make_async_copy(source, target, sems.at[0, index])
        for index, (source, target) in enumerate((
            (factor_hbm, factor), (lengths_hbm, lengths), (train_hbm, train), (ids_hbm, ids), (id_rows_hbm, id_rows),
        ))
    ]
    tall, wide = tokens // COPIES, proj // COPIES
    get_delta = [
        pltpu.make_async_copy(delta_hbm.at[rows], delta.at[rows], sems.at[1, index])
        for index in range(COPIES) for rows in (pl.ds(index * tall, tall),)
    ]
    get_table = [
        pltpu.make_async_copy(table_hbm.at[rows], table.at[rows], sems.at[2, index])
        for index in range(COPIES) for rows in (pl.ds(index * wide, wide),)
    ]
    for copy in small[:2] + get_delta + small[2:] + get_table:
        copy.start()
    small[0].wait()
    for index, copy in enumerate(get_delta):
        copy.wait()
        rows = pl.ds(index * tall, tall)
        output = lax.dot_general(
            delta[rows, :], factor[...], (((1,), (1,)), ((), ())), preferred_element_type=jnp.float32
        )
        looked[:, rows] = output.T
    mine = looked[pl.ds(pl.multiple_of(model * each, each), each), :]
    other = looked[pl.ds(pl.multiple_of((1 - model) * each, each), each), :]
    kept[...] = mine
    high, low = halves(other)
    sent[pl.ds(0, each), :] = high
    sent[pl.ds(each, each), :] = low
    for copy in small[1:3]:
        copy.wait()
    grams(lengths, train, slabs)
    for copy in small[3:] + get_table:
        copy.wait()
    lanes = lax.broadcasted_iota(jnp.int32, (proj, FBLK), 1)
    first = model * vocab_rows

    def group(g, carry):
        gathered = jnp.zeros((proj, FBLK), jnp.bfloat16)
        base = g * FBLK
        for j in range(FBLK):
            local = ids[base + j] - first
            local = jnp.where((local >= 0) & (local < vocab_rows), local, 0)
            block = table[:, pl.ds(pl.multiple_of((local >> 7) * FBLK, FBLK), FBLK)]
            gathered = jnp.where(lanes == j, pltpu.roll(block, (j - local) & (FBLK - 1), 1), gathered)
        local = id_rows[pl.ds(g, 1), :] - first
        owned = (local >= 0) & (local < vocab_rows)
        spread = jnp.where(owned, 1.0, 0.0)
        gathered = (gathered.astype(jnp.float32) * spread).astype(jnp.bfloat16)
        sent[pl.ds(2 * each, proj), pl.ds(pl.multiple_of(base, FBLK), FBLK)] = gathered
        return carry

    lax.fori_loop(0, tokens // FBLK, group, 0)


def merge_kernel(kept, sent, got, out):
    each = kept.shape[0]
    received = got[pl.ds(0, each), :].astype(jnp.float32) + got[pl.ds(each, each), :].astype(jnp.float32)
    high, low = halves(kept[...] + received)
    out[pl.ds(0, each), :] = high
    out[pl.ds(each, each), :] = low
    rows = pl.ds(2 * each, out.shape[0] - 2 * each)
    out[rows, :] = sent[rows, :] + got[rows, :]


def queries_kernel(each, factors, slab, high_out, low_out):
    tokens = factors.shape[1]
    proj = factors.shape[0] - 2 * each
    queries = high_out.shape[1]
    lengths = slab[pl.ds(FBLK + 1, 1), :]
    upto = jnp.where(square(0) <= square(1), 1.0, 0.0).astype(jnp.bfloat16)
    ends = lax.dot_general(
        jnp.broadcast_to(lengths, (8, queries)).astype(jnp.bfloat16), upto, (((1,), (0,)), ((), ())),
        preferred_element_type=jnp.float32,
    )[:1]
    starts = ends - lengths
    place = lax.broadcasted_iota(jnp.int32, (tokens, queries), 0).astype(jnp.float32)
    inside = jnp.where((place >= starts) & (place < ends), 1.0, 0.0).astype(jnp.bfloat16)
    output = factors[pl.ds(0, each), :].astype(jnp.float32) + factors[pl.ds(each, each), :].astype(jnp.float32)
    inputs = factors[pl.ds(2 * each, proj), :].astype(jnp.float32)
    step = 8
    for start in range(0, each, step):
        grads = jnp.concatenate(
            [(inputs * output[r:r + 1, :]).astype(jnp.bfloat16) for r in range(start, start + step)], axis=0
        )
        summed = jnp.dot(grads, inside, preferred_element_type=jnp.float32)
        high, low = halves(summed)
        high_out[pl.ds(start * proj, step * proj), :] = high
        low_out[pl.ds(start * proj, step * proj), :] = low


def scores_kernel(cycle, count, *refs):
    own, peers = refs[:cycle], refs[cycle:2 * cycle]
    highs, lows = refs[2 * cycle:2 * cycle + count], refs[2 * cycle + count:2 * cycle + 2 * count]
    train, sent, kept, pre = refs[2 * cycle + 2 * count:]
    mine, rep, model = lax.axis_index("dp"), lax.axis_index("rep"), lax.axis_index("mp")
    for half, slabs in ((rep, own), (1 - rep, peers)):
        for shift in range(cycle):
            owner = half * cycle + lax.rem(mine + cycle - shift, cycle)
            slab = slabs[shift]
            blocks = unpack(slab[pl.ds(0, FBLK), :], slab[pl.ds(FBLK, 1), :])
            for index, block in enumerate(blocks):
                rows = pl.ds(pl.multiple_of(owner * (2 * FBLK) + index * FBLK, FBLK), FBLK)
                high, low = halves(block)
                right_high = jnp.concatenate([ref[rows, :] for ref in highs], axis=1)
                right_low = jnp.concatenate([ref[rows, :] for ref in lows], axis=1)
                solved = jnp.dot(
                    jnp.concatenate([high, high, low], axis=1),
                    jnp.concatenate([right_high, right_low, right_high], axis=0),
                    preferred_element_type=jnp.float32,
                )
                pre[rows, :] = solved.astype(jnp.bfloat16)
    half_rows = sent.shape[0]
    for out, which in ((sent, 1 - model), (kept, model)):
        rows = pl.ds(pl.multiple_of(which * half_rows, half_rows), half_rows)
        out[...] = jnp.dot(train[rows, :], pre[...], preferred_element_type=jnp.float32).astype(jnp.bfloat16)


def total_kernel(cycle, count, *refs):
    pieces, out = refs[:-1], refs[-1]
    mine = lax.axis_index("dp")
    sums = []
    for kept, got in zip(pieces[::2], pieces[1::2]):
        both = kept[...].astype(jnp.float32) + got[...].astype(jnp.float32)
        sums += [both[:, index * FBLK:(index + 1) * FBLK] for index in range(count)]
    placed = []
    for source in range(cycle):
        shift = lax.rem(mine + cycle - source, cycle)
        value = sums[0]
        for index in range(1, cycle):
            value = jnp.where(shift == index, sums[index], value)
        placed.append(value)
    out[...] = jnp.stack(placed, axis=1).astype(jnp.bfloat16)


def shape(dims, dtype):
    return jax.ShapeDtypeStruct(dims, dtype)


def split_over_blocks(query_ids, query_delta, doc_lengths, vocab_factor, output_factor, train_grads):
    cycle = lax.axis_size("dp")
    tokens, width = query_delta.shape
    proj = output_factor.shape[1]
    each = proj // lax.axis_size("mp")
    vocab_rows = vocab_factor.shape[0]
    train_rows, feat = train_grads.shape
    queries = doc_lengths.shape[1]
    bf16, f32 = jnp.bfloat16, jnp.float32

    sent, kept, *slabs = call(
        first_kernel,
        [shape((2 * each + proj, tokens), bf16), shape((each, tokens), f32)] + [shape((SLAB, FBLK), f32)] * cycle,
        [HBM] * 7,
        [
            pltpu.SMEM((tokens,), jnp.int32),
            pltpu.VMEM((tokens // FBLK, FBLK), jnp.int32),
            pltpu.VMEM((tokens, width), bf16),
            pltpu.VMEM((proj, vocab_rows), bf16),
            pltpu.VMEM((proj, width), bf16),
            pltpu.VMEM((1, queries), jnp.int32),
            pltpu.VMEM((train_rows, feat), bf16),
            pltpu.VMEM((proj, tokens), f32),
            pltpu.SemaphoreType.DMA((3, 8)),
        ],
        vmem=62,
        flops=2 * tokens * width * proj,
        moved=2 * (tokens * width + proj * vocab_rows) * 2,
    )(
        query_ids, query_ids.reshape(tokens // FBLK, FBLK), query_delta, vocab_factor.T, output_factor.T,
        doc_lengths, train_grads,
    )
    got = passed_along(sent, "mp", 1)
    parts = [slabs[0]] + [passed_along(slabs[s], "dp", s) for s in range(1, cycle)]

    factors = call(
        merge_kernel,
        shape(sent.shape, bf16),
        [VMEM, VMEM, VMEM],
        vmem=16,
        flops=tokens * each,
        moved=8 * tokens * each * 4,
    )(kept, sent, got)
    gathered = [factors] + [passed_along(factors, "dp", s) for s in range(1, cycle)]

    inverse = call(
        functools.partial(factor_kernel, train_rows * cycle, 1.0 / proj),
        shape((SLAB, FBLK), f32),
        [VMEM] * cycle + [HBM],
        vmem=16,
        flops=10 ** 10,
        moved=10 ** 6,
    )(*parts, factors)
    inverses = [inverse] + [passed_along(inverse, "dp", s) for s in range(1, cycle)]
    peers = [passed_along(slab, "rep", 1) for slab in inverses]

    highs, lows = [], []
    for s in range(cycle):
        high, low = call(
            functools.partial(queries_kernel, each),
            [shape((feat, queries), bf16)] * 2,
            [VMEM, VMEM],
            vmem=24,
            flops=2 * feat * tokens * queries,
            moved=6 * feat * queries,
        )(gathered[s], parts[s])
        highs.append(high)
        lows.append(low)

    half_rows = train_rows // lax.axis_size("mp")
    count = cycle // 2
    pieces = []
    for start in range(0, cycle, count):
        outgoing, own = call(
            functools.partial(scores_kernel, cycle, count),
            [shape((half_rows, count * queries), bf16)] * 2,
            [VMEM] * (2 * cycle + 2 * count + 1),
            [pltpu.VMEM((feat, count * queries), bf16)],
            vmem=24,
            flops=2 * train_rows * feat * count * queries,
            moved=8 * feat * queries * count,
        )(*inverses, *peers, *highs[start:start + count], *lows[start:start + count], train_grads)
        pieces += [own, passed_along(outgoing, "mp", 1)]
    total = call(
        functools.partial(total_kernel, cycle, count),
        shape((half_rows, cycle, queries), bf16),
        [VMEM] * len(pieces),
        vmem=16,
        flops=half_rows * cycle * queries,
        moved=6 * half_rows * cycle * queries,
    )(*pieces)
    return total[:, :, None, :]


def doc_matrix(lengths_row, count):
    ends = jnp.cumsum(lengths_row)
    starts = ends - lengths_row
    place = jnp.arange(count, dtype=jnp.int32)
    inside = (place[None, :] >= starts[:, None]) & (place[None, :] < ends[:, None])
    return inside.astype(jnp.bfloat16)


def solve_block(factor, rhs):
    return jax.scipy.linalg.cho_solve((factor, True), rhs)


def general(query_ids, query_delta, doc_lengths, vocab_factor, output_factor, train_grads):
    model_count = lax.axis_size("mp")
    model_index = lax.axis_index("mp")
    vocab_rows = vocab_factor.shape[0]
    local_ids = query_ids - model_index * vocab_rows
    owned = (local_ids >= 0) & (local_ids < vocab_rows)
    looked = vocab_factor[jnp.clip(local_ids, 0, vocab_rows - 1)].astype(jnp.float32)
    vocab_part = jnp.where(owned[:, None], looked, jnp.zeros_like(looked))
    output_part = jnp.dot(query_delta, output_factor, preferred_element_type=jnp.float32)
    input_side, output_side = lax.psum((vocab_part, output_part), "mp")
    proj = output_side.shape[1]
    rows_each = proj // model_count
    mine = lax.dynamic_slice_in_dim(output_side, model_index * rows_each, rows_each, 1)
    token_count = query_ids.shape[0]
    token_grads = (
        (mine[:, :, None] * input_side[:, None, :])
        .reshape(token_count, rows_each * proj)
        .astype(jnp.bfloat16)
    )
    query_grads = jnp.dot(
        doc_matrix(doc_lengths[0], token_count), token_grads, preferred_element_type=jnp.float32
    )
    train_rows, feat_dev = train_grads.shape
    nblocks = feat_dev // FBLK
    tiled = train_grads.reshape(train_rows, nblocks, FBLK)
    local_gram = jnp.einsum("tbi,tbj->bij", tiled, tiled, preferred_element_type=jnp.float32)
    total_gram = lax.psum(local_gram, "dp")
    fisher = total_gram / (train_rows * lax.axis_size("dp"))
    shift_amount = damping * (jnp.trace(fisher, axis1=1, axis2=2) / FBLK)
    damped = fisher + shift_amount[:, None, None] * jnp.eye(FBLK, dtype=jnp.float32)[None]
    factor = jnp.linalg.cholesky(damped)
    queries = query_grads.shape[0]
    rhs = jnp.transpose(query_grads.reshape(queries, nblocks, FBLK), (1, 2, 0))
    solved = jax.vmap(solve_block)(factor, rhs)
    pre = (jnp.transpose(solved, (2, 0, 1)).reshape(queries, feat_dev) / proj).astype(jnp.bfloat16)
    cycle = lax.axis_size("dp")
    everyone = lax.all_gather(pre, "dp", axis=0, tiled=True)
    scores = lax.dot_general(
        train_grads, everyone, (((1,), (1,)), ((), ())), preferred_element_type=jnp.float32
    )
    scores = scores.astype(jnp.bfloat16).reshape(train_rows, cycle, queries)
    summed = lax.psum_scatter(scores, "mp", scatter_dimension=0, tiled=True)
    return summed[:, :, None, :]


def per_device(query_ids, query_delta, doc_lengths, vocab_factor, output_factor, train_grads):
    owners = lax.axis_size("dp") * lax.axis_size("rep")
    fits = (
        train_grads.shape[1] == 2 * FBLK * owners
        and lax.axis_size("mp") == 2
        and lax.axis_size("rep") == 2
        and doc_lengths.shape[1] == FBLK
        and vocab_factor.shape[0] % FBLK == 0
    )
    body = split_over_blocks if fits else general
    return body(query_ids, query_delta, doc_lengths, vocab_factor, output_factor, train_grads)


def solution(mesh):
    placed = (
        P(("groups", "dp", "rep")),
        P(("groups", "dp", "rep"), "mp"),
        P(("groups", "dp", "rep"), None),
        P("mp", None),
        P("mp", None),
        P(("groups", "dp"), "mp"),
    )
    return jax.shard_map(
        per_device,
        mesh=mesh,
        in_specs=placed,
        out_specs=P(("groups", "dp", "mp"), None, "rep", None),
        check_vma=False,
    )
```

```python
import functools
import jax
import jax.numpy as jnp
from jax import lax
from jax.experimental import pallas as pl
from jax.experimental.pallas import tpu as pltpu
from jax.sharding import PartitionSpec as P

FBLK = 128
SLAB = FBLK + 8
PANEL = 8
COPIES = 4

damping = 0.1

VMEM = pl.BlockSpec(memory_space=pltpu.VMEM)
SMEM = pl.BlockSpec(memory_space=pltpu.SMEM)
HBM = pl.BlockSpec(memory_space=pl.ANY)


def call(kernel, outs, in_specs, scratch=(), vmem=48, flops=0, moved=0):
    return pl.pallas_call(
        kernel,
        out_shape=outs,
        in_specs=in_specs,
        scratch_shapes=list(scratch),
        compiler_params=pltpu.CompilerParams(vmem_limit_bytes=vmem << 20),
        cost_estimate=pl.CostEstimate(flops=flops, bytes_accessed=moved, transcendentals=0),
    )


def passed_along(shard, axis, by):
    size = lax.axis_size(axis)
    return lax.ppermute(shard, axis, [(i, (i + by) % size) for i in range(size)])


def square(dim):
    return lax.broadcasted_iota(jnp.int32, (FBLK, FBLK), dim)


def halves(value):
    high = value.astype(jnp.bfloat16)
    return high, (value - high.astype(jnp.float32)).astype(jnp.bfloat16)


def pack(first, second, spare=None):
    row, col = square(0), square(1)
    body = jnp.where(row >= col, first, second)
    diagonal = jnp.sum(jnp.where(row == col, second, 0.0), axis=0, keepdims=True)
    place = lax.broadcasted_iota(jnp.int32, (8, FBLK), 0)
    tail = jnp.where(place == 0, diagonal, 0.0)
    if spare is not None:
        tail = jnp.where(place == 1, spare, tail)
    return body, tail


def unpack(body, diagonal):
    row, col = square(0), square(1)
    turned = body.T
    first = jnp.where(row >= col, body, turned)
    second = jnp.where(row < col, body, jnp.where(row > col, turned, diagonal))
    return first, second


def grams(lengths, train, slabs):
    cycle = len(slabs)
    mine, half = lax.axis_index("dp"), lax.axis_index("rep")
    spare = lengths[...].astype(jnp.float32)
    for shift, slab in enumerate(slabs):
        owner = half * cycle + lax.rem(mine + shift, cycle)
        start = pl.multiple_of(owner * (2 * FBLK), 2 * FBLK)
        part = train[:, pl.ds(start, 2 * FBLK)]
        gram = lax.dot_general(part, part, (((0,), (0,)), ((), ())), preferred_element_type=jnp.float32)
        body, tail = pack(gram[:FBLK, :FBLK], gram[FBLK:, FBLK:], spare)
        slab[pl.ds(0, FBLK), :] = body
        slab[pl.ds(FBLK, 8), :] = tail


def thirds(value):
    high = value.astype(jnp.bfloat16)
    rest = value - high.astype(jnp.float32)
    middle = rest.astype(jnp.bfloat16)
    return high, middle, (rest - middle.astype(jnp.float32)).astype(jnp.bfloat16)


def at_rows(panel, first):
    pair = 2 * PANEL
    blank = jnp.zeros((PANEL, FBLK), jnp.float32)
    panel = panel.astype(jnp.float32)
    piece = jnp.concatenate([panel, blank] if first % pair == 0 else [blank, panel], axis=0).astype(jnp.bfloat16)
    before = first // pair * pair
    pieces = [jnp.zeros((before, FBLK), jnp.bfloat16), piece, jnp.zeros((FBLK - before - pair, FBLK), jnp.bfloat16)]
    return jnp.concatenate([piece for piece in pieces if piece.shape[0]], axis=0)


def product(left, right, first):
    high, middle, low = thirds(left)
    right_high, right_middle, right_low = (at_rows(part, first) for part in thirds(right))
    both = jnp.concatenate([right_high, right_middle], axis=1)
    large = jnp.dot(
        jnp.concatenate([high, middle], axis=1), jnp.concatenate([both, both], axis=0),
        preferred_element_type=jnp.float32,
    )
    small = jnp.dot(
        jnp.concatenate([high, low], axis=1), jnp.concatenate([right_low, right_high], axis=0),
        preferred_element_type=jnp.float32,
    )
    return large[:, :FBLK] + (large[:, FBLK:] + small)


def eliminated(panel, first):
    lane = lax.broadcasted_iota(jnp.int32, (PANEL, FBLK), 1)
    sublane = lax.broadcasted_iota(jnp.int32, (PANEL, FBLK), 0)
    within = (lane >= first) & (lane < first + PANEL)
    count = range(PANEL)

    def across(value, row):
        return jnp.broadcast_to(value[row:row + 1, :], (PANEL, FBLK))

    columns = [jnp.broadcast_to(panel[:, first + j:first + j + 1], (PANEL, FBLK)) for j in count]
    pivots = [[across(columns[j], i) if j >= i else None for j in count] for i in count]
    rest = jnp.where(within, jnp.where(lane == first + sublane, 1.0, 0.0), panel)
    lines = [across(rest, i) for i in count]
    for i in count:
        scale = 1.0 / pivots[i][i]
        scaled = lines[i] * scale
        shares = [pivots[i][j] * scale if j > i else None for j in count]
        for m in range(i + 1, PANEL):
            lines[m] = lines[m] - pivots[i][m] * scaled
            for j in range(m, PANEL):
                pivots[m][j] = pivots[m][j] - shares[m] * pivots[i][j]
        lines[i] = scaled
        pivots[i] = shares
    for i in reversed(count):
        for m in range(i):
            lines[m] = lines[m] - pivots[m][i] * lines[i]
    result = lines[0]
    for i in range(1, PANEL):
        result = jnp.where(sublane == i, lines[i], result)
    return result


def inverted(blocks):
    lane = square(1)
    for first in range(0, FBLK, PANEL):
        within = (lane >= first) & (lane < first + PANEL)
        panels = [eliminated(block[first:first + PANEL, :], first) for block in blocks]
        updates = [product(block, panel, first) for block, panel in zip(blocks, panels)]
        rests = [jnp.where(within, 0.0, block) - update for block, update in zip(blocks, updates)]
        blocks = [
            jnp.concatenate(
                [part for part in (rest[:first], panel, rest[first + PANEL:]) if part.shape[0]], axis=0
            )
            for rest, panel in zip(rests, panels)
        ]
    return blocks


def factor_kernel(examples, scale, *refs):
    slabs, out = refs[:-2], refs[-1]
    body = slabs[0][pl.ds(0, FBLK), :]
    diagonal = slabs[0][pl.ds(FBLK, 1), :]
    for slab in slabs[1:]:
        body = body + slab[pl.ds(0, FBLK), :]
        diagonal = diagonal + slab[pl.ds(FBLK, 1), :]
    same = square(0) == square(1)
    damped = []
    for gram in unpack(body, diagonal):
        fisher = gram / examples
        trace = jnp.sum(jnp.sum(jnp.where(same, fisher, 0.0), axis=0, keepdims=True), axis=1, keepdims=True)
        damped.append(fisher + jnp.where(same, damping * (trace / FBLK), 0.0))
    first, second = inverted(damped)
    body, tail = pack(first * scale, second * scale)
    out[pl.ds(0, FBLK), :] = body
    out[pl.ds(FBLK, 8), :] = tail


def first_kernel(id_rows_hbm, delta_hbm, table_hbm, factor_hbm, lengths_hbm, train_hbm, sent, own, *refs):
    slabs, refs = refs[:-10], refs[-10:]
    id_rows, places, reads, delta, table, factor, lengths, train, looked, sems = refs
    model = lax.axis_index("mp")
    proj, vocab_rows = table.shape
    tokens = delta.shape[0]
    each = proj // lax.axis_size("mp")
    small = [
        pltpu.make_async_copy(source, target, sems.at[0, index])
        for index, (source, target) in enumerate((
            (id_rows_hbm, id_rows), (factor_hbm, factor), (lengths_hbm, lengths), (train_hbm, train),
        ))
    ]
    tall, wide = tokens // COPIES, proj // COPIES
    get_delta = [
        pltpu.make_async_copy(delta_hbm.at[rows], delta.at[rows], sems.at[1, index])
        for index in range(COPIES) for rows in (pl.ds(index * tall, tall),)
    ]
    get_table = [
        pltpu.make_async_copy(table_hbm.at[rows], table.at[rows], sems.at[2, index])
        for index in range(COPIES) for rows in (pl.ds(index * wide, wide),)
    ]
    for copy in small[:3] + get_delta + small[3:] + get_table:
        copy.start()
    small[0].wait()
    local = id_rows[...] - model * vocab_rows
    owned = (local >= 0) & (local < vocab_rows)
    local = jnp.where(owned, local, 0)
    low = FBLK - 1
    roll = (lax.broadcasted_iota(jnp.int32, local.shape, 1) - local) & low
    places[...] = (local & ~low) | roll
    fetch = pltpu.make_async_copy(places, reads, sems.at[0, 4])
    fetch.start()
    small[1].wait()
    for index, copy in enumerate(get_delta):
        copy.wait()
        rows = pl.ds(index * tall, tall)
        output = lax.dot_general(
            delta[rows, :], factor[...], (((1,), (1,)), ((), ())), preferred_element_type=jnp.float32
        )
        looked[:, rows] = output.T
    mine = looked[pl.ds(pl.multiple_of(model * each, each), each), :]
    other = looked[pl.ds(pl.multiple_of((1 - model) * each, each), each), :]
    for target, value in ((own, mine), (sent, other)):
        high, rest = halves(value)
        target[pl.ds(0, each), :] = high
        target[pl.ds(each, each), :] = rest
    for copy in small[2:]:
        copy.wait()
    grams(lengths, train, slabs)
    fetch.wait()
    for copy in get_table:
        copy.wait()
    lanes = lax.broadcasted_iota(jnp.int32, (proj, FBLK), 1)
    places[...] = owned.astype(jnp.int32)

    def group(g, carry):
        gathered = jnp.zeros((proj, FBLK), jnp.bfloat16)
        for j in range(FBLK):
            place = reads[g, j]
            block = table[:, pl.ds(pl.multiple_of(place & ~low, FBLK), FBLK)]
            gathered = jnp.where(lanes == j, pltpu.roll(block, place & low, 1), gathered)
        held = places[pl.ds(g, 1), :].astype(jnp.float32)
        gathered = (gathered.astype(jnp.float32) * held).astype(jnp.bfloat16)
        columns = pl.ds(pl.multiple_of(g * FBLK, FBLK), FBLK)
        sent[pl.ds(2 * each, proj), columns] = gathered
        own[pl.ds(2 * each, proj), columns] = gathered
        return carry

    lax.fori_loop(0, tokens // FBLK, group, 0)


def merge_kernel(each, own, got, out):
    def value(ref):
        return ref[pl.ds(0, each), :].astype(jnp.float32) + ref[pl.ds(each, each), :].astype(jnp.float32)

    high, low = halves(value(own) + value(got))
    out[pl.ds(0, each), :] = high
    out[pl.ds(each, each), :] = low
    rows = pl.ds(2 * each, out.shape[0] - 2 * each)
    out[rows, :] = own[rows, :] + got[rows, :]


def queries_kernel(each, factors, slab, *refs):
    after, high_out, low_out, again = refs if len(refs) == 4 else (None, *refs, None)
    if again is not None:
        again[...] = factors[...]
    tokens = factors.shape[1]
    proj = factors.shape[0] - 2 * each
    queries = high_out.shape[1]
    lengths = slab[pl.ds(FBLK + 1, 1), :]
    upto = jnp.where(square(0) <= square(1), 1.0, 0.0).astype(jnp.bfloat16)
    ends = lax.dot_general(
        jnp.broadcast_to(lengths, (8, queries)).astype(jnp.bfloat16), upto, (((1,), (0,)), ((), ())),
        preferred_element_type=jnp.float32,
    )[:1]
    starts = ends - lengths
    place = lax.broadcasted_iota(jnp.int32, (tokens, queries), 0).astype(jnp.float32)
    inside = jnp.where((place >= starts) & (place < ends), 1.0, 0.0).astype(jnp.bfloat16)
    output = factors[pl.ds(0, each), :].astype(jnp.float32) + factors[pl.ds(each, each), :].astype(jnp.float32)
    inputs = factors[pl.ds(2 * each, proj), :].astype(jnp.float32)
    step = 8
    for start in range(0, each, step):
        grads = jnp.concatenate(
            [(inputs * output[r:r + 1, :]).astype(jnp.bfloat16) for r in range(start, start + step)], axis=0
        )
        summed = jnp.dot(grads, inside, preferred_element_type=jnp.float32)
        high, low = halves(summed)
        high_out[pl.ds(start * proj, step * proj), :] = high
        low_out[pl.ds(start * proj, step * proj), :] = low


def scores_kernel(cycle, count, *refs):
    own, peers = refs[:cycle], refs[cycle:2 * cycle]
    highs, lows = refs[2 * cycle:2 * cycle + count], refs[2 * cycle + count:2 * cycle + 2 * count]
    train, sent, kept, pre = refs[2 * cycle + 2 * count:]
    mine, rep, model = lax.axis_index("dp"), lax.axis_index("rep"), lax.axis_index("mp")
    for half, slabs in ((rep, own), (1 - rep, peers)):
        for shift in range(cycle):
            owner = half * cycle + lax.rem(mine + cycle - shift, cycle)
            slab = slabs[shift]
            blocks = unpack(slab[pl.ds(0, FBLK), :], slab[pl.ds(FBLK, 1), :])
            for index, block in enumerate(blocks):
                rows = pl.ds(pl.multiple_of(owner * (2 * FBLK) + index * FBLK, FBLK), FBLK)
                high, low = halves(block)
                right_high = jnp.concatenate([ref[rows, :] for ref in highs], axis=1)
                right_low = jnp.concatenate([ref[rows, :] for ref in lows], axis=1)
                solved = jnp.dot(
                    jnp.concatenate([high, high, low], axis=1),
                    jnp.concatenate([right_high, right_low, right_high], axis=0),
                    preferred_element_type=jnp.float32,
                )
                pre[rows, :] = solved.astype(jnp.bfloat16)
    half_rows = sent.shape[0]
    for out, which in ((sent, 1 - model), (kept, model)):
        rows = pl.ds(pl.multiple_of(which * half_rows, half_rows), half_rows)
        out[...] = jnp.dot(train[rows, :], pre[...], preferred_element_type=jnp.float32).astype(jnp.bfloat16)


def total_kernel(order, *refs):
    pieces, out = refs[:-1], refs[-1]
    mine, cycle = lax.axis_index("dp"), len(order)
    sums = {}
    for kept, got in zip(pieces[::2], pieces[1::2]):
        both = kept[...].astype(jnp.float32) + got[...].astype(jnp.float32)
        for index in range(both.shape[1] // FBLK):
            sums[order[len(sums)]] = both[:, index * FBLK:(index + 1) * FBLK]
    placed = []
    for source in range(cycle):
        shift = lax.rem(mine + cycle - source, cycle)
        value = sums[0]
        for index in range(1, cycle):
            value = jnp.where(shift == index, sums[index], value)
        placed.append(value)
    out[...] = jnp.stack(placed, axis=1).astype(jnp.bfloat16)


def shape(dims, dtype):
    return jax.ShapeDtypeStruct(dims, dtype)


def split_over_blocks(query_ids, query_delta, doc_lengths, vocab_factor, output_factor, train_grads):
    cycle = lax.axis_size("dp")
    tokens, width = query_delta.shape
    proj = output_factor.shape[1]
    each = proj // lax.axis_size("mp")
    vocab_rows = vocab_factor.shape[0]
    train_rows, feat = train_grads.shape
    queries = doc_lengths.shape[1]
    bf16, f32 = jnp.bfloat16, jnp.float32

    sent, own, *slabs = call(
        first_kernel,
        [shape((2 * each + proj, tokens), bf16)] * 2 + [shape((SLAB, FBLK), f32)] * cycle,
        [HBM] * 6,
        [
            pltpu.VMEM((tokens // FBLK, FBLK), jnp.int32),
            pltpu.VMEM((tokens // FBLK, FBLK), jnp.int32),
            pltpu.SMEM((tokens // FBLK, FBLK), jnp.int32),
            pltpu.VMEM((tokens, width), bf16),
            pltpu.VMEM((proj, vocab_rows), bf16),
            pltpu.VMEM((proj, width), bf16),
            pltpu.VMEM((1, queries), jnp.int32),
            pltpu.VMEM((train_rows, feat), bf16),
            pltpu.VMEM((proj, tokens), f32),
            pltpu.SemaphoreType.DMA((3, 8)),
        ],
        vmem=62,
        flops=2 * tokens * width * proj,
        moved=2 * (tokens * width + proj * vocab_rows) * 2,
    )(
        query_ids.reshape(tokens // FBLK, FBLK), query_delta, vocab_factor.T, output_factor.T,
        doc_lengths, train_grads,
    )
    got = passed_along(sent, "mp", 1)
    parts = [slabs[0]] + [passed_along(slabs[s], "dp", s) for s in range(1, cycle)]

    factors = call(
        functools.partial(merge_kernel, each),
        shape(sent.shape, bf16),
        [VMEM, VMEM],
        vmem=16,
        flops=tokens * each,
        moved=8 * tokens * each * 4,
    )(own, got)
    late = cycle // 2
    gathered = [factors] + [passed_along(factors, "dp", s) if s != late else None for s in range(1, cycle)]

    inverse = call(
        functools.partial(factor_kernel, train_rows * cycle, 1.0 / proj),
        shape((SLAB, FBLK), f32),
        [VMEM] * cycle + [HBM],
        vmem=16,
        flops=10 ** 10,
        moved=10 ** 6,
    )(*parts, factors)
    inverses = [inverse] + [passed_along(inverse, "dp", s) for s in range(1, cycle)]
    peers = [passed_along(slab, "rep", 1) for slab in inverses]

    highs, lows = {}, {}
    for s in sorted(range(cycle), key=lambda shift: (shift == late, shift)):
        first = s == 0
        highs[s], lows[s], *again = call(
            functools.partial(queries_kernel, each),
            [shape((feat, queries), bf16)] * 2 + [shape(factors.shape, bf16)] * first,
            [VMEM, VMEM] + [HBM] * first,
            vmem=24,
            flops=2 * feat * tokens * queries,
            moved=6 * feat * queries,
        )(gathered[s], parts[s], *[inverse] * first)
        if first:
            gathered[late] = passed_along(again[0], "dp", late)

    half_rows = train_rows // lax.axis_size("mp")
    pieces, order = [], []
    for chosen in ([s for s in range(cycle) if s != late], [late]):
        count = len(chosen)
        outgoing, kept = call(
            functools.partial(scores_kernel, cycle, count),
            [shape((half_rows, count * queries), bf16)] * 2,
            [VMEM] * (2 * cycle + 2 * count + 1),
            [pltpu.VMEM((feat, count * queries), bf16)],
            vmem=24,
            flops=2 * train_rows * feat * count * queries,
            moved=8 * feat * queries * count,
        )(*inverses, *peers, *[highs[s] for s in chosen], *[lows[s] for s in chosen], train_grads)
        pieces += [kept, passed_along(outgoing, "mp", 1)]
        order += chosen
    total = call(
        functools.partial(total_kernel, order),
        shape((half_rows, cycle, queries), bf16),
        [VMEM] * len(pieces),
        vmem=16,
        flops=half_rows * cycle * queries,
        moved=6 * half_rows * cycle * queries,
    )(*pieces)
    return total[:, :, None, :]


def doc_matrix(lengths_row, count):
    ends = jnp.cumsum(lengths_row)
    starts = ends - lengths_row
    place = jnp.arange(count, dtype=jnp.int32)
    inside = (place[None, :] >= starts[:, None]) & (place[None, :] < ends[:, None])
    return inside.astype(jnp.bfloat16)


def solve_block(factor, rhs):
    return jax.scipy.linalg.cho_solve((factor, True), rhs)


def general(query_ids, query_delta, doc_lengths, vocab_factor, output_factor, train_grads):
    model_count = lax.axis_size("mp")
    model_index = lax.axis_index("mp")
    vocab_rows = vocab_factor.shape[0]
    local_ids = query_ids - model_index * vocab_rows
    owned = (local_ids >= 0) & (local_ids < vocab_rows)
    looked = vocab_factor[jnp.clip(local_ids, 0, vocab_rows - 1)].astype(jnp.float32)
    vocab_part = jnp.where(owned[:, None], looked, jnp.zeros_like(looked))
    output_part = jnp.dot(query_delta, output_factor, preferred_element_type=jnp.float32)
    input_side, output_side = lax.psum((vocab_part, output_part), "mp")
    proj = output_side.shape[1]
    rows_each = proj // model_count
    mine = lax.dynamic_slice_in_dim(output_side, model_index * rows_each, rows_each, 1)
    token_count = query_ids.shape[0]
    token_grads = (
        (mine[:, :, None] * input_side[:, None, :])
        .reshape(token_count, rows_each * proj)
        .astype(jnp.bfloat16)
    )
    query_grads = jnp.dot(
        doc_matrix(doc_lengths[0], token_count), token_grads, preferred_element_type=jnp.float32
    )
    train_rows, feat_dev = train_grads.shape
    nblocks = feat_dev // FBLK
    tiled = train_grads.reshape(train_rows, nblocks, FBLK)
    local_gram = jnp.einsum("tbi,tbj->bij", tiled, tiled, preferred_element_type=jnp.float32)
    total_gram = lax.psum(local_gram, "dp")
    fisher = total_gram / (train_rows * lax.axis_size("dp"))
    shift_amount = damping * (jnp.trace(fisher, axis1=1, axis2=2) / FBLK)
    damped = fisher + shift_amount[:, None, None] * jnp.eye(FBLK, dtype=jnp.float32)[None]
    factor = jnp.linalg.cholesky(damped)
    queries = query_grads.shape[0]
    rhs = jnp.transpose(query_grads.reshape(queries, nblocks, FBLK), (1, 2, 0))
    solved = jax.vmap(solve_block)(factor, rhs)
    pre = (jnp.transpose(solved, (2, 0, 1)).reshape(queries, feat_dev) / proj).astype(jnp.bfloat16)
    cycle = lax.axis_size("dp")
    everyone = lax.all_gather(pre, "dp", axis=0, tiled=True)
    scores = lax.dot_general(
        train_grads, everyone, (((1,), (1,)), ((), ())), preferred_element_type=jnp.float32
    )
    scores = scores.astype(jnp.bfloat16).reshape(train_rows, cycle, queries)
    summed = lax.psum_scatter(scores, "mp", scatter_dimension=0, tiled=True)
    return summed[:, :, None, :]


def per_device(query_ids, query_delta, doc_lengths, vocab_factor, output_factor, train_grads):
    owners = lax.axis_size("dp") * lax.axis_size("rep")
    fits = (
        train_grads.shape[1] == 2 * FBLK * owners
        and lax.axis_size("mp") == 2
        and lax.axis_size("rep") == 2
        and doc_lengths.shape[1] == FBLK
        and vocab_factor.shape[0] % FBLK == 0
    )
    body = split_over_blocks if fits else general
    return body(query_ids, query_delta, doc_lengths, vocab_factor, output_factor, train_grads)


def solution(mesh):
    placed = (
        P(("groups", "dp", "rep")),
        P(("groups", "dp", "rep"), "mp"),
        P(("groups", "dp", "rep"), None),
        P("mp", None),
        P("mp", None),
        P(("groups", "dp"), "mp"),
    )
    return jax.shard_map(
        per_device,
        mesh=mesh,
        in_specs=placed,
        out_specs=P(("groups", "dp", "mp"), None, "rep", None),
        check_vma=False,
    )
```

```python
import functools
import jax
import jax.numpy as jnp
from jax import lax
from jax.experimental import pallas as pl
from jax.experimental.pallas import tpu as pltpu
from jax.sharding import PartitionSpec as P

FBLK = 128
SLAB = FBLK + 8
PANEL = 8
ROWS = 16

damping = 0.1

VMEM = pl.BlockSpec(memory_space=pltpu.VMEM)
SMEM = pl.BlockSpec(memory_space=pltpu.SMEM)
HBM = pl.BlockSpec(memory_space=pl.ANY)


def call(kernel, outs, in_specs, scratch=(), vmem=48, flops=0, moved=0):
    return pl.pallas_call(
        kernel,
        out_shape=outs,
        in_specs=in_specs,
        scratch_shapes=list(scratch),
        compiler_params=pltpu.CompilerParams(vmem_limit_bytes=vmem << 20),
        cost_estimate=pl.CostEstimate(flops=flops, bytes_accessed=moved, transcendentals=0),
    )


def passed_along(shard, axis, by):
    size = lax.axis_size(axis)
    return lax.ppermute(shard, axis, [(i, (i + by) % size) for i in range(size)])


def square(dim):
    return lax.broadcasted_iota(jnp.int32, (FBLK, FBLK), dim)


def halves(value):
    high = value.astype(jnp.bfloat16)
    return high, (value - high.astype(jnp.float32)).astype(jnp.bfloat16)


def pack(first, second, spare=None):
    row, col = square(0), square(1)
    body = jnp.where(row >= col, first, second)
    diagonal = jnp.sum(jnp.where(row == col, second, 0.0), axis=0, keepdims=True)
    place = lax.broadcasted_iota(jnp.int32, (8, FBLK), 0)
    tail = jnp.where(place == 0, diagonal, 0.0)
    if spare is not None:
        tail = jnp.where(place == 1, spare, tail)
    return body, tail


def unpack(body, diagonal):
    row, col = square(0), square(1)
    turned = body.T
    first = jnp.where(row >= col, body, turned)
    second = jnp.where(row < col, body, jnp.where(row > col, turned, diagonal))
    return first, second


def grams(lengths, train, slabs):
    cycle = len(slabs)
    mine, half = lax.axis_index("dp"), lax.axis_index("rep")
    spare = lengths[...].astype(jnp.float32)
    for shift, slab in enumerate(slabs):
        owner = half * cycle + lax.rem(mine + shift, cycle)
        start = pl.multiple_of(owner * (2 * FBLK), 2 * FBLK)
        part = train[:, pl.ds(start, 2 * FBLK)]
        gram = lax.dot_general(part, part, (((0,), (0,)), ((), ())), preferred_element_type=jnp.float32)
        body, tail = pack(gram[:FBLK, :FBLK], gram[FBLK:, FBLK:], spare)
        slab[pl.ds(0, FBLK), :] = body
        slab[pl.ds(FBLK, 8), :] = tail


def thirds(value):
    high = value.astype(jnp.bfloat16)
    rest = value - high.astype(jnp.float32)
    middle = rest.astype(jnp.bfloat16)
    return high, middle, (rest - middle.astype(jnp.float32)).astype(jnp.bfloat16)


def at_rows(panel, first):
    pair = 2 * PANEL
    blank = jnp.zeros((PANEL, FBLK), jnp.float32)
    panel = panel.astype(jnp.float32)
    piece = jnp.concatenate([panel, blank] if first % pair == 0 else [blank, panel], axis=0).astype(jnp.bfloat16)
    before = first // pair * pair
    pieces = [jnp.zeros((before, FBLK), jnp.bfloat16), piece, jnp.zeros((FBLK - before - pair, FBLK), jnp.bfloat16)]
    return jnp.concatenate([piece for piece in pieces if piece.shape[0]], axis=0)


def product(left, right, first):
    high, middle, low = thirds(left)
    right_high, right_middle, right_low = (at_rows(part, first) for part in thirds(right))
    both = jnp.concatenate([right_high, right_middle], axis=1)
    large = jnp.dot(
        jnp.concatenate([high, middle], axis=1), jnp.concatenate([both, both], axis=0),
        preferred_element_type=jnp.float32,
    )
    small = jnp.dot(
        jnp.concatenate([high, low], axis=1), jnp.concatenate([right_low, right_high], axis=0),
        preferred_element_type=jnp.float32,
    )
    return large[:, :FBLK] + (large[:, FBLK:] + small)


def eliminated(panel, first):
    lane = lax.broadcasted_iota(jnp.int32, (PANEL, FBLK), 1)
    sublane = lax.broadcasted_iota(jnp.int32, (PANEL, FBLK), 0)
    within = (lane >= first) & (lane < first + PANEL)
    count = range(PANEL)

    def across(value, row):
        return jnp.broadcast_to(value[row:row + 1, :], (PANEL, FBLK))

    columns = [jnp.broadcast_to(panel[:, first + j:first + j + 1], (PANEL, FBLK)) for j in count]
    pivots = [[across(columns[j], i) if j >= i else None for j in count] for i in count]
    rest = jnp.where(within, jnp.where(lane == first + sublane, 1.0, 0.0), panel)
    lines = [across(rest, i) for i in count]
    for i in count:
        scale = 1.0 / pivots[i][i]
        scaled = lines[i] * scale
        shares = [pivots[i][j] * scale if j > i else None for j in count]
        for m in range(i + 1, PANEL):
            lines[m] = lines[m] - pivots[i][m] * scaled
            for j in range(m, PANEL):
                pivots[m][j] = pivots[m][j] - shares[m] * pivots[i][j]
        lines[i] = scaled
        pivots[i] = shares
    for i in reversed(count):
        for m in range(i):
            lines[m] = lines[m] - pivots[m][i] * lines[i]
    result = lines[0]
    for i in range(1, PANEL):
        result = jnp.where(sublane == i, lines[i], result)
    return result


def inverted(blocks):
    lane = square(1)
    for first in range(0, FBLK, PANEL):
        within = (lane >= first) & (lane < first + PANEL)
        panels = [eliminated(block[first:first + PANEL, :], first) for block in blocks]
        updates = [product(block, panel, first) for block, panel in zip(blocks, panels)]
        rests = [jnp.where(within, 0.0, block) - update for block, update in zip(blocks, updates)]
        blocks = [
            jnp.concatenate(
                [part for part in (rest[:first], panel, rest[first + PANEL:]) if part.shape[0]], axis=0
            )
            for rest, panel in zip(rests, panels)
        ]
    return blocks


def factor_kernel(examples, scale, *refs):
    slabs, out = refs[:-2], refs[-1]
    body = slabs[0][pl.ds(0, FBLK), :]
    diagonal = slabs[0][pl.ds(FBLK, 1), :]
    for slab in slabs[1:]:
        body = body + slab[pl.ds(0, FBLK), :]
        diagonal = diagonal + slab[pl.ds(FBLK, 1), :]
    same = square(0) == square(1)
    damped = []
    for gram in unpack(body, diagonal):
        fisher = gram / examples
        trace = jnp.sum(jnp.sum(jnp.where(same, fisher, 0.0), axis=0, keepdims=True), axis=1, keepdims=True)
        damped.append(fisher + jnp.where(same, damping * (trace / FBLK), 0.0))
    first, second = inverted(damped)
    body, tail = pack(first * scale, second * scale)
    out[pl.ds(0, FBLK), :] = body
    out[pl.ds(FBLK, 8), :] = tail


def first_kernel(id_rows_hbm, delta_hbm, table_hbm, factor_hbm, lengths_hbm, train_hbm, sent, own, *refs):
    slabs, refs = refs[:-10], refs[-10:]
    id_rows, places, reads, delta, table, factor, lengths, train, looked, sems = refs
    model = lax.axis_index("mp")
    proj, vocab_rows = table.shape
    tokens = delta.shape[0]
    each = proj // lax.axis_size("mp")
    groups = tokens // FBLK
    get_ids, get_factor, get_lengths, get_train = (
        pltpu.make_async_copy(source, target, sems.at[0, index])
        for index, (source, target) in enumerate((
            (id_rows_hbm, id_rows), (factor_hbm, factor), (lengths_hbm, lengths), (train_hbm, train),
        ))
    )
    get_table = [
        pltpu.make_async_copy(table_hbm.at[rows], table.at[rows], sems.at[1, index])
        for index in range(proj // ROWS) for rows in (pl.ds(index * ROWS, ROWS),)
    ]

    def get_delta(g):
        rows = pl.ds(pl.multiple_of(g * FBLK, FBLK), FBLK)
        return pltpu.make_async_copy(delta_hbm.at[rows], delta.at[rows], sems.at[2, g])

    for copy in (get_ids, get_lengths, get_train, *get_table, get_factor, *(get_delta(g) for g in range(groups))):
        copy.start()
    get_ids.wait()
    local = id_rows[...] - model * vocab_rows
    owned = (local >= 0) & (local < vocab_rows)
    local = jnp.where(owned, local, 0)
    low = FBLK - 1
    roll = (lax.broadcasted_iota(jnp.int32, local.shape, 1) - local) & low
    places[...] = (local & ~low) | roll
    fetch = pltpu.make_async_copy(places, reads, sems.at[0, 4])
    fetch.start()
    get_lengths.wait()
    get_train.wait()
    grams(lengths, train, slabs)
    fetch.wait()
    places[...] = owned.astype(jnp.int32)
    for copy in get_table:
        copy.wait()
    get_factor.wait()
    lanes = lax.broadcasted_iota(jnp.int32, (ROWS, FBLK), 1)

    def group(g, carry):
        columns = pl.ds(pl.multiple_of(g * FBLK, FBLK), FBLK)
        get_delta(g).wait()
        output = lax.dot_general(
            delta[columns, :], factor[...], (((1,), (1,)), ((), ())), preferred_element_type=jnp.float32
        )
        looked[:, columns] = output.T
        gathered = [jnp.zeros((ROWS, FBLK), jnp.bfloat16) for _ in range(proj // ROWS)]
        for j in range(FBLK):
            place = reads[g, j]
            start, by, here = pl.multiple_of(place & ~low, FBLK), place & low, lanes == j
            for index in range(proj // ROWS):
                block = table[pl.ds(index * ROWS, ROWS), pl.ds(start, FBLK)]
                gathered[index] = jnp.where(here, pltpu.roll(block, by, 1), gathered[index])
        held = places[pl.ds(g, 1), :].astype(jnp.float32)
        for index, value in enumerate(gathered):
            value = (value.astype(jnp.float32) * held).astype(jnp.bfloat16)
            rows = pl.ds(2 * each + index * ROWS, ROWS)
            sent[rows, columns] = value
            own[rows, columns] = value
        return carry

    lax.fori_loop(0, groups, group, 0)
    mine = looked[pl.ds(pl.multiple_of(model * each, each), each), :]
    other = looked[pl.ds(pl.multiple_of((1 - model) * each, each), each), :]
    for target, value in ((own, mine), (sent, other)):
        high, rest = halves(value)
        target[pl.ds(0, each), :] = high
        target[pl.ds(each, each), :] = rest


def merge_kernel(each, own, got, out):
    def value(ref):
        return ref[pl.ds(0, each), :].astype(jnp.float32) + ref[pl.ds(each, each), :].astype(jnp.float32)

    high, low = halves(value(own) + value(got))
    out[pl.ds(0, each), :] = high
    out[pl.ds(each, each), :] = low
    rows = pl.ds(2 * each, out.shape[0] - 2 * each)
    out[rows, :] = own[rows, :] + got[rows, :]


def queries_kernel(each, source_of, choose, count, *refs):
    factor_refs, slabs, (high_out, low_out) = refs[:count], refs[count:count + 4], refs[-2:]
    mine = lax.axis_index("dp")
    tokens = factor_refs[0].shape[1]
    proj = factor_refs[0].shape[0] - 2 * each
    queries = high_out.shape[1]

    def part(rows):
        value = factor_refs[0][rows, :].astype(jnp.float32)
        if count == 2:
            value = jnp.where(choose(mine), factor_refs[1][rows, :].astype(jnp.float32), value)
        return value

    shift = lax.rem(mine + len(slabs) - source_of(mine), len(slabs))
    lengths = slabs[0][pl.ds(FBLK + 1, 1), :]
    for index in range(1, len(slabs)):
        lengths = jnp.where(shift == index, slabs[index][pl.ds(FBLK + 1, 1), :], lengths)
    upto = jnp.where(square(0) <= square(1), 1.0, 0.0).astype(jnp.bfloat16)
    ends = lax.dot_general(
        jnp.broadcast_to(lengths, (8, queries)).astype(jnp.bfloat16), upto, (((1,), (0,)), ((), ())),
        preferred_element_type=jnp.float32,
    )[:1]
    starts = ends - lengths
    place = lax.broadcasted_iota(jnp.int32, (tokens, queries), 0).astype(jnp.float32)
    inside = jnp.where((place >= starts) & (place < ends), 1.0, 0.0).astype(jnp.bfloat16)
    output = part(pl.ds(0, each)) + part(pl.ds(each, each))
    inputs = part(pl.ds(2 * each, proj))
    step = 8
    for start in range(0, each, step):
        grads = jnp.concatenate(
            [(inputs * output[r:r + 1, :]).astype(jnp.bfloat16) for r in range(start, start + step)], axis=0
        )
        summed = jnp.dot(grads, inside, preferred_element_type=jnp.float32)
        high, low = halves(summed)
        high_out[pl.ds(start * proj, step * proj), :] = high
        low_out[pl.ds(start * proj, step * proj), :] = low


def scores_kernel(cycle, count, *refs):
    own, peers = refs[:cycle], refs[cycle:2 * cycle]
    highs, lows = refs[2 * cycle:2 * cycle + count], refs[2 * cycle + count:2 * cycle + 2 * count]
    train, sent, kept, pre = refs[2 * cycle + 2 * count:]
    mine, rep, model = lax.axis_index("dp"), lax.axis_index("rep"), lax.axis_index("mp")
    for half, slabs in ((rep, own), (1 - rep, peers)):
        for shift in range(cycle):
            owner = half * cycle + lax.rem(mine + cycle - shift, cycle)
            slab = slabs[shift]
            blocks = unpack(slab[pl.ds(0, FBLK), :], slab[pl.ds(FBLK, 1), :])
            for index, block in enumerate(blocks):
                rows = pl.ds(pl.multiple_of(owner * (2 * FBLK) + index * FBLK, FBLK), FBLK)
                high, low = halves(block)
                right_high = jnp.concatenate([ref[rows, :] for ref in highs], axis=1)
                right_low = jnp.concatenate([ref[rows, :] for ref in lows], axis=1)
                solved = jnp.dot(
                    jnp.concatenate([high, high, low], axis=1),
                    jnp.concatenate([right_high, right_low, right_high], axis=0),
                    preferred_element_type=jnp.float32,
                )
                pre[rows, :] = solved.astype(jnp.bfloat16)
    half_rows = sent.shape[0]
    for out, which in ((sent, 1 - model), (kept, model)):
        rows = pl.ds(pl.multiple_of(which * half_rows, half_rows), half_rows)
        out[...] = jnp.dot(train[rows, :], pre[...], preferred_element_type=jnp.float32).astype(jnp.bfloat16)


def total_kernel(sources, *refs):
    pieces, out = refs[:-1], refs[-1]
    mine = lax.axis_index("dp")
    sums = []
    for kept, got in zip(pieces[::2], pieces[1::2]):
        both = kept[...].astype(jnp.float32) + got[...].astype(jnp.float32)
        sums += [both[:, start:start + FBLK] for start in range(0, both.shape[1], FBLK)]
    placed = []
    for source in range(len(sums)):
        value = sums[0]
        for index in range(1, len(sums)):
            value = jnp.where(sources[index](mine) == source, sums[index], value)
        placed.append(value)
    out[...] = jnp.stack(placed, axis=1).astype(jnp.bfloat16)


def shape(dims, dtype):
    return jax.ShapeDtypeStruct(dims, dtype)


def split_over_blocks(query_ids, query_delta, doc_lengths, vocab_factor, output_factor, train_grads):
    cycle = lax.axis_size("dp")
    tokens, width = query_delta.shape
    proj = output_factor.shape[1]
    each = proj // lax.axis_size("mp")
    vocab_rows = vocab_factor.shape[0]
    train_rows, feat = train_grads.shape
    queries = doc_lengths.shape[1]
    bf16, f32 = jnp.bfloat16, jnp.float32

    sent, own, *slabs = call(
        first_kernel,
        [shape((2 * each + proj, tokens), bf16)] * 2 + [shape((SLAB, FBLK), f32)] * cycle,
        [HBM] * 6,
        [
            pltpu.VMEM((tokens // FBLK, FBLK), jnp.int32),
            pltpu.VMEM((tokens // FBLK, FBLK), jnp.int32),
            pltpu.SMEM((tokens // FBLK, FBLK), jnp.int32),
            pltpu.VMEM((tokens, width), bf16),
            pltpu.VMEM((proj, vocab_rows), bf16),
            pltpu.VMEM((proj, width), bf16),
            pltpu.VMEM((1, queries), jnp.int32),
            pltpu.VMEM((train_rows, feat), bf16),
            pltpu.VMEM((proj, tokens), f32),
            pltpu.SemaphoreType.DMA((3, 8)),
        ],
        vmem=62,
        flops=2 * tokens * width * proj,
        moved=2 * (tokens * width + proj * vocab_rows) * 2,
    )(
        query_ids.reshape(tokens // FBLK, FBLK), query_delta, vocab_factor.T, output_factor.T,
        doc_lengths, train_grads,
    )
    got = passed_along(sent, "mp", 1)
    parts = [slabs[0]] + [passed_along(slabs[s], "dp", s) for s in range(1, cycle)]

    factors = call(
        functools.partial(merge_kernel, each),
        shape(sent.shape, bf16),
        [VMEM, VMEM],
        vmem=16,
        flops=tokens * each,
        moved=8 * tokens * each * 4,
    )(own, got)
    last = cycle - 1
    from_two = passed_along(factors, "dp", 2)
    from_below = lax.ppermute(factors, "dp", [(i, i + 1) for i in range(last)])
    from_above = lax.ppermute(factors, "dp", [(i + 1, i) for i in range(last)])
    from_far = lax.ppermute(from_two, "dp", [(1, 0), (last - 1, last)])
    sources = (
        (lambda d: d, None, (factors,)),
        (lambda d: jnp.where(d == 0, 1, d - 1), lambda d: d == 0, (from_below, from_above)),
        (lambda d: lax.rem(d + 2, cycle), None, (from_two,)),
        (lambda d: jnp.where(d == 0, last, jnp.where(d == last, 0, d + 1)), lambda d: (d == 0) | (d == last),
         (from_above, from_far)),
    )

    inverse = call(
        functools.partial(factor_kernel, train_rows * cycle, 1.0 / proj),
        shape((SLAB, FBLK), f32),
        [VMEM] * cycle + [HBM],
        vmem=16,
        flops=10 ** 10,
        moved=10 ** 6,
    )(*parts, factors)
    inverses = [inverse] + [passed_along(inverse, "dp", s) for s in range(1, cycle)]
    peers = [passed_along(slab, "rep", 1) for slab in inverses]

    highs, lows = [], []
    for index, (source_of, choose, arrays) in enumerate(sources):
        before = [inverse] if index == 0 else []
        high, low = call(
            functools.partial(queries_kernel, each, source_of, choose, len(arrays)),
            [shape((feat, queries), bf16)] * 2,
            [VMEM] * (len(arrays) + cycle) + [HBM] * len(before),
            vmem=24,
            flops=2 * feat * tokens * queries,
            moved=6 * feat * queries,
        )(*arrays, *parts, *before)
        highs.append(high)
        lows.append(low)

    half_rows = train_rows // lax.axis_size("mp")
    pieces = []
    for chosen in (slice(0, last), slice(last, cycle)):
        count = len(highs[chosen])
        outgoing, kept = call(
            functools.partial(scores_kernel, cycle, count),
            [shape((half_rows, count * queries), bf16)] * 2,
            [VMEM] * (2 * cycle + 2 * count + 1),
            [pltpu.VMEM((feat, count * queries), bf16)],
            vmem=24,
            flops=2 * train_rows * feat * count * queries,
            moved=8 * feat * queries * count,
        )(*inverses, *peers, *highs[chosen], *lows[chosen], train_grads)
        pieces += [kept, passed_along(outgoing, "mp", 1)]
    total = call(
        functools.partial(total_kernel, [source_of for source_of, _, _ in sources]),
        shape((half_rows, cycle, queries), bf16),
        [VMEM] * len(pieces),
        vmem=16,
        flops=half_rows * cycle * queries,
        moved=6 * half_rows * cycle * queries,
    )(*pieces)
    return total[:, :, None, :]


def doc_matrix(lengths_row, count):
    ends = jnp.cumsum(lengths_row)
    starts = ends - lengths_row
    place = jnp.arange(count, dtype=jnp.int32)
    inside = (place[None, :] >= starts[:, None]) & (place[None, :] < ends[:, None])
    return inside.astype(jnp.bfloat16)


def solve_block(factor, rhs):
    return jax.scipy.linalg.cho_solve((factor, True), rhs)


def general(query_ids, query_delta, doc_lengths, vocab_factor, output_factor, train_grads):
    model_count = lax.axis_size("mp")
    model_index = lax.axis_index("mp")
    vocab_rows = vocab_factor.shape[0]
    local_ids = query_ids - model_index * vocab_rows
    owned = (local_ids >= 0) & (local_ids < vocab_rows)
    looked = vocab_factor[jnp.clip(local_ids, 0, vocab_rows - 1)].astype(jnp.float32)
    vocab_part = jnp.where(owned[:, None], looked, jnp.zeros_like(looked))
    output_part = jnp.dot(query_delta, output_factor, preferred_element_type=jnp.float32)
    input_side, output_side = lax.psum((vocab_part, output_part), "mp")
    proj = output_side.shape[1]
    rows_each = proj // model_count
    mine = lax.dynamic_slice_in_dim(output_side, model_index * rows_each, rows_each, 1)
    token_count = query_ids.shape[0]
    token_grads = (
        (mine[:, :, None] * input_side[:, None, :])
        .reshape(token_count, rows_each * proj)
        .astype(jnp.bfloat16)
    )
    query_grads = jnp.dot(
        doc_matrix(doc_lengths[0], token_count), token_grads, preferred_element_type=jnp.float32
    )
    train_rows, feat_dev = train_grads.shape
    nblocks = feat_dev // FBLK
    tiled = train_grads.reshape(train_rows, nblocks, FBLK)
    local_gram = jnp.einsum("tbi,tbj->bij", tiled, tiled, preferred_element_type=jnp.float32)
    total_gram = lax.psum(local_gram, "dp")
    fisher = total_gram / (train_rows * lax.axis_size("dp"))
    shift_amount = damping * (jnp.trace(fisher, axis1=1, axis2=2) / FBLK)
    damped = fisher + shift_amount[:, None, None] * jnp.eye(FBLK, dtype=jnp.float32)[None]
    factor = jnp.linalg.cholesky(damped)
    queries = query_grads.shape[0]
    rhs = jnp.transpose(query_grads.reshape(queries, nblocks, FBLK), (1, 2, 0))
    solved = jax.vmap(solve_block)(factor, rhs)
    pre = (jnp.transpose(solved, (2, 0, 1)).reshape(queries, feat_dev) / proj).astype(jnp.bfloat16)
    cycle = lax.axis_size("dp")
    everyone = lax.all_gather(pre, "dp", axis=0, tiled=True)
    scores = lax.dot_general(
        train_grads, everyone, (((1,), (1,)), ((), ())), preferred_element_type=jnp.float32
    )
    scores = scores.astype(jnp.bfloat16).reshape(train_rows, cycle, queries)
    summed = lax.psum_scatter(scores, "mp", scatter_dimension=0, tiled=True)
    return summed[:, :, None, :]


def per_device(query_ids, query_delta, doc_lengths, vocab_factor, output_factor, train_grads):
    owners = lax.axis_size("dp") * lax.axis_size("rep")
    fits = (
        train_grads.shape[1] == 2 * FBLK * owners
        and lax.axis_size("dp") == 4
        and lax.axis_size("mp") == 2
        and lax.axis_size("rep") == 2
        and doc_lengths.shape[1] == FBLK
        and vocab_factor.shape[0] % FBLK == 0
    )
    body = split_over_blocks if fits else general
    return body(query_ids, query_delta, doc_lengths, vocab_factor, output_factor, train_grads)


def solution(mesh):
    placed = (
        P(("groups", "dp", "rep")),
        P(("groups", "dp", "rep"), "mp"),
        P(("groups", "dp", "rep"), None),
        P("mp", None),
        P("mp", None),
        P(("groups", "dp"), "mp"),
    )
    return jax.shard_map(
        per_device,
        mesh=mesh,
        in_specs=placed,
        out_specs=P(("groups", "dp", "mp"), None, "rep", None),
        check_vma=False,
    )
```

```python
import functools
import jax
import jax.numpy as jnp
from jax import lax
from jax.experimental import pallas as pl
from jax.experimental.pallas import tpu as pltpu
from jax.sharding import PartitionSpec as P

FBLK = 128
SLAB = FBLK + 8
PANEL = 8
ROWS = 16

damping = 0.1

VMEM = pl.BlockSpec(memory_space=pltpu.VMEM)
SMEM = pl.BlockSpec(memory_space=pltpu.SMEM)
HBM = pl.BlockSpec(memory_space=pl.ANY)


def call(kernel, outs, in_specs, scratch=(), vmem=48, flops=0, moved=0):
    return pl.pallas_call(
        kernel,
        out_shape=outs,
        in_specs=in_specs,
        scratch_shapes=list(scratch),
        compiler_params=pltpu.CompilerParams(vmem_limit_bytes=vmem << 20),
        cost_estimate=pl.CostEstimate(flops=flops, bytes_accessed=moved, transcendentals=0),
    )


def passed_along(shard, axis, by):
    size = lax.axis_size(axis)
    return lax.ppermute(shard, axis, [(i, (i + by) % size) for i in range(size)])


def square(dim):
    return lax.broadcasted_iota(jnp.int32, (FBLK, FBLK), dim)


def halves(value):
    high = value.astype(jnp.bfloat16)
    return high, (value - high.astype(jnp.float32)).astype(jnp.bfloat16)


def pack(first, second, spare=None):
    row, col = square(0), square(1)
    body = jnp.where(row >= col, first, second)
    diagonal = jnp.sum(jnp.where(row == col, second, 0.0), axis=0, keepdims=True)
    place = lax.broadcasted_iota(jnp.int32, (8, FBLK), 0)
    tail = jnp.where(place == 0, diagonal, 0.0)
    if spare is not None:
        tail = jnp.where(place == 1, spare, tail)
    return body, tail


def unpack(body, diagonal):
    row, col = square(0), square(1)
    turned = body.T
    first = jnp.where(row >= col, body, turned)
    second = jnp.where(row < col, body, jnp.where(row > col, turned, diagonal))
    return first, second


def gram_kernel(lengths_hbm, train_hbm, *refs):
    slabs, (lengths, train, sems) = refs[:-3], refs[-3:]
    cycle = len(slabs)
    mine, half = lax.axis_index("dp"), lax.axis_index("rep")
    width = 2 * FBLK

    def columns(shift):
        owner = half * cycle + lax.rem(mine + shift, cycle)
        return pl.ds(pl.multiple_of(owner * width, width), width)

    get_lengths = pltpu.make_async_copy(lengths_hbm, lengths, sems.at[cycle])
    get_train = [
        pltpu.make_async_copy(train_hbm.at[:, columns(shift)], train.at[shift], sems.at[shift]) for shift in range(cycle)
    ]
    for copy in (get_lengths, *get_train):
        copy.start()
    get_lengths.wait()
    spare = lengths[...].astype(jnp.float32)
    for shift, slab in enumerate(slabs):
        get_train[shift].wait()
        part = train[shift]
        gram = lax.dot_general(part, part, (((0,), (0,)), ((), ())), preferred_element_type=jnp.float32)
        body, tail = pack(gram[:FBLK, :FBLK], gram[FBLK:, FBLK:], spare)
        slab[pl.ds(0, FBLK), :] = body
        slab[pl.ds(FBLK, 8), :] = tail


def thirds(value):
    high = value.astype(jnp.bfloat16)
    rest = value - high.astype(jnp.float32)
    middle = rest.astype(jnp.bfloat16)
    return high, middle, (rest - middle.astype(jnp.float32)).astype(jnp.bfloat16)


def at_rows(panel, first):
    pair = 2 * PANEL
    blank = jnp.zeros((PANEL, FBLK), jnp.float32)
    panel = panel.astype(jnp.float32)
    piece = jnp.concatenate([panel, blank] if first % pair == 0 else [blank, panel], axis=0).astype(jnp.bfloat16)
    before = first // pair * pair
    pieces = [jnp.zeros((before, FBLK), jnp.bfloat16), piece, jnp.zeros((FBLK - before - pair, FBLK), jnp.bfloat16)]
    return jnp.concatenate([piece for piece in pieces if piece.shape[0]], axis=0)


def product(left, right, first):
    high, middle, low = thirds(left)
    right_high, right_middle, right_low = (at_rows(part, first) for part in thirds(right))
    both = jnp.concatenate([right_high, right_middle], axis=1)
    large = jnp.dot(
        jnp.concatenate([high, middle], axis=1), jnp.concatenate([both, both], axis=0),
        preferred_element_type=jnp.float32,
    )
    small = jnp.dot(
        jnp.concatenate([high, low], axis=1), jnp.concatenate([right_low, right_high], axis=0),
        preferred_element_type=jnp.float32,
    )
    return large[:, :FBLK] + (large[:, FBLK:] + small)


def eliminated(panel, first):
    lane = lax.broadcasted_iota(jnp.int32, (PANEL, FBLK), 1)
    sublane = lax.broadcasted_iota(jnp.int32, (PANEL, FBLK), 0)
    within = (lane >= first) & (lane < first + PANEL)
    count = range(PANEL)

    def across(value, row):
        return jnp.broadcast_to(value[row:row + 1, :], (PANEL, FBLK))

    columns = [jnp.broadcast_to(panel[:, first + j:first + j + 1], (PANEL, FBLK)) for j in count]
    pivots = [[across(columns[j], i) if j >= i else None for j in count] for i in count]
    rest = jnp.where(within, jnp.where(lane == first + sublane, 1.0, 0.0), panel)
    lines = [across(rest, i) for i in count]
    for i in count:
        scale = 1.0 / pivots[i][i]
        scaled = lines[i] * scale
        shares = [pivots[i][j] * scale if j > i else None for j in count]
        for m in range(i + 1, PANEL):
            lines[m] = lines[m] - pivots[i][m] * scaled
            for j in range(m, PANEL):
                pivots[m][j] = pivots[m][j] - shares[m] * pivots[i][j]
        lines[i] = scaled
        pivots[i] = shares
    for i in reversed(count):
        for m in range(i):
            lines[m] = lines[m] - pivots[m][i] * lines[i]
    result = lines[0]
    for i in range(1, PANEL):
        result = jnp.where(sublane == i, lines[i], result)
    return result


def inverted(blocks):
    lane = square(1)
    for first in range(0, FBLK, PANEL):
        within = (lane >= first) & (lane < first + PANEL)
        panels = [eliminated(block[first:first + PANEL, :], first) for block in blocks]
        updates = [product(block, panel, first) for block, panel in zip(blocks, panels)]
        rests = [jnp.where(within, 0.0, block) - update for block, update in zip(blocks, updates)]
        blocks = [
            jnp.concatenate(
                [part for part in (rest[:first], panel, rest[first + PANEL:]) if part.shape[0]], axis=0
            )
            for rest, panel in zip(rests, panels)
        ]
    return blocks


def factor_kernel(examples, scale, *refs):
    slabs, out = refs[:-1], refs[-1]
    body = slabs[0][pl.ds(0, FBLK), :]
    diagonal = slabs[0][pl.ds(FBLK, 1), :]
    for slab in slabs[1:]:
        body = body + slab[pl.ds(0, FBLK), :]
        diagonal = diagonal + slab[pl.ds(FBLK, 1), :]
    same = square(0) == square(1)
    damped = []
    for gram in unpack(body, diagonal):
        fisher = gram / examples
        trace = jnp.sum(jnp.sum(jnp.where(same, fisher, 0.0), axis=0, keepdims=True), axis=1, keepdims=True)
        damped.append(fisher + jnp.where(same, damping * (trace / FBLK), 0.0))
    first, second = inverted(damped)
    body, tail = pack(first * scale, second * scale)
    out[pl.ds(0, FBLK), :] = body
    out[pl.ds(FBLK, 8), :] = tail


def tokens_kernel(id_rows_hbm, delta_hbm, table_hbm, factor_hbm, after, sent, own, *refs):
    id_rows, places, reads, delta, table, factor, looked, sems = refs
    model = lax.axis_index("mp")
    proj, vocab_rows = table.shape
    tokens = delta.shape[0]
    each = proj // lax.axis_size("mp")
    groups = tokens // FBLK
    get_ids = pltpu.make_async_copy(id_rows_hbm, id_rows, sems.at[0, 0])
    get_factor = pltpu.make_async_copy(factor_hbm, factor, sems.at[0, 1])
    get_table = [
        pltpu.make_async_copy(table_hbm.at[rows], table.at[rows], sems.at[1, index])
        for index in range(proj // ROWS) for rows in (pl.ds(index * ROWS, ROWS),)
    ]

    def get_delta(g):
        rows = pl.ds(pl.multiple_of(g * FBLK, FBLK), FBLK)
        return pltpu.make_async_copy(delta_hbm.at[rows], delta.at[rows], sems.at[2, g])

    for copy in (get_ids, *get_table, get_factor, *(get_delta(g) for g in range(groups))):
        copy.start()
    get_ids.wait()
    local = id_rows[...] - model * vocab_rows
    owned = (local >= 0) & (local < vocab_rows)
    local = jnp.where(owned, local, 0)
    low = FBLK - 1
    roll = (lax.broadcasted_iota(jnp.int32, local.shape, 1) - local) & low
    places[...] = (local & ~low) | roll
    fetch = pltpu.make_async_copy(places, reads, sems.at[0, 2])
    fetch.start()
    fetch.wait()
    places[...] = owned.astype(jnp.int32)
    for copy in get_table:
        copy.wait()
    get_factor.wait()
    lanes = lax.broadcasted_iota(jnp.int32, (ROWS, FBLK), 1)

    def group(g, carry):
        columns = pl.ds(pl.multiple_of(g * FBLK, FBLK), FBLK)
        get_delta(g).wait()
        output = lax.dot_general(
            delta[columns, :], factor[...], (((1,), (1,)), ((), ())), preferred_element_type=jnp.float32
        )
        looked[:, columns] = output.T
        gathered = [jnp.zeros((ROWS, FBLK), jnp.bfloat16) for _ in range(proj // ROWS)]
        for j in range(FBLK):
            place = reads[g, j]
            start, by, here = pl.multiple_of(place & ~low, FBLK), place & low, lanes == j
            for index in range(proj // ROWS):
                block = table[pl.ds(index * ROWS, ROWS), pl.ds(start, FBLK)]
                gathered[index] = jnp.where(here, pltpu.roll(block, by, 1), gathered[index])
        held = places[pl.ds(g, 1), :].astype(jnp.float32)
        for index, value in enumerate(gathered):
            value = (value.astype(jnp.float32) * held).astype(jnp.bfloat16)
            rows = pl.ds(2 * each + index * ROWS, ROWS)
            sent[rows, columns] = value
            own[rows, columns] = value
        return carry

    lax.fori_loop(0, groups, group, 0)
    mine = looked[pl.ds(pl.multiple_of(model * each, each), each), :]
    other = looked[pl.ds(pl.multiple_of((1 - model) * each, each), each), :]
    for target, value in ((own, mine), (sent, other)):
        high, rest = halves(value)
        target[pl.ds(0, each), :] = high
        target[pl.ds(each, each), :] = rest


def merge_kernel(each, own, got, after, out):
    def value(ref):
        return ref[pl.ds(0, each), :].astype(jnp.float32) + ref[pl.ds(each, each), :].astype(jnp.float32)

    high, low = halves(value(own) + value(got))
    out[pl.ds(0, each), :] = high
    out[pl.ds(each, each), :] = low
    rows = pl.ds(2 * each, out.shape[0] - 2 * each)
    out[rows, :] = own[rows, :] + got[rows, :]


def queries_kernel(each, source_of, choose, count, *refs):
    factor_refs, slabs, (high_out, low_out) = refs[:count], refs[count:-2], refs[-2:]
    mine = lax.axis_index("dp")
    tokens = factor_refs[0].shape[1]
    proj = factor_refs[0].shape[0] - 2 * each
    queries = high_out.shape[1]

    def part(rows):
        value = factor_refs[0][rows, :].astype(jnp.float32)
        if count == 2:
            value = jnp.where(choose(mine), factor_refs[1][rows, :].astype(jnp.float32), value)
        return value

    shift = lax.rem(mine + len(slabs) - source_of(mine), len(slabs))
    lengths = slabs[0][pl.ds(FBLK + 1, 1), :]
    for index in range(1, len(slabs)):
        lengths = jnp.where(shift == index, slabs[index][pl.ds(FBLK + 1, 1), :], lengths)
    upto = jnp.where(square(0) <= square(1), 1.0, 0.0).astype(jnp.bfloat16)
    ends = lax.dot_general(
        jnp.broadcast_to(lengths, (8, queries)).astype(jnp.bfloat16), upto, (((1,), (0,)), ((), ())),
        preferred_element_type=jnp.float32,
    )[:1]
    starts = ends - lengths
    place = lax.broadcasted_iota(jnp.int32, (tokens, queries), 0).astype(jnp.float32)
    inside = jnp.where((place >= starts) & (place < ends), 1.0, 0.0).astype(jnp.bfloat16)
    output = part(pl.ds(0, each)) + part(pl.ds(each, each))
    inputs = part(pl.ds(2 * each, proj))
    step = 8
    for start in range(0, each, step):
        grads = jnp.concatenate(
            [(inputs * output[r:r + 1, :]).astype(jnp.bfloat16) for r in range(start, start + step)], axis=0
        )
        summed = jnp.dot(grads, inside, preferred_element_type=jnp.float32)
        high, low = halves(summed)
        high_out[pl.ds(start * proj, step * proj), :] = high
        low_out[pl.ds(start * proj, step * proj), :] = low


def scores_kernel(cycle, count, *refs):
    own, peers = refs[:cycle], refs[cycle:2 * cycle]
    highs, lows = refs[2 * cycle:2 * cycle + count], refs[2 * cycle + count:2 * cycle + 2 * count]
    train, sent, kept, pre = refs[2 * cycle + 2 * count:]
    mine, rep, model = lax.axis_index("dp"), lax.axis_index("rep"), lax.axis_index("mp")
    for half, slabs in ((rep, own), (1 - rep, peers)):
        for shift in range(cycle):
            owner = half * cycle + lax.rem(mine + cycle - shift, cycle)
            slab = slabs[shift]
            blocks = unpack(slab[pl.ds(0, FBLK), :], slab[pl.ds(FBLK, 1), :])
            for index, block in enumerate(blocks):
                rows = pl.ds(pl.multiple_of(owner * (2 * FBLK) + index * FBLK, FBLK), FBLK)
                high, low = halves(block)
                right_high = jnp.concatenate([ref[rows, :] for ref in highs], axis=1)
                right_low = jnp.concatenate([ref[rows, :] for ref in lows], axis=1)
                solved = jnp.dot(
                    jnp.concatenate([high, high, low], axis=1),
                    jnp.concatenate([right_high, right_low, right_high], axis=0),
                    preferred_element_type=jnp.float32,
                )
                pre[rows, :] = solved.astype(jnp.bfloat16)
    half_rows = sent.shape[0]
    for out, which in ((sent, 1 - model), (kept, model)):
        rows = pl.ds(pl.multiple_of(which * half_rows, half_rows), half_rows)
        out[...] = jnp.dot(train[rows, :], pre[...], preferred_element_type=jnp.float32).astype(jnp.bfloat16)


def total_kernel(sources, *refs):
    pieces, out = refs[:-1], refs[-1]
    mine = lax.axis_index("dp")
    sums = []
    for kept, got in zip(pieces[::2], pieces[1::2]):
        both = kept[...].astype(jnp.float32) + got[...].astype(jnp.float32)
        sums += [both[:, start:start + FBLK] for start in range(0, both.shape[1], FBLK)]
    placed = []
    for source in range(len(sums)):
        value = sums[0]
        for index in range(1, len(sums)):
            value = jnp.where(sources[index](mine) == source, sums[index], value)
        placed.append(value)
    out[...] = jnp.stack(placed, axis=1).astype(jnp.bfloat16)


def shape(dims, dtype):
    return jax.ShapeDtypeStruct(dims, dtype)


def split_over_blocks(query_ids, query_delta, doc_lengths, vocab_factor, output_factor, train_grads):
    cycle = lax.axis_size("dp")
    tokens, width = query_delta.shape
    proj = output_factor.shape[1]
    each = proj // lax.axis_size("mp")
    vocab_rows = vocab_factor.shape[0]
    train_rows, feat = train_grads.shape
    queries = doc_lengths.shape[1]
    bf16, f32 = jnp.bfloat16, jnp.float32

    slabs = call(
        gram_kernel,
        [shape((SLAB, FBLK), f32)] * cycle,
        [HBM] * 2,
        [
            pltpu.VMEM((1, queries), jnp.int32),
            pltpu.VMEM((cycle, train_rows, 2 * FBLK), bf16),
            pltpu.SemaphoreType.DMA((cycle + 1,)),
        ],
        vmem=62,
        flops=train_rows * feat * FBLK * 2,
        moved=train_rows * feat,
    )(doc_lengths, train_grads)
    parts = [slabs[0]] + [passed_along(slabs[s], "dp", s) for s in range(1, cycle)]

    sent, own = call(
        tokens_kernel,
        [shape((2 * each + proj, tokens), bf16)] * 2,
        [HBM] * 5,
        [
            pltpu.VMEM((tokens // FBLK, FBLK), jnp.int32),
            pltpu.VMEM((tokens // FBLK, FBLK), jnp.int32),
            pltpu.SMEM((tokens // FBLK, FBLK), jnp.int32),
            pltpu.VMEM((tokens, width), bf16),
            pltpu.VMEM((proj, vocab_rows), bf16),
            pltpu.VMEM((proj, width), bf16),
            pltpu.VMEM((proj, tokens), f32),
            pltpu.SemaphoreType.DMA((3, 8)),
        ],
        vmem=62,
        flops=2 * tokens * width * proj,
        moved=2 * (tokens * width + proj * vocab_rows) * 2,
    )(query_ids.reshape(tokens // FBLK, FBLK), query_delta, vocab_factor.T, output_factor.T, slabs[0])
    got = passed_along(sent, "mp", 1)

    inverse = call(
        functools.partial(factor_kernel, train_rows * cycle, 1.0 / proj),
        shape((SLAB, FBLK), f32),
        [VMEM] * cycle,
        vmem=16,
        flops=10 ** 10,
        moved=10 ** 6,
    )(*parts)
    inverses = [inverse] + [passed_along(inverse, "dp", s) for s in range(1, cycle)]
    peers = [passed_along(slab, "rep", 1) for slab in inverses]

    factors = call(
        functools.partial(merge_kernel, each),
        shape(sent.shape, bf16),
        [VMEM, VMEM, HBM],
        vmem=16,
        flops=tokens * each,
        moved=8 * tokens * each * 4,
    )(own, got, inverse)
    last = cycle - 1
    from_two = passed_along(factors, "dp", 2)
    from_below = lax.ppermute(factors, "dp", [(i, i + 1) for i in range(last)])
    from_above = lax.ppermute(factors, "dp", [(i + 1, i) for i in range(last)])
    from_far = lax.ppermute(from_two, "dp", [(1, 0), (last - 1, last)])
    sources = (
        (lambda d: d, None, (factors,)),
        (lambda d: jnp.where(d == 0, 1, d - 1), lambda d: d == 0, (from_below, from_above)),
        (lambda d: lax.rem(d + 2, cycle), None, (from_two,)),
        (lambda d: jnp.where(d == 0, last, jnp.where(d == last, 0, d + 1)), lambda d: (d == 0) | (d == last),
         (from_above, from_far)),
    )

    highs, lows = [], []
    for index, (source_of, choose, arrays) in enumerate(sources):
        high, low = call(
            functools.partial(queries_kernel, each, source_of, choose, len(arrays)),
            [shape((feat, queries), bf16)] * 2,
            [VMEM] * (len(arrays) + cycle),
            vmem=24,
            flops=2 * feat * tokens * queries,
            moved=6 * feat * queries,
        )(*arrays, *parts)
        highs.append(high)
        lows.append(low)

    half_rows = train_rows // lax.axis_size("mp")
    pieces = []
    for chosen in (slice(0, last), slice(last, cycle)):
        count = len(highs[chosen])
        outgoing, kept = call(
            functools.partial(scores_kernel, cycle, count),
            [shape((half_rows, count * queries), bf16)] * 2,
            [VMEM] * (2 * cycle + 2 * count + 1),
            [pltpu.VMEM((feat, count * queries), bf16)],
            vmem=24,
            flops=2 * train_rows * feat * count * queries,
            moved=8 * feat * queries * count,
        )(*inverses, *peers, *highs[chosen], *lows[chosen], train_grads)
        pieces += [kept, passed_along(outgoing, "mp", 1)]
    total = call(
        functools.partial(total_kernel, [source_of for source_of, _, _ in sources]),
        shape((half_rows, cycle, queries), bf16),
        [VMEM] * len(pieces),
        vmem=16,
        flops=half_rows * cycle * queries,
        moved=6 * half_rows * cycle * queries,
    )(*pieces)
    return total[:, :, None, :]


def doc_matrix(lengths_row, count):
    ends = jnp.cumsum(lengths_row)
    starts = ends - lengths_row
    place = jnp.arange(count, dtype=jnp.int32)
    inside = (place[None, :] >= starts[:, None]) & (place[None, :] < ends[:, None])
    return inside.astype(jnp.bfloat16)


def solve_block(factor, rhs):
    return jax.scipy.linalg.cho_solve((factor, True), rhs)


def general(query_ids, query_delta, doc_lengths, vocab_factor, output_factor, train_grads):
    model_count = lax.axis_size("mp")
    model_index = lax.axis_index("mp")
    vocab_rows = vocab_factor.shape[0]
    local_ids = query_ids - model_index * vocab_rows
    owned = (local_ids >= 0) & (local_ids < vocab_rows)
    looked = vocab_factor[jnp.clip(local_ids, 0, vocab_rows - 1)].astype(jnp.float32)
    vocab_part = jnp.where(owned[:, None], looked, jnp.zeros_like(looked))
    output_part = jnp.dot(query_delta, output_factor, preferred_element_type=jnp.float32)
    input_side, output_side = lax.psum((vocab_part, output_part), "mp")
    proj = output_side.shape[1]
    rows_each = proj // model_count
    mine = lax.dynamic_slice_in_dim(output_side, model_index * rows_each, rows_each, 1)
    token_count = query_ids.shape[0]
    token_grads = (
        (mine[:, :, None] * input_side[:, None, :])
        .reshape(token_count, rows_each * proj)
        .astype(jnp.bfloat16)
    )
    query_grads = jnp.dot(
        doc_matrix(doc_lengths[0], token_count), token_grads, preferred_element_type=jnp.float32
    )
    train_rows, feat_dev = train_grads.shape
    nblocks = feat_dev // FBLK
    tiled = train_grads.reshape(train_rows, nblocks, FBLK)
    local_gram = jnp.einsum("tbi,tbj->bij", tiled, tiled, preferred_element_type=jnp.float32)
    total_gram = lax.psum(local_gram, "dp")
    fisher = total_gram / (train_rows * lax.axis_size("dp"))
    shift_amount = damping * (jnp.trace(fisher, axis1=1, axis2=2) / FBLK)
    damped = fisher + shift_amount[:, None, None] * jnp.eye(FBLK, dtype=jnp.float32)[None]
    factor = jnp.linalg.cholesky(damped)
    queries = query_grads.shape[0]
    rhs = jnp.transpose(query_grads.reshape(queries, nblocks, FBLK), (1, 2, 0))
    solved = jax.vmap(solve_block)(factor, rhs)
    pre = (jnp.transpose(solved, (2, 0, 1)).reshape(queries, feat_dev) / proj).astype(jnp.bfloat16)
    cycle = lax.axis_size("dp")
    everyone = lax.all_gather(pre, "dp", axis=0, tiled=True)
    scores = lax.dot_general(
        train_grads, everyone, (((1,), (1,)), ((), ())), preferred_element_type=jnp.float32
    )
    scores = scores.astype(jnp.bfloat16).reshape(train_rows, cycle, queries)
    summed = lax.psum_scatter(scores, "mp", scatter_dimension=0, tiled=True)
    return summed[:, :, None, :]


def per_device(query_ids, query_delta, doc_lengths, vocab_factor, output_factor, train_grads):
    owners = lax.axis_size("dp") * lax.axis_size("rep")
    fits = (
        train_grads.shape[1] == 2 * FBLK * owners
        and lax.axis_size("dp") == 4
        and lax.axis_size("mp") == 2
        and lax.axis_size("rep") == 2
        and doc_lengths.shape[1] == FBLK
        and vocab_factor.shape[0] % FBLK == 0
    )
    body = split_over_blocks if fits else general
    return body(query_ids, query_delta, doc_lengths, vocab_factor, output_factor, train_grads)


def solution(mesh):
    placed = (
        P(("groups", "dp", "rep")),
        P(("groups", "dp", "rep"), "mp"),
        P(("groups", "dp", "rep"), None),
        P("mp", None),
        P("mp", None),
        P(("groups", "dp"), "mp"),
    )
    return jax.shard_map(
        per_device,
        mesh=mesh,
        in_specs=placed,
        out_specs=P(("groups", "dp", "mp"), None, "rep", None),
        check_vma=False,
    )
```

```python
import functools
import jax
import jax.numpy as jnp
from jax import lax
from jax.experimental import pallas as pl
from jax.experimental.pallas import tpu as pltpu
from jax.sharding import PartitionSpec as P

FBLK = 128
SLAB = FBLK + 8
PANEL = 8
ROWS = 16

damping = 0.1

VMEM = pl.BlockSpec(memory_space=pltpu.VMEM)
SMEM = pl.BlockSpec(memory_space=pltpu.SMEM)
HBM = pl.BlockSpec(memory_space=pl.ANY)


def call(kernel, outs, in_specs, scratch=(), vmem=48, flops=0, moved=0):
    return pl.pallas_call(
        kernel,
        out_shape=outs,
        in_specs=in_specs,
        scratch_shapes=list(scratch),
        compiler_params=pltpu.CompilerParams(vmem_limit_bytes=vmem << 20),
        cost_estimate=pl.CostEstimate(flops=flops, bytes_accessed=moved, transcendentals=0),
    )


def passed_along(shard, axis, by):
    size = lax.axis_size(axis)
    return lax.ppermute(shard, axis, [(i, (i + by) % size) for i in range(size)])


def square(dim):
    return lax.broadcasted_iota(jnp.int32, (FBLK, FBLK), dim)


def halves(value):
    high = value.astype(jnp.bfloat16)
    return high, (value - high.astype(jnp.float32)).astype(jnp.bfloat16)


def pack(first, second, spare=None):
    row, col = square(0), square(1)
    body = jnp.where(row >= col, first, second)
    diagonal = jnp.sum(jnp.where(row == col, second, 0.0), axis=0, keepdims=True)
    place = lax.broadcasted_iota(jnp.int32, (8, FBLK), 0)
    tail = jnp.where(place == 0, diagonal, 0.0)
    if spare is not None:
        tail = jnp.where(place == 1, spare, tail)
    return body, tail


def unpack(body, diagonal):
    row, col = square(0), square(1)
    turned = body.T
    first = jnp.where(row >= col, body, turned)
    second = jnp.where(row < col, body, jnp.where(row > col, turned, diagonal))
    return first, second


def grams(lengths, train, slabs):
    cycle = len(slabs)
    mine, half = lax.axis_index("dp"), lax.axis_index("rep")
    spare = lengths[...].astype(jnp.float32)
    for shift, slab in enumerate(slabs):
        owner = half * cycle + lax.rem(mine + shift, cycle)
        start = pl.multiple_of(owner * (2 * FBLK), 2 * FBLK)
        part = train[:, pl.ds(start, 2 * FBLK)]
        gram = lax.dot_general(part, part, (((0,), (0,)), ((), ())), preferred_element_type=jnp.float32)
        body, tail = pack(gram[:FBLK, :FBLK], gram[FBLK:, FBLK:], spare)
        slab[pl.ds(0, FBLK), :] = body
        slab[pl.ds(FBLK, 8), :] = tail


def thirds(value):
    high = value.astype(jnp.bfloat16)
    rest = value - high.astype(jnp.float32)
    middle = rest.astype(jnp.bfloat16)
    return high, middle, (rest - middle.astype(jnp.float32)).astype(jnp.bfloat16)


def at_rows(panel, first):
    pair = 2 * PANEL
    blank = jnp.zeros((PANEL, FBLK), jnp.float32)
    panel = panel.astype(jnp.float32)
    piece = jnp.concatenate([panel, blank] if first % pair == 0 else [blank, panel], axis=0).astype(jnp.bfloat16)
    before = first // pair * pair
    pieces = [jnp.zeros((before, FBLK), jnp.bfloat16), piece, jnp.zeros((FBLK - before - pair, FBLK), jnp.bfloat16)]
    return jnp.concatenate([piece for piece in pieces if piece.shape[0]], axis=0)


def product(left, right, first):
    high, middle, low = thirds(left)
    right_high, right_middle, right_low = (at_rows(part, first) for part in thirds(right))
    both = jnp.concatenate([right_high, right_middle], axis=1)
    large = jnp.dot(
        jnp.concatenate([high, middle], axis=1), jnp.concatenate([both, both], axis=0),
        preferred_element_type=jnp.float32,
    )
    small = jnp.dot(
        jnp.concatenate([high, low], axis=1), jnp.concatenate([right_low, right_high], axis=0),
        preferred_element_type=jnp.float32,
    )
    return large[:, :FBLK] + (large[:, FBLK:] + small)


def eliminated(panel, first):
    lane = lax.broadcasted_iota(jnp.int32, (PANEL, FBLK), 1)
    sublane = lax.broadcasted_iota(jnp.int32, (PANEL, FBLK), 0)
    within = (lane >= first) & (lane < first + PANEL)
    count = range(PANEL)

    def across(value, row):
        return jnp.broadcast_to(value[row:row + 1, :], (PANEL, FBLK))

    columns = [jnp.broadcast_to(panel[:, first + j:first + j + 1], (PANEL, FBLK)) for j in count]
    pivots = [[across(columns[j], i) if j >= i else None for j in count] for i in count]
    rest = jnp.where(within, jnp.where(lane == first + sublane, 1.0, 0.0), panel)
    lines = [across(rest, i) for i in count]
    for i in count:
        scale = 1.0 / pivots[i][i]
        scaled = lines[i] * scale
        shares = [pivots[i][j] * scale if j > i else None for j in count]
        for m in range(i + 1, PANEL):
            lines[m] = lines[m] - pivots[i][m] * scaled
            for j in range(m, PANEL):
                pivots[m][j] = pivots[m][j] - shares[m] * pivots[i][j]
        lines[i] = scaled
        pivots[i] = shares
    for i in reversed(count):
        for m in range(i):
            lines[m] = lines[m] - pivots[m][i] * lines[i]
    result = lines[0]
    for i in range(1, PANEL):
        result = jnp.where(sublane == i, lines[i], result)
    return result


def inverted(blocks):
    lane = square(1)
    for first in range(0, FBLK, PANEL):
        within = (lane >= first) & (lane < first + PANEL)
        panels = [eliminated(block[first:first + PANEL, :], first) for block in blocks]
        updates = [product(block, panel, first) for block, panel in zip(blocks, panels)]
        rests = [jnp.where(within, 0.0, block) - update for block, update in zip(blocks, updates)]
        blocks = [
            jnp.concatenate(
                [part for part in (rest[:first], panel, rest[first + PANEL:]) if part.shape[0]], axis=0
            )
            for rest, panel in zip(rests, panels)
        ]
    return blocks


def factor_kernel(examples, scale, *refs):
    slabs, out = refs[:-2], refs[-1]
    body = slabs[0][pl.ds(0, FBLK), :]
    diagonal = slabs[0][pl.ds(FBLK, 1), :]
    for slab in slabs[1:]:
        body = body + slab[pl.ds(0, FBLK), :]
        diagonal = diagonal + slab[pl.ds(FBLK, 1), :]
    same = square(0) == square(1)
    damped = []
    for gram in unpack(body, diagonal):
        fisher = gram / examples
        trace = jnp.sum(jnp.sum(jnp.where(same, fisher, 0.0), axis=0, keepdims=True), axis=1, keepdims=True)
        damped.append(fisher + jnp.where(same, damping * (trace / FBLK), 0.0))
    first, second = inverted(damped)
    body, tail = pack(first * scale, second * scale)
    out[pl.ds(0, FBLK), :] = body
    out[pl.ds(FBLK, 8), :] = tail


def first_kernel(id_rows_hbm, delta_hbm, table_hbm, factor_hbm, lengths_hbm, train_hbm, sent, own, *refs):
    slabs, refs = refs[:-10], refs[-10:]
    id_rows, places, reads, delta, table, factor, lengths, train, looked, sems = refs
    model = lax.axis_index("mp")
    proj, vocab_rows = table.shape
    tokens = delta.shape[0]
    each = proj // lax.axis_size("mp")
    groups, pieces = tokens // FBLK, proj // ROWS
    get_ids, get_factor, get_lengths, get_train = (
        pltpu.make_async_copy(source, target, sems.at[0, index])
        for index, (source, target) in enumerate((
            (id_rows_hbm, id_rows), (factor_hbm, factor), (lengths_hbm, lengths), (train_hbm, train),
        ))
    )
    get_table = [
        pltpu.make_async_copy(table_hbm.at[rows], table.at[rows], sems.at[1, index])
        for index in range(pieces) for rows in (pl.ds(index * ROWS, ROWS),)
    ]

    def get_delta(g):
        rows = pl.ds(pl.multiple_of(g * FBLK, FBLK), FBLK)
        return pltpu.make_async_copy(delta_hbm.at[rows], delta.at[rows], sems.at[2, g])

    first = (get_ids, get_table[0], get_lengths, get_train)
    for copy in (*first, *get_table[1:], get_factor, *(get_delta(g) for g in range(groups))):
        copy.start()
    get_ids.wait()
    local = id_rows[...] - model * vocab_rows
    owned = (local >= 0) & (local < vocab_rows)
    local = jnp.where(owned, local, 0)
    low = FBLK - 1
    roll = (lax.broadcasted_iota(jnp.int32, local.shape, 1) - local) & low
    places[...] = (local & ~low) | roll
    fetch = pltpu.make_async_copy(places, reads, sems.at[0, 4])
    fetch.start()
    fetch.wait()
    places[...] = owned.astype(jnp.int32)
    lanes = lax.broadcasted_iota(jnp.int32, (ROWS, FBLK), 1)

    def gather(piece, g):
        columns = pl.ds(pl.multiple_of(g * FBLK, FBLK), FBLK)
        gathered = jnp.zeros((ROWS, FBLK), jnp.bfloat16)
        for j in range(FBLK):
            place = reads[g, j]
            block = table[pl.ds(piece * ROWS, ROWS), pl.ds(pl.multiple_of(place & ~low, FBLK), FBLK)]
            gathered = jnp.where(lanes == j, pltpu.roll(block, place & low, 1), gathered)
        held = places[pl.ds(g, 1), :].astype(jnp.float32)
        gathered = (gathered.astype(jnp.float32) * held).astype(jnp.bfloat16)
        rows = pl.ds(2 * each + piece * ROWS, ROWS)
        sent[rows, columns] = gathered
        own[rows, columns] = gathered

    def project(g):
        columns = pl.ds(pl.multiple_of(g * FBLK, FBLK), FBLK)
        get_delta(g).wait()
        output = lax.dot_general(
            delta[columns, :], factor[...], (((1,), (1,)), ((), ())), preferred_element_type=jnp.float32
        )
        looked[:, columns] = output.T

    for piece in range(pieces):
        get_table[piece].wait()
        if piece == 1:
            get_lengths.wait()
            get_train.wait()
            grams(lengths, train, slabs)
        if piece == pieces - 1:
            get_factor.wait()

        def group(g, carry):
            if piece == pieces - 1:
                project(g)
            gather(piece, g)
            return carry

        lax.fori_loop(0, groups, group, 0)
    mine = looked[pl.ds(pl.multiple_of(model * each, each), each), :]
    other = looked[pl.ds(pl.multiple_of((1 - model) * each, each), each), :]
    for target, value in ((own, mine), (sent, other)):
        high, rest = halves(value)
        target[pl.ds(0, each), :] = high
        target[pl.ds(each, each), :] = rest


def merge_kernel(each, own, got, out):
    def value(ref):
        return ref[pl.ds(0, each), :].astype(jnp.float32) + ref[pl.ds(each, each), :].astype(jnp.float32)

    high, low = halves(value(own) + value(got))
    out[pl.ds(0, each), :] = high
    out[pl.ds(each, each), :] = low
    rows = pl.ds(2 * each, out.shape[0] - 2 * each)
    out[rows, :] = own[rows, :] + got[rows, :]


def queries_kernel(each, factors, slab, *refs):
    after, high_out, low_out, again = refs if len(refs) == 4 else (None, *refs, None)
    if again is not None:
        again[...] = factors[...]
    tokens = factors.shape[1]
    proj = factors.shape[0] - 2 * each
    queries = high_out.shape[1]
    lengths = slab[pl.ds(FBLK + 1, 1), :]
    upto = jnp.where(square(0) <= square(1), 1.0, 0.0).astype(jnp.bfloat16)
    ends = lax.dot_general(
        jnp.broadcast_to(lengths, (8, queries)).astype(jnp.bfloat16), upto, (((1,), (0,)), ((), ())),
        preferred_element_type=jnp.float32,
    )[:1]
    starts = ends - lengths
    place = lax.broadcasted_iota(jnp.int32, (tokens, queries), 0).astype(jnp.float32)
    inside = jnp.where((place >= starts) & (place < ends), 1.0, 0.0).astype(jnp.bfloat16)
    output = factors[pl.ds(0, each), :].astype(jnp.float32) + factors[pl.ds(each, each), :].astype(jnp.float32)
    inputs = factors[pl.ds(2 * each, proj), :].astype(jnp.float32)
    step = 8
    for start in range(0, each, step):
        grads = jnp.concatenate(
            [(inputs * output[r:r + 1, :]).astype(jnp.bfloat16) for r in range(start, start + step)], axis=0
        )
        summed = jnp.dot(grads, inside, preferred_element_type=jnp.float32)
        high, low = halves(summed)
        high_out[pl.ds(start * proj, step * proj), :] = high
        low_out[pl.ds(start * proj, step * proj), :] = low


def hand_kernel(slab, *refs):
    refs[-1][...] = slab[...]


def scores_kernel(cycle, count, *refs):
    own, peers = refs[:cycle], refs[cycle:2 * cycle]
    highs, lows = refs[2 * cycle:2 * cycle + count], refs[2 * cycle + count:2 * cycle + 2 * count]
    train, sent, kept, pre = refs[2 * cycle + 2 * count:]
    mine, rep, model = lax.axis_index("dp"), lax.axis_index("rep"), lax.axis_index("mp")
    for half, slabs in ((rep, own), (1 - rep, peers)):
        for shift in range(cycle):
            owner = half * cycle + lax.rem(mine + cycle - shift, cycle)
            slab = slabs[shift]
            blocks = unpack(slab[pl.ds(0, FBLK), :], slab[pl.ds(FBLK, 1), :])
            for index, block in enumerate(blocks):
                rows = pl.ds(pl.multiple_of(owner * (2 * FBLK) + index * FBLK, FBLK), FBLK)
                high, low = halves(block)
                right_high = jnp.concatenate([ref[rows, :] for ref in highs], axis=1)
                right_low = jnp.concatenate([ref[rows, :] for ref in lows], axis=1)
                solved = jnp.dot(
                    jnp.concatenate([high, high, low], axis=1),
                    jnp.concatenate([right_high, right_low, right_high], axis=0),
                    preferred_element_type=jnp.float32,
                )
                pre[rows, :] = solved.astype(jnp.bfloat16)
    half_rows = sent.shape[0]
    for out, which in ((sent, 1 - model), (kept, model)):
        rows = pl.ds(pl.multiple_of(which * half_rows, half_rows), half_rows)
        out[...] = jnp.dot(train[rows, :], pre[...], preferred_element_type=jnp.float32).astype(jnp.bfloat16)


def total_kernel(order, *refs):
    pieces, out = refs[:-1], refs[-1]
    mine, cycle = lax.axis_index("dp"), len(order)
    sums = {}
    for kept, got in zip(pieces[::2], pieces[1::2]):
        both = kept[...].astype(jnp.float32) + got[...].astype(jnp.float32)
        for index in range(both.shape[1] // FBLK):
            sums[order[len(sums)]] = both[:, index * FBLK:(index + 1) * FBLK]
    placed = []
    for source in range(cycle):
        shift = lax.rem(mine + cycle - source, cycle)
        value = sums[0]
        for index in range(1, cycle):
            value = jnp.where(shift == index, sums[index], value)
        placed.append(value)
    out[...] = jnp.stack(placed, axis=1).astype(jnp.bfloat16)


def shape(dims, dtype):
    return jax.ShapeDtypeStruct(dims, dtype)


def split_over_blocks(query_ids, query_delta, doc_lengths, vocab_factor, output_factor, train_grads):
    cycle = lax.axis_size("dp")
    tokens, width = query_delta.shape
    proj = output_factor.shape[1]
    each = proj // lax.axis_size("mp")
    vocab_rows = vocab_factor.shape[0]
    train_rows, feat = train_grads.shape
    queries = doc_lengths.shape[1]
    bf16, f32 = jnp.bfloat16, jnp.float32

    sent, own, *slabs = call(
        first_kernel,
        [shape((2 * each + proj, tokens), bf16)] * 2 + [shape((SLAB, FBLK), f32)] * cycle,
        [HBM] * 6,
        [
            pltpu.VMEM((tokens // FBLK, FBLK), jnp.int32),
            pltpu.VMEM((tokens // FBLK, FBLK), jnp.int32),
            pltpu.SMEM((tokens // FBLK, FBLK), jnp.int32),
            pltpu.VMEM((tokens, width), bf16),
            pltpu.VMEM((proj, vocab_rows), bf16),
            pltpu.VMEM((proj, width), bf16),
            pltpu.VMEM((1, queries), jnp.int32),
            pltpu.VMEM((train_rows, feat), bf16),
            pltpu.VMEM((proj, tokens), f32),
            pltpu.SemaphoreType.DMA((3, 8)),
        ],
        vmem=62,
        flops=2 * tokens * width * proj,
        moved=2 * (tokens * width + proj * vocab_rows) * 2,
    )(
        query_ids.reshape(tokens // FBLK, FBLK), query_delta, vocab_factor.T, output_factor.T,
        doc_lengths, train_grads,
    )
    got = passed_along(sent, "mp", 1)
    parts = [slabs[0]] + [passed_along(slabs[s], "dp", s) for s in range(1, cycle)]

    factors = call(
        functools.partial(merge_kernel, each),
        shape(sent.shape, bf16),
        [VMEM, VMEM],
        vmem=16,
        flops=tokens * each,
        moved=8 * tokens * each * 4,
    )(own, got)
    late = cycle // 2
    gathered = [factors] + [passed_along(factors, "dp", s) if s != late else None for s in range(1, cycle)]

    inverse = call(
        functools.partial(factor_kernel, train_rows * cycle, 1.0 / proj),
        shape((SLAB, FBLK), f32),
        [VMEM] * cycle + [HBM],
        vmem=16,
        flops=10 ** 10,
        moved=10 ** 6,
    )(*parts, factors)
    inverses = [inverse] + [passed_along(inverse, "dp", s) for s in range(1, cycle)]
    highs, lows = {}, {}
    for s in sorted(range(cycle), key=lambda shift: (shift == late, shift)):
        first = s == 0
        highs[s], lows[s], *again = call(
            functools.partial(queries_kernel, each),
            [shape((feat, queries), bf16)] * 2 + [shape(factors.shape, bf16)] * first,
            [VMEM, VMEM] + [HBM] * first,
            vmem=24,
            flops=2 * feat * tokens * queries,
            moved=6 * feat * queries,
        )(gathered[s], parts[s], *[inverse] * first)
        if first:
            gathered[late] = passed_along(again[0], "dp", late)
    handed = list(inverses)
    handed[late] = call(
        hand_kernel,
        shape((SLAB, FBLK), f32),
        [VMEM] + [HBM] * (cycle - 2),
        vmem=16,
        moved=8 * SLAB * FBLK,
    )(inverses[late], *[highs[s] for s in range(1, cycle) if s != late])
    peers = [passed_along(slab, "rep", 1) for slab in handed]

    half_rows = train_rows // lax.axis_size("mp")
    pieces, order = [], []
    for chosen in ([s for s in range(cycle) if s != late], [late]):
        count = len(chosen)
        outgoing, kept = call(
            functools.partial(scores_kernel, cycle, count),
            [shape((half_rows, count * queries), bf16)] * 2,
            [VMEM] * (2 * cycle + 2 * count + 1),
            [pltpu.VMEM((feat, count * queries), bf16)],
            vmem=24,
            flops=2 * train_rows * feat * count * queries,
            moved=8 * feat * queries * count,
        )(*inverses, *peers, *[highs[s] for s in chosen], *[lows[s] for s in chosen], train_grads)
        pieces += [kept, passed_along(outgoing, "mp", 1)]
        order += chosen
    total = call(
        functools.partial(total_kernel, order),
        shape((half_rows, cycle, queries), bf16),
        [VMEM] * len(pieces),
        vmem=16,
        flops=half_rows * cycle * queries,
        moved=6 * half_rows * cycle * queries,
    )(*pieces)
    return total[:, :, None, :]


def doc_matrix(lengths_row, count):
    ends = jnp.cumsum(lengths_row)
    starts = ends - lengths_row
    place = jnp.arange(count, dtype=jnp.int32)
    inside = (place[None, :] >= starts[:, None]) & (place[None, :] < ends[:, None])
    return inside.astype(jnp.bfloat16)


def solve_block(factor, rhs):
    return jax.scipy.linalg.cho_solve((factor, True), rhs)


def general(query_ids, query_delta, doc_lengths, vocab_factor, output_factor, train_grads):
    model_count = lax.axis_size("mp")
    model_index = lax.axis_index("mp")
    vocab_rows = vocab_factor.shape[0]
    local_ids = query_ids - model_index * vocab_rows
    owned = (local_ids >= 0) & (local_ids < vocab_rows)
    looked = vocab_factor[jnp.clip(local_ids, 0, vocab_rows - 1)].astype(jnp.float32)
    vocab_part = jnp.where(owned[:, None], looked, jnp.zeros_like(looked))
    output_part = jnp.dot(query_delta, output_factor, preferred_element_type=jnp.float32)
    input_side, output_side = lax.psum((vocab_part, output_part), "mp")
    proj = output_side.shape[1]
    rows_each = proj // model_count
    mine = lax.dynamic_slice_in_dim(output_side, model_index * rows_each, rows_each, 1)
    token_count = query_ids.shape[0]
    token_grads = (
        (mine[:, :, None] * input_side[:, None, :])
        .reshape(token_count, rows_each * proj)
        .astype(jnp.bfloat16)
    )
    query_grads = jnp.dot(
        doc_matrix(doc_lengths[0], token_count), token_grads, preferred_element_type=jnp.float32
    )
    train_rows, feat_dev = train_grads.shape
    nblocks = feat_dev // FBLK
    tiled = train_grads.reshape(train_rows, nblocks, FBLK)
    local_gram = jnp.einsum("tbi,tbj->bij", tiled, tiled, preferred_element_type=jnp.float32)
    total_gram = lax.psum(local_gram, "dp")
    fisher = total_gram / (train_rows * lax.axis_size("dp"))
    shift_amount = damping * (jnp.trace(fisher, axis1=1, axis2=2) / FBLK)
    damped = fisher + shift_amount[:, None, None] * jnp.eye(FBLK, dtype=jnp.float32)[None]
    factor = jnp.linalg.cholesky(damped)
    queries = query_grads.shape[0]
    rhs = jnp.transpose(query_grads.reshape(queries, nblocks, FBLK), (1, 2, 0))
    solved = jax.vmap(solve_block)(factor, rhs)
    pre = (jnp.transpose(solved, (2, 0, 1)).reshape(queries, feat_dev) / proj).astype(jnp.bfloat16)
    cycle = lax.axis_size("dp")
    everyone = lax.all_gather(pre, "dp", axis=0, tiled=True)
    scores = lax.dot_general(
        train_grads, everyone, (((1,), (1,)), ((), ())), preferred_element_type=jnp.float32
    )
    scores = scores.astype(jnp.bfloat16).reshape(train_rows, cycle, queries)
    summed = lax.psum_scatter(scores, "mp", scatter_dimension=0, tiled=True)
    return summed[:, :, None, :]


def per_device(query_ids, query_delta, doc_lengths, vocab_factor, output_factor, train_grads):
    owners = lax.axis_size("dp") * lax.axis_size("rep")
    fits = (
        train_grads.shape[1] == 2 * FBLK * owners
        and lax.axis_size("mp") == 2
        and lax.axis_size("rep") == 2
        and doc_lengths.shape[1] == FBLK
        and vocab_factor.shape[0] % FBLK == 0
    )
    body = split_over_blocks if fits else general
    return body(query_ids, query_delta, doc_lengths, vocab_factor, output_factor, train_grads)


def solution(mesh):
    placed = (
        P(("groups", "dp", "rep")),
        P(("groups", "dp", "rep"), "mp"),
        P(("groups", "dp", "rep"), None),
        P("mp", None),
        P("mp", None),
        P(("groups", "dp"), "mp"),
    )
    return jax.shard_map(
        per_device,
        mesh=mesh,
        in_specs=placed,
        out_specs=P(("groups", "dp", "mp"), None, "rep", None),
        check_vma=False,
    )
```

```python
import functools
import jax
import jax.numpy as jnp
from jax import lax
from jax.experimental import pallas as pl
from jax.experimental.pallas import tpu as pltpu
from jax.sharding import PartitionSpec as P

FBLK = 128
SLAB = FBLK + 8
PANEL = 8
ROWS = 16

damping = 0.1

VMEM = pl.BlockSpec(memory_space=pltpu.VMEM)
SMEM = pl.BlockSpec(memory_space=pltpu.SMEM)
HBM = pl.BlockSpec(memory_space=pl.ANY)


def call(kernel, outs, in_specs, scratch=(), vmem=48, flops=0, moved=0):
    return pl.pallas_call(
        kernel,
        out_shape=outs,
        in_specs=in_specs,
        scratch_shapes=list(scratch),
        compiler_params=pltpu.CompilerParams(vmem_limit_bytes=vmem << 20),
        cost_estimate=pl.CostEstimate(flops=flops, bytes_accessed=moved, transcendentals=0),
    )


def swapped(shard, axis, by):
    return lax.ppermute(shard, axis, [(i, i ^ by) for i in range(lax.axis_size(axis))])


def square(dim):
    return lax.broadcasted_iota(jnp.int32, (FBLK, FBLK), dim)


def halves(value):
    high = value.astype(jnp.bfloat16)
    return high, (value - high.astype(jnp.float32)).astype(jnp.bfloat16)


def pack(first, second, spare=None):
    row, col = square(0), square(1)
    body = jnp.where(row >= col, first, second)
    diagonal = jnp.sum(jnp.where(row == col, second, 0.0), axis=0, keepdims=True)
    place = lax.broadcasted_iota(jnp.int32, (8, FBLK), 0)
    tail = jnp.where(place == 0, diagonal, 0.0)
    if spare is not None:
        tail = jnp.where(place == 1, spare, tail)
    return body, tail


def unpack(body, diagonal):
    row, col = square(0), square(1)
    turned = body.T
    first = jnp.where(row >= col, body, turned)
    second = jnp.where(row < col, body, jnp.where(row > col, turned, diagonal))
    return first, second


def grams(lengths, train, slabs):
    cycle = len(slabs)
    mine, half = lax.axis_index("dp"), lax.axis_index("rep")
    spare = lengths[...].astype(jnp.float32)
    for shift, slab in enumerate(slabs):
        owner = half * cycle + (mine ^ shift)
        start = pl.multiple_of(owner * (2 * FBLK), 2 * FBLK)
        part = train[:, pl.ds(start, 2 * FBLK)]
        gram = lax.dot_general(part, part, (((0,), (0,)), ((), ())), preferred_element_type=jnp.float32)
        body, tail = pack(gram[:FBLK, :FBLK], gram[FBLK:, FBLK:], spare)
        slab[pl.ds(0, FBLK), :] = body
        slab[pl.ds(FBLK, 8), :] = tail


def thirds(value):
    high = value.astype(jnp.bfloat16)
    rest = value - high.astype(jnp.float32)
    middle = rest.astype(jnp.bfloat16)
    return high, middle, (rest - middle.astype(jnp.float32)).astype(jnp.bfloat16)


def at_rows(panel, first):
    pair = 2 * PANEL
    blank = jnp.zeros((PANEL, FBLK), jnp.float32)
    panel = panel.astype(jnp.float32)
    piece = jnp.concatenate([panel, blank] if first % pair == 0 else [blank, panel], axis=0).astype(jnp.bfloat16)
    before = first // pair * pair
    pieces = [jnp.zeros((before, FBLK), jnp.bfloat16), piece, jnp.zeros((FBLK - before - pair, FBLK), jnp.bfloat16)]
    return jnp.concatenate([piece for piece in pieces if piece.shape[0]], axis=0)


def product(left, right, first):
    high, middle, low = thirds(left)
    right_high, right_middle, right_low = (at_rows(part, first) for part in thirds(right))
    both = jnp.concatenate([right_high, right_middle], axis=1)
    large = jnp.dot(
        jnp.concatenate([high, middle], axis=1), jnp.concatenate([both, both], axis=0),
        preferred_element_type=jnp.float32,
    )
    small = jnp.dot(
        jnp.concatenate([high, low], axis=1), jnp.concatenate([right_low, right_high], axis=0),
        preferred_element_type=jnp.float32,
    )
    return large[:, :FBLK] + (large[:, FBLK:] + small)


def eliminated(panel, first):
    lane = lax.broadcasted_iota(jnp.int32, (PANEL, FBLK), 1)
    sublane = lax.broadcasted_iota(jnp.int32, (PANEL, FBLK), 0)
    within = (lane >= first) & (lane < first + PANEL)
    count = range(PANEL)

    def across(value, row):
        return jnp.broadcast_to(value[row:row + 1, :], (PANEL, FBLK))

    columns = [jnp.broadcast_to(panel[:, first + j:first + j + 1], (PANEL, FBLK)) for j in count]
    pivots = [[across(columns[j], i) if j >= i else None for j in count] for i in count]
    rest = jnp.where(within, jnp.where(lane == first + sublane, 1.0, 0.0), panel)
    lines = [across(rest, i) for i in count]
    for i in count:
        scale = 1.0 / pivots[i][i]
        scaled = lines[i] * scale
        shares = [pivots[i][j] * scale if j > i else None for j in count]
        for m in range(i + 1, PANEL):
            lines[m] = lines[m] - pivots[i][m] * scaled
            for j in range(m, PANEL):
                pivots[m][j] = pivots[m][j] - shares[m] * pivots[i][j]
        lines[i] = scaled
        pivots[i] = shares
    for i in reversed(count):
        for m in range(i):
            lines[m] = lines[m] - pivots[m][i] * lines[i]
    result = lines[0]
    for i in range(1, PANEL):
        result = jnp.where(sublane == i, lines[i], result)
    return result


def inverted(blocks):
    lane = square(1)
    for first in range(0, FBLK, PANEL):
        within = (lane >= first) & (lane < first + PANEL)
        panels = [eliminated(block[first:first + PANEL, :], first) for block in blocks]
        updates = [product(block, panel, first) for block, panel in zip(blocks, panels)]
        rests = [jnp.where(within, 0.0, block) - update for block, update in zip(blocks, updates)]
        blocks = [
            jnp.concatenate(
                [part for part in (rest[:first], panel, rest[first + PANEL:]) if part.shape[0]], axis=0
            )
            for rest, panel in zip(rests, panels)
        ]
    return blocks


def factor_kernel(examples, scale, *refs):
    slabs, out = refs[:-2], refs[-1]
    body = slabs[0][pl.ds(0, FBLK), :]
    diagonal = slabs[0][pl.ds(FBLK, 1), :]
    for slab in slabs[1:]:
        body = body + slab[pl.ds(0, FBLK), :]
        diagonal = diagonal + slab[pl.ds(FBLK, 1), :]
    same = square(0) == square(1)
    damped = []
    for gram in unpack(body, diagonal):
        fisher = gram / examples
        trace = jnp.sum(jnp.sum(jnp.where(same, fisher, 0.0), axis=0, keepdims=True), axis=1, keepdims=True)
        damped.append(fisher + jnp.where(same, damping * (trace / FBLK), 0.0))
    first, second = inverted(damped)
    body, tail = pack(first * scale, second * scale)
    out[pl.ds(0, FBLK), :] = body
    out[pl.ds(FBLK, 8), :] = tail


def first_kernel(id_rows_hbm, delta_hbm, table_hbm, factor_hbm, lengths_hbm, train_hbm, sent, own, *refs):
    slabs, refs = refs[:-12], refs[-12:]
    id_rows, starts, rolls, start_of, roll_of, delta, table, factor, lengths, train, looked, sems = refs
    model = lax.axis_index("mp")
    proj, vocab_rows = table.shape
    tokens = delta.shape[0]
    each = proj // lax.axis_size("mp")
    groups = tokens // FBLK
    get_ids, get_factor, get_lengths, get_train = (
        pltpu.make_async_copy(source, target, sems.at[0, index])
        for index, (source, target) in enumerate((
            (id_rows_hbm, id_rows), (factor_hbm, factor), (lengths_hbm, lengths), (train_hbm, train),
        ))
    )
    get_table = [
        pltpu.make_async_copy(table_hbm.at[rows], table.at[rows], sems.at[1, index])
        for index in range(proj // ROWS) for rows in (pl.ds(index * ROWS, ROWS),)
    ]

    def get_delta(g):
        rows = pl.ds(pl.multiple_of(g * FBLK, FBLK), FBLK)
        return pltpu.make_async_copy(delta_hbm.at[rows], delta.at[rows], sems.at[2, g])

    for copy in (get_ids, get_lengths, get_train, *get_table, get_factor, *(get_delta(g) for g in range(groups))):
        copy.start()
    get_ids.wait()
    local = id_rows[...] - model * vocab_rows
    owned = (local >= 0) & (local < vocab_rows)
    local = jnp.where(owned, local, 0)
    low = FBLK - 1
    starts[...] = local & ~low
    rolls[...] = (lax.broadcasted_iota(jnp.int32, local.shape, 1) - local) & low
    fetches = [pltpu.make_async_copy(starts, start_of, sems.at[0, 4]), pltpu.make_async_copy(rolls, roll_of, sems.at[0, 5])]
    for fetch in fetches:
        fetch.start()
    get_lengths.wait()
    get_train.wait()
    grams(lengths, train, slabs)
    for fetch in fetches:
        fetch.wait()
    starts[...] = owned.astype(jnp.int32)
    for copy in get_table:
        copy.wait()
    get_factor.wait()
    lanes = lax.broadcasted_iota(jnp.int32, (ROWS, FBLK), 1)

    def group(g, carry):
        columns = pl.ds(pl.multiple_of(g * FBLK, FBLK), FBLK)
        get_delta(g).wait()
        output = lax.dot_general(
            delta[columns, :], factor[...], (((1,), (1,)), ((), ())), preferred_element_type=jnp.float32
        )
        looked[:, columns] = output.T
        gathered = [jnp.zeros((ROWS, FBLK), jnp.bfloat16) for _ in range(proj // ROWS)]
        for j in range(FBLK):
            start, by, here = pl.multiple_of(start_of[g, j], FBLK), roll_of[g, j], lanes == j
            for index in range(proj // ROWS):
                block = table[pl.ds(index * ROWS, ROWS), pl.ds(start, FBLK)]
                gathered[index] = jnp.where(here, pltpu.roll(block, by, 1), gathered[index])
        held = starts[pl.ds(g, 1), :].astype(jnp.float32)
        for index, value in enumerate(gathered):
            value = (value.astype(jnp.float32) * held).astype(jnp.bfloat16)
            rows = pl.ds(2 * each + index * ROWS, ROWS)
            sent[rows, columns] = value
            own[rows, columns] = value
        return carry

    lax.fori_loop(0, groups, group, 0)
    mine = looked[pl.ds(pl.multiple_of(model * each, each), each), :]
    other = looked[pl.ds(pl.multiple_of((1 - model) * each, each), each), :]
    for target, value in ((own, mine), (sent, other)):
        high, rest = halves(value)
        target[pl.ds(0, each), :] = high
        target[pl.ds(each, each), :] = rest


def merge_kernel(each, own, got, out):
    def value(ref):
        return ref[pl.ds(0, each), :].astype(jnp.float32) + ref[pl.ds(each, each), :].astype(jnp.float32)

    high, low = halves(value(own) + value(got))
    out[pl.ds(0, each), :] = high
    out[pl.ds(each, each), :] = low
    rows = pl.ds(2 * each, out.shape[0] - 2 * each)
    out[rows, :] = own[rows, :] + got[rows, :]


def queries_kernel(each, factors, slab, *refs):
    high_out, low_out = refs[-2:]
    if len(refs) == 4:
        source, high_out, low_out, copy = refs
        copy[...] = source[...]
    tokens = factors.shape[1]
    proj = factors.shape[0] - 2 * each
    queries = high_out.shape[1]
    lengths = slab[pl.ds(FBLK + 1, 1), :]
    upto = jnp.where(square(0) <= square(1), 1.0, 0.0).astype(jnp.bfloat16)
    ends = lax.dot_general(
        jnp.broadcast_to(lengths, (8, queries)).astype(jnp.bfloat16), upto, (((1,), (0,)), ((), ())),
        preferred_element_type=jnp.float32,
    )[:1]
    starts = ends - lengths
    place = lax.broadcasted_iota(jnp.int32, (tokens, queries), 0).astype(jnp.float32)
    inside = jnp.where((place >= starts) & (place < ends), 1.0, 0.0).astype(jnp.bfloat16)
    output = factors[pl.ds(0, each), :].astype(jnp.float32) + factors[pl.ds(each, each), :].astype(jnp.float32)
    inputs = factors[pl.ds(2 * each, proj), :].astype(jnp.float32)
    step = 8
    for start in range(0, each, step):
        grads = jnp.concatenate(
            [(inputs * output[r:r + 1, :]).astype(jnp.bfloat16) for r in range(start, start + step)], axis=0
        )
        summed = jnp.dot(grads, inside, preferred_element_type=jnp.float32)
        high, low = halves(summed)
        high_out[pl.ds(start * proj, step * proj), :] = high
        low_out[pl.ds(start * proj, step * proj), :] = low


def hand_kernel(slab, *refs):
    refs[-1][...] = slab[...]


def scores_kernel(cycle, count, *refs):
    own, peers = refs[:cycle], refs[cycle:2 * cycle]
    highs, lows = refs[2 * cycle:2 * cycle + count], refs[2 * cycle + count:2 * cycle + 2 * count]
    train, sent, kept, pre = refs[2 * cycle + 2 * count:]
    mine, rep, model = lax.axis_index("dp"), lax.axis_index("rep"), lax.axis_index("mp")
    for half, slabs in ((rep, own), (1 - rep, peers)):
        for shift in range(cycle):
            owner = half * cycle + (mine ^ shift)
            slab = slabs[shift]
            blocks = unpack(slab[pl.ds(0, FBLK), :], slab[pl.ds(FBLK, 1), :])
            for index, block in enumerate(blocks):
                rows = pl.ds(pl.multiple_of(owner * (2 * FBLK) + index * FBLK, FBLK), FBLK)
                high, low = halves(block)
                right_high = jnp.concatenate([ref[rows, :] for ref in highs], axis=1)
                right_low = jnp.concatenate([ref[rows, :] for ref in lows], axis=1)
                solved = jnp.dot(
                    jnp.concatenate([high, high, low], axis=1),
                    jnp.concatenate([right_high, right_low, right_high], axis=0),
                    preferred_element_type=jnp.float32,
                )
                pre[rows, :] = solved.astype(jnp.bfloat16)
    half_rows = sent.shape[0]
    for out, which in ((sent, 1 - model), (kept, model)):
        rows = pl.ds(pl.multiple_of(which * half_rows, half_rows), half_rows)
        out[...] = jnp.dot(train[rows, :], pre[...], preferred_element_type=jnp.float32).astype(jnp.bfloat16)


def total_kernel(order, *refs):
    pieces, out = refs[:-1], refs[-1]
    mine, cycle = lax.axis_index("dp"), len(order)
    sums = {}
    for kept, got in zip(pieces[::2], pieces[1::2]):
        both = kept[...].astype(jnp.float32) + got[...].astype(jnp.float32)
        for index in range(both.shape[1] // FBLK):
            sums[order[len(sums)]] = both[:, index * FBLK:(index + 1) * FBLK]
    placed = []
    for source in range(cycle):
        shift = mine ^ source
        value = sums[0]
        for index in range(1, cycle):
            value = jnp.where(shift == index, sums[index], value)
        placed.append(value)
    out[...] = jnp.concatenate(placed, axis=1).astype(jnp.bfloat16)


def shape(dims, dtype):
    return jax.ShapeDtypeStruct(dims, dtype)


def split_over_blocks(query_ids, query_delta, doc_lengths, vocab_factor, output_factor, train_grads):
    cycle = lax.axis_size("dp")
    tokens, width = query_delta.shape
    proj = output_factor.shape[1]
    each = proj // lax.axis_size("mp")
    vocab_rows = vocab_factor.shape[0]
    train_rows, feat = train_grads.shape
    queries = doc_lengths.shape[1]
    bf16, f32 = jnp.bfloat16, jnp.float32

    sent, own, *slabs = call(
        first_kernel,
        [shape((2 * each + proj, tokens), bf16)] * 2 + [shape((SLAB, FBLK), f32)] * cycle,
        [HBM] * 6,
        [
            pltpu.VMEM((tokens // FBLK, FBLK), jnp.int32),
            pltpu.VMEM((tokens // FBLK, FBLK), jnp.int32),
            pltpu.VMEM((tokens // FBLK, FBLK), jnp.int32),
            pltpu.SMEM((tokens // FBLK, FBLK), jnp.int32),
            pltpu.SMEM((tokens // FBLK, FBLK), jnp.int32),
            pltpu.VMEM((tokens, width), bf16),
            pltpu.VMEM((proj, vocab_rows), bf16),
            pltpu.VMEM((proj, width), bf16),
            pltpu.VMEM((1, queries), jnp.int32),
            pltpu.VMEM((train_rows, feat), bf16),
            pltpu.VMEM((proj, tokens), f32),
            pltpu.SemaphoreType.DMA((3, 8)),
        ],
        vmem=62,
        flops=2 * tokens * width * proj,
        moved=2 * (tokens * width + proj * vocab_rows) * 2,
    )(
        query_ids.reshape(tokens // FBLK, FBLK), query_delta, vocab_factor.T, output_factor.T,
        doc_lengths, train_grads,
    )
    got = swapped(sent, "mp", 1)
    parts = [slabs[0]] + [swapped(slabs[s], "dp", s) for s in range(1, cycle)]

    factors = call(
        functools.partial(merge_kernel, each),
        shape(sent.shape, bf16),
        [VMEM, VMEM],
        vmem=16,
        flops=tokens * each,
        moved=8 * tokens * each * 4,
    )(own, got)
    late = cycle - 1
    gathered = [factors] + [swapped(factors, "dp", s) if s != late else None for s in range(1, cycle)]

    inverse = call(
        functools.partial(factor_kernel, train_rows * cycle, 1.0 / proj),
        shape((SLAB, FBLK), f32),
        [VMEM] * cycle + [HBM],
        vmem=16,
        flops=10 ** 10,
        moved=10 ** 6,
    )(*parts, factors)
    inverses = [inverse] + [swapped(inverse, "dp", s) for s in range(1, cycle)]
    highs, lows = {}, {}
    for s in range(cycle):
        extra = {0: [inverse], 1: [factors]}.get(s, [])
        highs[s], lows[s], *again = call(
            functools.partial(queries_kernel, each),
            [shape((feat, queries), bf16)] * 2 + [shape(factors.shape, bf16)] * (s == 1),
            [VMEM, VMEM] + [HBM if s == 0 else VMEM] * len(extra),
            vmem=24,
            flops=2 * feat * tokens * queries,
            moved=6 * feat * queries,
        )(gathered[s], parts[s], *extra)
        if s == 1:
            gathered[late] = swapped(again[0], "dp", late)
    handed = list(inverses)
    handed[late] = call(
        hand_kernel,
        shape((SLAB, FBLK), f32),
        [VMEM] + [HBM] * (cycle - 1),
        vmem=16,
        moved=8 * SLAB * FBLK,
    )(inverses[late], *[highs[s] for s in range(cycle) if s != late])
    peers = [swapped(slab, "rep", 1) for slab in handed]

    half_rows = train_rows // lax.axis_size("mp")
    pieces, order = [], []
    for chosen in ([s for s in range(cycle) if s != late], [late]):
        count = len(chosen)
        outgoing, kept = call(
            functools.partial(scores_kernel, cycle, count),
            [shape((half_rows, count * queries), bf16)] * 2,
            [VMEM] * (2 * cycle + 2 * count + 1),
            [pltpu.VMEM((feat, count * queries), bf16)],
            vmem=24,
            flops=2 * train_rows * feat * count * queries,
            moved=8 * feat * queries * count,
        )(*inverses, *peers, *[highs[s] for s in chosen], *[lows[s] for s in chosen], train_grads)
        pieces += [kept, swapped(outgoing, "mp", 1)]
        order += chosen
    total = call(
        functools.partial(total_kernel, order),
        shape((half_rows, cycle * queries), bf16),
        [VMEM] * len(pieces),
        vmem=16,
        flops=half_rows * cycle * queries,
        moved=6 * half_rows * cycle * queries,
    )(*pieces)
    return total.reshape(half_rows, cycle, 1, queries)


def doc_matrix(lengths_row, count):
    ends = jnp.cumsum(lengths_row)
    starts = ends - lengths_row
    place = jnp.arange(count, dtype=jnp.int32)
    inside = (place[None, :] >= starts[:, None]) & (place[None, :] < ends[:, None])
    return inside.astype(jnp.bfloat16)


def solve_block(factor, rhs):
    return jax.scipy.linalg.cho_solve((factor, True), rhs)


def general(query_ids, query_delta, doc_lengths, vocab_factor, output_factor, train_grads):
    model_count = lax.axis_size("mp")
    model_index = lax.axis_index("mp")
    vocab_rows = vocab_factor.shape[0]
    local_ids = query_ids - model_index * vocab_rows
    owned = (local_ids >= 0) & (local_ids < vocab_rows)
    looked = vocab_factor[jnp.clip(local_ids, 0, vocab_rows - 1)].astype(jnp.float32)
    vocab_part = jnp.where(owned[:, None], looked, jnp.zeros_like(looked))
    output_part = jnp.dot(query_delta, output_factor, preferred_element_type=jnp.float32)
    input_side, output_side = lax.psum((vocab_part, output_part), "mp")
    proj = output_side.shape[1]
    rows_each = proj // model_count
    mine = lax.dynamic_slice_in_dim(output_side, model_index * rows_each, rows_each, 1)
    token_count = query_ids.shape[0]
    token_grads = (
        (mine[:, :, None] * input_side[:, None, :])
        .reshape(token_count, rows_each * proj)
        .astype(jnp.bfloat16)
    )
    query_grads = jnp.dot(
        doc_matrix(doc_lengths[0], token_count), token_grads, preferred_element_type=jnp.float32
    )
    train_rows, feat_dev = train_grads.shape
    nblocks = feat_dev // FBLK
    tiled = train_grads.reshape(train_rows, nblocks, FBLK)
    local_gram = jnp.einsum("tbi,tbj->bij", tiled, tiled, preferred_element_type=jnp.float32)
    total_gram = lax.psum(local_gram, "dp")
    fisher = total_gram / (train_rows * lax.axis_size("dp"))
    shift_amount = damping * (jnp.trace(fisher, axis1=1, axis2=2) / FBLK)
    damped = fisher + shift_amount[:, None, None] * jnp.eye(FBLK, dtype=jnp.float32)[None]
    factor = jnp.linalg.cholesky(damped)
    queries = query_grads.shape[0]
    rhs = jnp.transpose(query_grads.reshape(queries, nblocks, FBLK), (1, 2, 0))
    solved = jax.vmap(solve_block)(factor, rhs)
    pre = (jnp.transpose(solved, (2, 0, 1)).reshape(queries, feat_dev) / proj).astype(jnp.bfloat16)
    cycle = lax.axis_size("dp")
    everyone = lax.all_gather(pre, "dp", axis=0, tiled=True)
    scores = lax.dot_general(
        train_grads, everyone, (((1,), (1,)), ((), ())), preferred_element_type=jnp.float32
    )
    scores = scores.astype(jnp.bfloat16).reshape(train_rows, cycle, queries)
    summed = lax.psum_scatter(scores, "mp", scatter_dimension=0, tiled=True)
    return summed[:, :, None, :]


def per_device(query_ids, query_delta, doc_lengths, vocab_factor, output_factor, train_grads):
    owners = lax.axis_size("dp") * lax.axis_size("rep")
    fits = (
        train_grads.shape[1] == 2 * FBLK * owners
        and lax.axis_size("dp") == 4
        and lax.axis_size("mp") == 2
        and lax.axis_size("rep") == 2
        and doc_lengths.shape[1] == FBLK
        and vocab_factor.shape[0] % FBLK == 0
    )
    body = split_over_blocks if fits else general
    return body(query_ids, query_delta, doc_lengths, vocab_factor, output_factor, train_grads)


def solution(mesh):
    placed = (
        P(("groups", "dp", "rep")),
        P(("groups", "dp", "rep"), "mp"),
        P(("groups", "dp", "rep"), None),
        P("mp", None),
        P("mp", None),
        P(("groups", "dp"), "mp"),
    )
    return jax.shard_map(
        per_device,
        mesh=mesh,
        in_specs=placed,
        out_specs=P(("groups", "dp", "mp"), None, "rep", None),
        check_vma=False,
    )
```

```python
import functools
import jax
import jax.numpy as jnp
from jax import lax
from jax.experimental import pallas as pl
from jax.experimental.pallas import tpu as pltpu
from jax.sharding import PartitionSpec as P

FBLK = 128
SLAB = FBLK + 8
PANEL = 8
ROWS = 16

damping = 0.1

VMEM = pl.BlockSpec(memory_space=pltpu.VMEM)
SMEM = pl.BlockSpec(memory_space=pltpu.SMEM)
HBM = pl.BlockSpec(memory_space=pl.ANY)


def call(kernel, outs, in_specs, scratch=(), vmem=48, flops=0, moved=0):
    return pl.pallas_call(
        kernel,
        out_shape=outs,
        in_specs=in_specs,
        scratch_shapes=list(scratch),
        compiler_params=pltpu.CompilerParams(vmem_limit_bytes=vmem << 20),
        cost_estimate=pl.CostEstimate(flops=flops, bytes_accessed=moved, transcendentals=0),
    )


def swapped(shard, axis, by):
    return lax.ppermute(shard, axis, [(i, i ^ by) for i in range(lax.axis_size(axis))])


def square(dim):
    return lax.broadcasted_iota(jnp.int32, (FBLK, FBLK), dim)


def halves(value):
    high = value.astype(jnp.bfloat16)
    return high, (value - high.astype(jnp.float32)).astype(jnp.bfloat16)


def pack(first, second, spare=None):
    row, col = square(0), square(1)
    body = jnp.where(row >= col, first, second)
    diagonal = jnp.sum(jnp.where(row == col, second, 0.0), axis=0, keepdims=True)
    place = lax.broadcasted_iota(jnp.int32, (8, FBLK), 0)
    tail = jnp.where(place == 0, diagonal, 0.0)
    if spare is not None:
        tail = jnp.where(place == 1, spare, tail)
    return body, tail


def unpack(body, diagonal):
    row, col = square(0), square(1)
    turned = body.T
    first = jnp.where(row >= col, body, turned)
    second = jnp.where(row < col, body, jnp.where(row > col, turned, diagonal))
    return first, second


def grams(lengths, train, slabs):
    cycle = len(slabs)
    mine, half = lax.axis_index("dp"), lax.axis_index("rep")
    spare = lengths[...].astype(jnp.float32)
    for shift, slab in enumerate(slabs):
        owner = half * cycle + (mine ^ shift)
        start = pl.multiple_of(owner * (2 * FBLK), 2 * FBLK)
        part = train[:, pl.ds(start, 2 * FBLK)]
        gram = lax.dot_general(part, part, (((0,), (0,)), ((), ())), preferred_element_type=jnp.float32)
        body, tail = pack(gram[:FBLK, :FBLK], gram[FBLK:, FBLK:], spare)
        slab[pl.ds(0, FBLK), :] = body
        slab[pl.ds(FBLK, 8), :] = tail


def thirds(value):
    high = value.astype(jnp.bfloat16)
    rest = value - high.astype(jnp.float32)
    middle = rest.astype(jnp.bfloat16)
    return high, middle, (rest - middle.astype(jnp.float32)).astype(jnp.bfloat16)


def at_rows(panel, first):
    pair = 2 * PANEL
    blank = jnp.zeros((PANEL, FBLK), jnp.float32)
    panel = panel.astype(jnp.float32)
    piece = jnp.concatenate([panel, blank] if first % pair == 0 else [blank, panel], axis=0).astype(jnp.bfloat16)
    before = first // pair * pair
    pieces = [jnp.zeros((before, FBLK), jnp.bfloat16), piece, jnp.zeros((FBLK - before - pair, FBLK), jnp.bfloat16)]
    return jnp.concatenate([piece for piece in pieces if piece.shape[0]], axis=0)


def product(left, right, first):
    high, middle, low = thirds(left)
    right_high, right_middle, right_low = (at_rows(part, first) for part in thirds(right))
    both = jnp.concatenate([right_high, right_middle], axis=1)
    large = jnp.dot(
        jnp.concatenate([high, middle], axis=1), jnp.concatenate([both, both], axis=0),
        preferred_element_type=jnp.float32,
    )
    small = jnp.dot(
        jnp.concatenate([high, low], axis=1), jnp.concatenate([right_low, right_high], axis=0),
        preferred_element_type=jnp.float32,
    )
    return large[:, :FBLK] + (large[:, FBLK:] + small)


def eliminated(panel, first):
    lane = lax.broadcasted_iota(jnp.int32, (PANEL, FBLK), 1)
    sublane = lax.broadcasted_iota(jnp.int32, (PANEL, FBLK), 0)
    within = (lane >= first) & (lane < first + PANEL)
    count = range(PANEL)

    def across(value, row):
        return jnp.broadcast_to(value[row:row + 1, :], (PANEL, FBLK))

    columns = [jnp.broadcast_to(panel[:, first + j:first + j + 1], (PANEL, FBLK)) for j in count]
    pivots = [[across(columns[j], i) if j >= i else None for j in count] for i in count]
    rest = jnp.where(within, jnp.where(lane == first + sublane, 1.0, 0.0), panel)
    lines = [across(rest, i) for i in count]
    for i in count:
        scale = 1.0 / pivots[i][i]
        scaled = lines[i] * scale
        shares = [pivots[i][j] * scale if j > i else None for j in count]
        for m in range(i + 1, PANEL):
            lines[m] = lines[m] - pivots[i][m] * scaled
            for j in range(m, PANEL):
                pivots[m][j] = pivots[m][j] - shares[m] * pivots[i][j]
        lines[i] = scaled
        pivots[i] = shares
    for i in reversed(count):
        for m in range(i):
            lines[m] = lines[m] - pivots[m][i] * lines[i]
    result = lines[0]
    for i in range(1, PANEL):
        result = jnp.where(sublane == i, lines[i], result)
    return result


def inverted(blocks):
    lane = square(1)
    for first in range(0, FBLK, PANEL):
        within = (lane >= first) & (lane < first + PANEL)
        panels = [eliminated(block[first:first + PANEL, :], first) for block in blocks]
        updates = [product(block, panel, first) for block, panel in zip(blocks, panels)]
        rests = [jnp.where(within, 0.0, block) - update for block, update in zip(blocks, updates)]
        blocks = [
            jnp.concatenate(
                [part for part in (rest[:first], panel, rest[first + PANEL:]) if part.shape[0]], axis=0
            )
            for rest, panel in zip(rests, panels)
        ]
    return blocks


def factor_kernel(examples, scale, *refs):
    slabs, out = refs[:-2], refs[-1]
    body = slabs[0][pl.ds(0, FBLK), :]
    diagonal = slabs[0][pl.ds(FBLK, 1), :]
    for slab in slabs[1:]:
        body = body + slab[pl.ds(0, FBLK), :]
        diagonal = diagonal + slab[pl.ds(FBLK, 1), :]
    same = square(0) == square(1)
    damped = []
    for gram in unpack(body, diagonal):
        fisher = gram / examples
        trace = jnp.sum(jnp.sum(jnp.where(same, fisher, 0.0), axis=0, keepdims=True), axis=1, keepdims=True)
        damped.append(fisher + jnp.where(same, damping * (trace / FBLK), 0.0))
    first, second = inverted(damped)
    body, tail = pack(first * scale, second * scale)
    out[pl.ds(0, FBLK), :] = body
    out[pl.ds(FBLK, 8), :] = tail


def first_kernel(id_rows_hbm, delta_hbm, table_hbm, factor_hbm, lengths_hbm, train_hbm, sent, own, *refs):
    slabs, refs = refs[:-12], refs[-12:]
    id_rows, starts, rolls, start_of, roll_of, delta, table, factor, lengths, train, looked, sems = refs
    model = lax.axis_index("mp")
    proj, vocab_rows = table.shape
    tokens = delta.shape[0]
    each = proj // lax.axis_size("mp")
    groups = tokens // FBLK
    get_ids, get_factor, get_lengths, get_train = (
        pltpu.make_async_copy(source, target, sems.at[0, index])
        for index, (source, target) in enumerate((
            (id_rows_hbm, id_rows), (factor_hbm, factor), (lengths_hbm, lengths), (train_hbm, train),
        ))
    )
    get_table = [
        pltpu.make_async_copy(table_hbm.at[rows], table.at[rows], sems.at[1, index])
        for index in range(proj // ROWS) for rows in (pl.ds(index * ROWS, ROWS),)
    ]

    def get_delta(g):
        rows = pl.ds(pl.multiple_of(g * FBLK, FBLK), FBLK)
        return pltpu.make_async_copy(delta_hbm.at[rows], delta.at[rows], sems.at[2, g])

    for copy in (get_ids, get_lengths, get_train, *get_table, get_factor, *(get_delta(g) for g in range(groups))):
        copy.start()
    get_ids.wait()
    local = id_rows[...] - model * vocab_rows
    owned = (local >= 0) & (local < vocab_rows)
    local = jnp.where(owned, local, 0)
    low = FBLK - 1
    starts[...] = local & ~low
    rolls[...] = (lax.broadcasted_iota(jnp.int32, local.shape, 1) - local) & low
    fetches = [pltpu.make_async_copy(starts, start_of, sems.at[0, 4]), pltpu.make_async_copy(rolls, roll_of, sems.at[0, 5])]
    for fetch in fetches:
        fetch.start()
    get_lengths.wait()
    get_train.wait()
    grams(lengths, train, slabs)
    for fetch in fetches:
        fetch.wait()
    starts[...] = owned.astype(jnp.int32)
    for copy in get_table:
        copy.wait()
    get_factor.wait()
    lanes = lax.broadcasted_iota(jnp.int32, (ROWS, FBLK), 1)

    def group(g, carry):
        columns = pl.ds(pl.multiple_of(g * FBLK, FBLK), FBLK)
        get_delta(g).wait()
        output = lax.dot_general(
            delta[columns, :], factor[...], (((1,), (1,)), ((), ())), preferred_element_type=jnp.float32
        )
        looked[:, columns] = output.T
        gathered = [jnp.zeros((ROWS, FBLK), jnp.bfloat16) for _ in range(proj // ROWS)]
        for j in range(FBLK):
            start, by, here = pl.multiple_of(start_of[g, j], FBLK), roll_of[g, j], lanes == j
            for index in range(proj // ROWS):
                block = table[pl.ds(index * ROWS, ROWS), pl.ds(start, FBLK)]
                gathered[index] = jnp.where(here, pltpu.roll(block, by, 1), gathered[index])
        held = starts[pl.ds(g, 1), :].astype(jnp.float32)
        for index, value in enumerate(gathered):
            value = (value.astype(jnp.float32) * held).astype(jnp.bfloat16)
            rows = pl.ds(2 * each + index * ROWS, ROWS)
            sent[rows, columns] = value
            own[rows, columns] = value
        return carry

    lax.fori_loop(0, groups, group, 0)
    mine = looked[pl.ds(pl.multiple_of(model * each, each), each), :]
    other = looked[pl.ds(pl.multiple_of((1 - model) * each, each), each), :]
    for target, value in ((own, mine), (sent, other)):
        high, rest = halves(value)
        target[pl.ds(0, each), :] = high
        target[pl.ds(each, each), :] = rest


def merge_kernel(each, own, got, out):
    def value(ref):
        return ref[pl.ds(0, each), :].astype(jnp.float32) + ref[pl.ds(each, each), :].astype(jnp.float32)

    high, low = halves(value(own) + value(got))
    out[pl.ds(0, each), :] = high
    out[pl.ds(each, each), :] = low
    rows = pl.ds(2 * each, out.shape[0] - 2 * each)
    out[rows, :] = own[rows, :] + got[rows, :]


def queries_kernel(each, ends_of, factors, slab, *refs):
    far, refs = (refs[0], refs[1:]) if ends_of else (None, refs)
    high_out, low_out = refs[-2:]
    if len(refs) == 4:
        source, high_out, low_out, copy = refs
        copy[...] = source[...]
    tokens = factors.shape[1]
    proj = factors.shape[0] - 2 * each
    queries = high_out.shape[1]
    mine = lax.axis_index("dp")

    def part(first, count):
        value = factors[pl.ds(first, count), :].astype(jnp.float32)
        if ends_of:
            at_end = (mine == 0) | (mine == ends_of - 1)
            value = jnp.where(at_end, far[pl.ds(first, count), :].astype(jnp.float32), value)
        return value

    lengths = slab[pl.ds(FBLK + 1, 1), :]
    upto = jnp.where(square(0) <= square(1), 1.0, 0.0).astype(jnp.bfloat16)
    ends = lax.dot_general(
        jnp.broadcast_to(lengths, (8, queries)).astype(jnp.bfloat16), upto, (((1,), (0,)), ((), ())),
        preferred_element_type=jnp.float32,
    )[:1]
    starts = ends - lengths
    place = lax.broadcasted_iota(jnp.int32, (tokens, queries), 0).astype(jnp.float32)
    inside = jnp.where((place >= starts) & (place < ends), 1.0, 0.0).astype(jnp.bfloat16)
    output = part(0, each) + part(each, each)
    inputs = part(2 * each, proj)
    step = 8
    for start in range(0, each, step):
        grads = jnp.concatenate(
            [(inputs * output[r:r + 1, :]).astype(jnp.bfloat16) for r in range(start, start + step)], axis=0
        )
        summed = jnp.dot(grads, inside, preferred_element_type=jnp.float32)
        high, low = halves(summed)
        high_out[pl.ds(start * proj, step * proj), :] = high
        low_out[pl.ds(start * proj, step * proj), :] = low


def hand_kernel(slab, *refs):
    refs[-1][...] = slab[...]


def scores_kernel(cycle, count, *refs):
    own, peers = refs[:cycle], refs[cycle:2 * cycle]
    highs, lows = refs[2 * cycle:2 * cycle + count], refs[2 * cycle + count:2 * cycle + 2 * count]
    train, sent, kept, pre = refs[2 * cycle + 2 * count:]
    mine, rep, model = lax.axis_index("dp"), lax.axis_index("rep"), lax.axis_index("mp")
    for half, slabs in ((rep, own), (1 - rep, peers)):
        for shift in range(cycle):
            owner = half * cycle + (mine ^ shift)
            slab = slabs[shift]
            blocks = unpack(slab[pl.ds(0, FBLK), :], slab[pl.ds(FBLK, 1), :])
            for index, block in enumerate(blocks):
                rows = pl.ds(pl.multiple_of(owner * (2 * FBLK) + index * FBLK, FBLK), FBLK)
                high, low = halves(block)
                right_high = jnp.concatenate([ref[rows, :] for ref in highs], axis=1)
                right_low = jnp.concatenate([ref[rows, :] for ref in lows], axis=1)
                solved = jnp.dot(
                    jnp.concatenate([high, high, low], axis=1),
                    jnp.concatenate([right_high, right_low, right_high], axis=0),
                    preferred_element_type=jnp.float32,
                )
                pre[rows, :] = solved.astype(jnp.bfloat16)
    half_rows = sent.shape[0]
    for out, which in ((sent, 1 - model), (kept, model)):
        rows = pl.ds(pl.multiple_of(which * half_rows, half_rows), half_rows)
        out[...] = jnp.dot(train[rows, :], pre[...], preferred_element_type=jnp.float32).astype(jnp.bfloat16)


def total_kernel(order, *refs):
    pieces, out = refs[:-1], refs[-1]
    mine, cycle = lax.axis_index("dp"), len(order)
    sums = {}
    for kept, got in zip(pieces[::2], pieces[1::2]):
        both = kept[...].astype(jnp.float32) + got[...].astype(jnp.float32)
        for index in range(both.shape[1] // FBLK):
            sums[order[len(sums)]] = both[:, index * FBLK:(index + 1) * FBLK]
    placed = []
    for source in range(cycle):
        shift = mine ^ source
        value = sums[0]
        for index in range(1, cycle):
            value = jnp.where(shift == index, sums[index], value)
        placed.append(value)
    out[...] = jnp.concatenate(placed, axis=1).astype(jnp.bfloat16)


def shape(dims, dtype):
    return jax.ShapeDtypeStruct(dims, dtype)


def split_over_blocks(query_ids, query_delta, doc_lengths, vocab_factor, output_factor, train_grads):
    cycle = lax.axis_size("dp")
    tokens, width = query_delta.shape
    proj = output_factor.shape[1]
    each = proj // lax.axis_size("mp")
    vocab_rows = vocab_factor.shape[0]
    train_rows, feat = train_grads.shape
    queries = doc_lengths.shape[1]
    bf16, f32 = jnp.bfloat16, jnp.float32

    sent, own, *slabs = call(
        first_kernel,
        [shape((2 * each + proj, tokens), bf16)] * 2 + [shape((SLAB, FBLK), f32)] * cycle,
        [HBM] * 6,
        [
            pltpu.VMEM((tokens // FBLK, FBLK), jnp.int32),
            pltpu.VMEM((tokens // FBLK, FBLK), jnp.int32),
            pltpu.VMEM((tokens // FBLK, FBLK), jnp.int32),
            pltpu.SMEM((tokens // FBLK, FBLK), jnp.int32),
            pltpu.SMEM((tokens // FBLK, FBLK), jnp.int32),
            pltpu.VMEM((tokens, width), bf16),
            pltpu.VMEM((proj, vocab_rows), bf16),
            pltpu.VMEM((proj, width), bf16),
            pltpu.VMEM((1, queries), jnp.int32),
            pltpu.VMEM((train_rows, feat), bf16),
            pltpu.VMEM((proj, tokens), f32),
            pltpu.SemaphoreType.DMA((3, 8)),
        ],
        vmem=62,
        flops=2 * tokens * width * proj,
        moved=2 * (tokens * width + proj * vocab_rows) * 2,
    )(
        query_ids.reshape(tokens // FBLK, FBLK), query_delta, vocab_factor.T, output_factor.T,
        doc_lengths, train_grads,
    )
    got = swapped(sent, "mp", 1)
    parts = [slabs[0]] + [swapped(slabs[s], "dp", s) for s in range(1, cycle)]

    factors = call(
        functools.partial(merge_kernel, each),
        shape(sent.shape, bf16),
        [VMEM, VMEM],
        vmem=16,
        flops=tokens * each,
        moved=8 * tokens * each * 4,
    )(own, got)
    late = cycle - 1
    gathered = [factors] + [swapped(factors, "dp", s) if s != late else None for s in range(1, cycle)]

    inverse = call(
        functools.partial(factor_kernel, train_rows * cycle, 1.0 / proj),
        shape((SLAB, FBLK), f32),
        [VMEM] * cycle + [HBM],
        vmem=16,
        flops=10 ** 10,
        moved=10 ** 6,
    )(*parts, factors)
    inverses = [inverse] + [swapped(inverse, "dp", s) for s in range(1, cycle)]
    copies = {0: [inverse], 1: [factors], 2: [gathered[2]]}
    highs, lows, far = {}, {}, []
    for s in range(cycle):
        extra = copies.get(s, far)
        copied = s in (1, 2)
        highs[s], lows[s], *again = call(
            functools.partial(queries_kernel, each, cycle if s == late else 0),
            [shape((feat, queries), bf16)] * 2 + [shape(factors.shape, bf16)] * copied,
            [VMEM, VMEM] + [HBM if s == 0 else VMEM] * len(extra),
            vmem=24,
            flops=2 * feat * tokens * queries,
            moved=6 * feat * queries,
        )(gathered[s], parts[s], *extra)
        if s == 1:
            gathered[late] = lax.ppermute(again[0], "dp", [(1, 2), (2, 1)])
        if s == 2:
            far = [lax.ppermute(again[0], "dp", [(1, 0), (2, 3)])]
    handed = list(inverses)
    handed[late] = call(
        hand_kernel,
        shape((SLAB, FBLK), f32),
        [VMEM] + [HBM] * (cycle - 1),
        vmem=16,
        moved=8 * SLAB * FBLK,
    )(inverses[late], *[highs[s] for s in range(cycle) if s != late])
    peers = [swapped(slab, "rep", 1) for slab in handed]

    half_rows = train_rows // lax.axis_size("mp")
    pieces, order = [], []
    for chosen in ([s for s in range(cycle) if s != late], [late]):
        count = len(chosen)
        outgoing, kept = call(
            functools.partial(scores_kernel, cycle, count),
            [shape((half_rows, count * queries), bf16)] * 2,
            [VMEM] * (2 * cycle + 2 * count + 1),
            [pltpu.VMEM((feat, count * queries), bf16)],
            vmem=24,
            flops=2 * train_rows * feat * count * queries,
            moved=8 * feat * queries * count,
        )(*inverses, *peers, *[highs[s] for s in chosen], *[lows[s] for s in chosen], train_grads)
        pieces += [kept, swapped(outgoing, "mp", 1)]
        order += chosen
    total = call(
        functools.partial(total_kernel, order),
        shape((half_rows, cycle * queries), bf16),
        [VMEM] * len(pieces),
        vmem=16,
        flops=half_rows * cycle * queries,
        moved=6 * half_rows * cycle * queries,
    )(*pieces)
    return total.reshape(half_rows, cycle, 1, queries)


def doc_matrix(lengths_row, count):
    ends = jnp.cumsum(lengths_row)
    starts = ends - lengths_row
    place = jnp.arange(count, dtype=jnp.int32)
    inside = (place[None, :] >= starts[:, None]) & (place[None, :] < ends[:, None])
    return inside.astype(jnp.bfloat16)


def solve_block(factor, rhs):
    return jax.scipy.linalg.cho_solve((factor, True), rhs)


def general(query_ids, query_delta, doc_lengths, vocab_factor, output_factor, train_grads):
    model_count = lax.axis_size("mp")
    model_index = lax.axis_index("mp")
    vocab_rows = vocab_factor.shape[0]
    local_ids = query_ids - model_index * vocab_rows
    owned = (local_ids >= 0) & (local_ids < vocab_rows)
    looked = vocab_factor[jnp.clip(local_ids, 0, vocab_rows - 1)].astype(jnp.float32)
    vocab_part = jnp.where(owned[:, None], looked, jnp.zeros_like(looked))
    output_part = jnp.dot(query_delta, output_factor, preferred_element_type=jnp.float32)
    input_side, output_side = lax.psum((vocab_part, output_part), "mp")
    proj = output_side.shape[1]
    rows_each = proj // model_count
    mine = lax.dynamic_slice_in_dim(output_side, model_index * rows_each, rows_each, 1)
    token_count = query_ids.shape[0]
    token_grads = (
        (mine[:, :, None] * input_side[:, None, :])
        .reshape(token_count, rows_each * proj)
        .astype(jnp.bfloat16)
    )
    query_grads = jnp.dot(
        doc_matrix(doc_lengths[0], token_count), token_grads, preferred_element_type=jnp.float32
    )
    train_rows, feat_dev = train_grads.shape
    nblocks = feat_dev // FBLK
    tiled = train_grads.reshape(train_rows, nblocks, FBLK)
    local_gram = jnp.einsum("tbi,tbj->bij", tiled, tiled, preferred_element_type=jnp.float32)
    total_gram = lax.psum(local_gram, "dp")
    fisher = total_gram / (train_rows * lax.axis_size("dp"))
    shift_amount = damping * (jnp.trace(fisher, axis1=1, axis2=2) / FBLK)
    damped = fisher + shift_amount[:, None, None] * jnp.eye(FBLK, dtype=jnp.float32)[None]
    factor = jnp.linalg.cholesky(damped)
    queries = query_grads.shape[0]
    rhs = jnp.transpose(query_grads.reshape(queries, nblocks, FBLK), (1, 2, 0))
    solved = jax.vmap(solve_block)(factor, rhs)
    pre = (jnp.transpose(solved, (2, 0, 1)).reshape(queries, feat_dev) / proj).astype(jnp.bfloat16)
    cycle = lax.axis_size("dp")
    everyone = lax.all_gather(pre, "dp", axis=0, tiled=True)
    scores = lax.dot_general(
        train_grads, everyone, (((1,), (1,)), ((), ())), preferred_element_type=jnp.float32
    )
    scores = scores.astype(jnp.bfloat16).reshape(train_rows, cycle, queries)
    summed = lax.psum_scatter(scores, "mp", scatter_dimension=0, tiled=True)
    return summed[:, :, None, :]


def per_device(query_ids, query_delta, doc_lengths, vocab_factor, output_factor, train_grads):
    owners = lax.axis_size("dp") * lax.axis_size("rep")
    fits = (
        train_grads.shape[1] == 2 * FBLK * owners
        and lax.axis_size("dp") == 4
        and lax.axis_size("mp") == 2
        and lax.axis_size("rep") == 2
        and doc_lengths.shape[1] == FBLK
        and vocab_factor.shape[0] % FBLK == 0
    )
    body = split_over_blocks if fits else general
    return body(query_ids, query_delta, doc_lengths, vocab_factor, output_factor, train_grads)


def solution(mesh):
    placed = (
        P(("groups", "dp", "rep")),
        P(("groups", "dp", "rep"), "mp"),
        P(("groups", "dp", "rep"), None),
        P("mp", None),
        P("mp", None),
        P(("groups", "dp"), "mp"),
    )
    return jax.shard_map(
        per_device,
        mesh=mesh,
        in_specs=placed,
        out_specs=P(("groups", "dp", "mp"), None, "rep", None),
        check_vma=False,
    )
```

```python
import functools
import jax
import jax.numpy as jnp
from jax import lax
from jax.experimental import pallas as pl
from jax.experimental.pallas import tpu as pltpu
from jax.sharding import PartitionSpec as P

FBLK = 128
SLAB = FBLK + 8
PANEL = 8
ROWS = 16

damping = 0.1

VMEM = pl.BlockSpec(memory_space=pltpu.VMEM)
SMEM = pl.BlockSpec(memory_space=pltpu.SMEM)
HBM = pl.BlockSpec(memory_space=pl.ANY)


def call(kernel, outs, in_specs, scratch=(), vmem=48, flops=0, moved=0):
    return pl.pallas_call(
        kernel,
        out_shape=outs,
        in_specs=in_specs,
        scratch_shapes=list(scratch),
        compiler_params=pltpu.CompilerParams(vmem_limit_bytes=vmem << 20),
        cost_estimate=pl.CostEstimate(flops=flops, bytes_accessed=moved, transcendentals=0),
    )


def swapped(shard, axis, by):
    return lax.ppermute(shard, axis, [(i, i ^ by) for i in range(lax.axis_size(axis))])


def square(dim):
    return lax.broadcasted_iota(jnp.int32, (FBLK, FBLK), dim)


def halves(value):
    high = value.astype(jnp.bfloat16)
    return high, (value - high.astype(jnp.float32)).astype(jnp.bfloat16)


def pack(first, second, spare=None):
    row, col = square(0), square(1)
    body = jnp.where(row >= col, first, second)
    diagonal = jnp.sum(jnp.where(row == col, second, 0.0), axis=0, keepdims=True)
    place = lax.broadcasted_iota(jnp.int32, (8, FBLK), 0)
    tail = jnp.where(place == 0, diagonal, 0.0)
    if spare is not None:
        tail = jnp.where(place == 1, spare, tail)
    return body, tail


def unpack(body, diagonal):
    row, col = square(0), square(1)
    turned = body.T
    first = jnp.where(row >= col, body, turned)
    second = jnp.where(row < col, body, jnp.where(row > col, turned, diagonal))
    return first, second


def grams(lengths, train, slabs):
    cycle = len(slabs)
    mine, half = lax.axis_index("dp"), lax.axis_index("rep")
    spare = lengths[...].astype(jnp.float32)
    for shift, slab in enumerate(slabs):
        owner = half * cycle + (mine ^ shift)
        start = pl.multiple_of(owner * (2 * FBLK), 2 * FBLK)
        part = train[:, pl.ds(start, 2 * FBLK)]
        gram = lax.dot_general(part, part, (((0,), (0,)), ((), ())), preferred_element_type=jnp.float32)
        body, tail = pack(gram[:FBLK, :FBLK], gram[FBLK:, FBLK:], spare)
        slab[pl.ds(0, FBLK), :] = body
        slab[pl.ds(FBLK, 8), :] = tail


def thirds(value):
    high = value.astype(jnp.bfloat16)
    rest = value - high.astype(jnp.float32)
    middle = rest.astype(jnp.bfloat16)
    return high, middle, (rest - middle.astype(jnp.float32)).astype(jnp.bfloat16)


def at_rows(panel, first):
    pair = 2 * PANEL
    blank = jnp.zeros((PANEL, FBLK), jnp.float32)
    panel = panel.astype(jnp.float32)
    piece = jnp.concatenate([panel, blank] if first % pair == 0 else [blank, panel], axis=0).astype(jnp.bfloat16)
    before = first // pair * pair
    pieces = [jnp.zeros((before, FBLK), jnp.bfloat16), piece, jnp.zeros((FBLK - before - pair, FBLK), jnp.bfloat16)]
    return jnp.concatenate([piece for piece in pieces if piece.shape[0]], axis=0)


def product(left, right, first):
    high, middle, low = thirds(left)
    right_high, right_middle, right_low = (at_rows(part, first) for part in thirds(right))
    both = jnp.concatenate([right_high, right_middle], axis=1)
    large = jnp.dot(
        jnp.concatenate([high, middle], axis=1), jnp.concatenate([both, both], axis=0),
        preferred_element_type=jnp.float32,
    )
    small = jnp.dot(
        jnp.concatenate([high, low], axis=1), jnp.concatenate([right_low, right_high], axis=0),
        preferred_element_type=jnp.float32,
    )
    return large[:, :FBLK] + (large[:, FBLK:] + small)


def eliminated(panel, first):
    lane = lax.broadcasted_iota(jnp.int32, (PANEL, FBLK), 1)
    sublane = lax.broadcasted_iota(jnp.int32, (PANEL, FBLK), 0)
    within = (lane >= first) & (lane < first + PANEL)
    count = range(PANEL)

    def across(value, row):
        return jnp.broadcast_to(value[row:row + 1, :], (PANEL, FBLK))

    columns = [jnp.broadcast_to(panel[:, first + j:first + j + 1], (PANEL, FBLK)) for j in count]
    pivots = [[across(columns[j], i) if j >= i else None for j in count] for i in count]
    rest = jnp.where(within, jnp.where(lane == first + sublane, 1.0, 0.0), panel)
    lines = [across(rest, i) for i in count]
    for i in count:
        scale = 1.0 / pivots[i][i]
        scaled = lines[i] * scale
        shares = [pivots[i][j] * scale if j > i else None for j in count]
        for m in range(i + 1, PANEL):
            lines[m] = lines[m] - pivots[i][m] * scaled
            for j in range(m, PANEL):
                pivots[m][j] = pivots[m][j] - shares[m] * pivots[i][j]
        lines[i] = scaled
        pivots[i] = shares
    for i in reversed(count):
        for m in range(i):
            lines[m] = lines[m] - pivots[m][i] * lines[i]
    result = lines[0]
    for i in range(1, PANEL):
        result = jnp.where(sublane == i, lines[i], result)
    return result


def inverted(blocks):
    lane = square(1)
    for first in range(0, FBLK, PANEL):
        within = (lane >= first) & (lane < first + PANEL)
        panels = [eliminated(block[first:first + PANEL, :], first) for block in blocks]
        updates = [product(block, panel, first) for block, panel in zip(blocks, panels)]
        rests = [jnp.where(within, 0.0, block) - update for block, update in zip(blocks, updates)]
        blocks = [
            jnp.concatenate(
                [part for part in (rest[:first], panel, rest[first + PANEL:]) if part.shape[0]], axis=0
            )
            for rest, panel in zip(rests, panels)
        ]
    return blocks


def factor_kernel(examples, scale, *refs):
    slabs, out = refs[:-2], refs[-1]
    body = slabs[0][pl.ds(0, FBLK), :]
    diagonal = slabs[0][pl.ds(FBLK, 1), :]
    for slab in slabs[1:]:
        body = body + slab[pl.ds(0, FBLK), :]
        diagonal = diagonal + slab[pl.ds(FBLK, 1), :]
    same = square(0) == square(1)
    damped = []
    for gram in unpack(body, diagonal):
        fisher = gram / examples
        trace = jnp.sum(jnp.sum(jnp.where(same, fisher, 0.0), axis=0, keepdims=True), axis=1, keepdims=True)
        damped.append(fisher + jnp.where(same, damping * (trace / FBLK), 0.0))
    first, second = inverted(damped)
    body, tail = pack(first * scale, second * scale)
    out[pl.ds(0, FBLK), :] = body
    out[pl.ds(FBLK, 8), :] = tail


def first_kernel(id_rows_hbm, delta_hbm, table_hbm, factor_hbm, lengths_hbm, train_hbm, sent, own, *refs):
    slabs, refs = refs[:-12], refs[-12:]
    id_rows, starts, rolls, start_of, roll_of, delta, table, factor, lengths, train, looked, sems = refs
    model = lax.axis_index("mp")
    proj, vocab_rows = table.shape
    tokens = delta.shape[0]
    each = proj // lax.axis_size("mp")
    groups = tokens // FBLK
    get_ids, get_factor, get_lengths, get_train = (
        pltpu.make_async_copy(source, target, sems.at[0, index])
        for index, (source, target) in enumerate((
            (id_rows_hbm, id_rows), (factor_hbm, factor), (lengths_hbm, lengths), (train_hbm, train),
        ))
    )
    get_table = [
        pltpu.make_async_copy(table_hbm.at[rows], table.at[rows], sems.at[1, index])
        for index in range(proj // ROWS) for rows in (pl.ds(index * ROWS, ROWS),)
    ]

    def get_delta(g):
        rows = pl.ds(pl.multiple_of(g * FBLK, FBLK), FBLK)
        return pltpu.make_async_copy(delta_hbm.at[rows], delta.at[rows], sems.at[2, g])

    for copy in (get_ids, get_lengths, get_train, *get_table, get_factor, *(get_delta(g) for g in range(groups))):
        copy.start()
    get_ids.wait()
    local = id_rows[...] - model * vocab_rows
    owned = (local >= 0) & (local < vocab_rows)
    local = jnp.where(owned, local, 0)
    low = FBLK - 1
    starts[...] = local & ~low
    rolls[...] = (lax.broadcasted_iota(jnp.int32, local.shape, 1) - local) & low
    fetches = [pltpu.make_async_copy(starts, start_of, sems.at[0, 4]), pltpu.make_async_copy(rolls, roll_of, sems.at[0, 5])]
    for fetch in fetches:
        fetch.start()
    get_lengths.wait()
    get_train.wait()
    grams(lengths, train, slabs)
    for fetch in fetches:
        fetch.wait()
    starts[...] = owned.astype(jnp.int32)
    for copy in get_table:
        copy.wait()
    get_factor.wait()
    lanes = lax.broadcasted_iota(jnp.int32, (ROWS, FBLK), 1)

    def group(g, carry):
        columns = pl.ds(pl.multiple_of(g * FBLK, FBLK), FBLK)
        get_delta(g).wait()
        output = lax.dot_general(
            delta[columns, :], factor[...], (((1,), (1,)), ((), ())), preferred_element_type=jnp.float32
        )
        looked[:, columns] = output.T
        gathered = [jnp.zeros((ROWS, FBLK), jnp.bfloat16) for _ in range(proj // ROWS)]
        for j in range(FBLK):
            start, by, here = pl.multiple_of(start_of[g, j], FBLK), roll_of[g, j], lanes == j
            for index in range(proj // ROWS):
                block = table[pl.ds(index * ROWS, ROWS), pl.ds(start, FBLK)]
                gathered[index] = jnp.where(here, pltpu.roll(block, by, 1), gathered[index])
        held = starts[pl.ds(g, 1), :].astype(jnp.float32)
        for index, value in enumerate(gathered):
            value = (value.astype(jnp.float32) * held).astype(jnp.bfloat16)
            rows = pl.ds(2 * each + index * ROWS, ROWS)
            sent[rows, columns] = value
            own[rows, columns] = value
        return carry

    lax.fori_loop(0, groups, group, 0)
    mine = looked[pl.ds(pl.multiple_of(model * each, each), each), :]
    other = looked[pl.ds(pl.multiple_of((1 - model) * each, each), each), :]
    for target, value in ((own, mine), (sent, other)):
        high, rest = halves(value)
        target[pl.ds(0, each), :] = high
        target[pl.ds(each, each), :] = rest


def merge_kernel(each, own, got, out):
    def value(ref):
        return ref[pl.ds(0, each), :].astype(jnp.float32) + ref[pl.ds(each, each), :].astype(jnp.float32)

    high, low = halves(value(own) + value(got))
    out[pl.ds(0, each), :] = high
    out[pl.ds(each, each), :] = low
    rows = pl.ds(2 * each, out.shape[0] - 2 * each)
    out[rows, :] = own[rows, :] + got[rows, :]


def queries_kernel(each, ends_of, factors, slab, *refs):
    far, refs = (refs[0], refs[1:]) if ends_of else (None, refs)
    high_out, low_out = refs[-2:]
    if len(refs) == 4:
        source, high_out, low_out, copy = refs
        copy[...] = source[...]
    tokens = factors.shape[1]
    proj = factors.shape[0] - 2 * each
    queries = high_out.shape[1]
    mine = lax.axis_index("dp")

    def part(first, count):
        value = factors[pl.ds(first, count), :].astype(jnp.float32)
        if ends_of:
            at_end = (mine == 0) | (mine == ends_of - 1)
            value = jnp.where(at_end, far[pl.ds(first, count), :].astype(jnp.float32), value)
        return value

    lengths = slab[pl.ds(FBLK + 1, 1), :]
    upto = jnp.where(square(0) <= square(1), 1.0, 0.0).astype(jnp.bfloat16)
    ends = lax.dot_general(
        jnp.broadcast_to(lengths, (8, queries)).astype(jnp.bfloat16), upto, (((1,), (0,)), ((), ())),
        preferred_element_type=jnp.float32,
    )[:1]
    starts = ends - lengths
    place = lax.broadcasted_iota(jnp.int32, (tokens, queries), 0).astype(jnp.float32)
    inside = jnp.where((place >= starts) & (place < ends), 1.0, 0.0).astype(jnp.bfloat16)
    output = part(0, each) + part(each, each)
    inputs = part(2 * each, proj)
    step = 8
    for start in range(0, each, step):
        grads = jnp.concatenate(
            [(inputs * output[r:r + 1, :]).astype(jnp.bfloat16) for r in range(start, start + step)], axis=0
        )
        summed = jnp.dot(grads, inside, preferred_element_type=jnp.float32)
        high, low = halves(summed)
        high_out[pl.ds(start * proj, step * proj), :] = high
        low_out[pl.ds(start * proj, step * proj), :] = low


def hand_kernel(count, *refs):
    for source, copy in zip(refs[:count], refs[-count:]):
        copy[...] = source[...]


def scores_kernel(cycle, count, *refs):
    own, peers = refs[:cycle], refs[cycle:2 * cycle]
    highs, lows = refs[2 * cycle:2 * cycle + count], refs[2 * cycle + count:2 * cycle + 2 * count]
    train, sent, kept, pre = refs[2 * cycle + 2 * count:]
    mine, rep, model = lax.axis_index("dp"), lax.axis_index("rep"), lax.axis_index("mp")
    for half, slabs in ((rep, own), (1 - rep, peers)):
        for shift in range(cycle):
            owner = half * cycle + (mine ^ shift)
            slab = slabs[shift]
            blocks = unpack(slab[pl.ds(0, FBLK), :], slab[pl.ds(FBLK, 1), :])
            for index, block in enumerate(blocks):
                rows = pl.ds(pl.multiple_of(owner * (2 * FBLK) + index * FBLK, FBLK), FBLK)
                high, low = halves(block)
                right_high = jnp.concatenate([ref[rows, :] for ref in highs], axis=1)
                right_low = jnp.concatenate([ref[rows, :] for ref in lows], axis=1)
                solved = jnp.dot(
                    jnp.concatenate([high, high, low], axis=1),
                    jnp.concatenate([right_high, right_low, right_high], axis=0),
                    preferred_element_type=jnp.float32,
                )
                pre[rows, :] = solved.astype(jnp.bfloat16)
    half_rows = sent.shape[0]
    for out, which in ((sent, 1 - model), (kept, model)):
        rows = pl.ds(pl.multiple_of(which * half_rows, half_rows), half_rows)
        out[...] = jnp.dot(train[rows, :], pre[...], preferred_element_type=jnp.float32).astype(jnp.bfloat16)


def total_kernel(order, *refs):
    pieces, out = refs[:-1], refs[-1]
    mine, cycle = lax.axis_index("dp"), len(order)
    sums = {}
    for kept, got in zip(pieces[::2], pieces[1::2]):
        both = kept[...].astype(jnp.float32) + got[...].astype(jnp.float32)
        for index in range(both.shape[1] // FBLK):
            sums[order[len(sums)]] = both[:, index * FBLK:(index + 1) * FBLK]
    placed = []
    for source in range(cycle):
        shift = mine ^ source
        value = sums[0]
        for index in range(1, cycle):
            value = jnp.where(shift == index, sums[index], value)
        placed.append(value)
    out[...] = jnp.concatenate(placed, axis=1).astype(jnp.bfloat16)


def shape(dims, dtype):
    return jax.ShapeDtypeStruct(dims, dtype)


def split_over_blocks(query_ids, query_delta, doc_lengths, vocab_factor, output_factor, train_grads):
    cycle = lax.axis_size("dp")
    tokens, width = query_delta.shape
    proj = output_factor.shape[1]
    each = proj // lax.axis_size("mp")
    vocab_rows = vocab_factor.shape[0]
    train_rows, feat = train_grads.shape
    queries = doc_lengths.shape[1]
    bf16, f32 = jnp.bfloat16, jnp.float32

    sent, own, *slabs = call(
        first_kernel,
        [shape((2 * each + proj, tokens), bf16)] * 2 + [shape((SLAB, FBLK), f32)] * cycle,
        [HBM] * 6,
        [
            pltpu.VMEM((tokens // FBLK, FBLK), jnp.int32),
            pltpu.VMEM((tokens // FBLK, FBLK), jnp.int32),
            pltpu.VMEM((tokens // FBLK, FBLK), jnp.int32),
            pltpu.SMEM((tokens // FBLK, FBLK), jnp.int32),
            pltpu.SMEM((tokens // FBLK, FBLK), jnp.int32),
            pltpu.VMEM((tokens, width), bf16),
            pltpu.VMEM((proj, vocab_rows), bf16),
            pltpu.VMEM((proj, width), bf16),
            pltpu.VMEM((1, queries), jnp.int32),
            pltpu.VMEM((train_rows, feat), bf16),
            pltpu.VMEM((proj, tokens), f32),
            pltpu.SemaphoreType.DMA((3, 8)),
        ],
        vmem=62,
        flops=2 * tokens * width * proj,
        moved=2 * (tokens * width + proj * vocab_rows) * 2,
    )(
        query_ids.reshape(tokens // FBLK, FBLK), query_delta, vocab_factor.T, output_factor.T,
        doc_lengths, train_grads,
    )
    got = swapped(sent, "mp", 1)
    own, kept = call(
        functools.partial(hand_kernel, 2),
        [shape(own.shape, bf16), shape((SLAB, FBLK), f32)],
        [VMEM, VMEM],
        vmem=16,
        moved=4 * own.size,
    )(own, slabs[0])
    parts = [kept] + [swapped(slabs[s], "dp", s) for s in range(1, cycle)]

    factors = call(
        functools.partial(merge_kernel, each),
        shape(sent.shape, bf16),
        [VMEM, VMEM],
        vmem=16,
        flops=tokens * each,
        moved=8 * tokens * each * 4,
    )(own, got)
    late = cycle - 1
    gathered = [factors] + [swapped(factors, "dp", s) if s != late else None for s in range(1, cycle)]

    inverse = call(
        functools.partial(factor_kernel, train_rows * cycle, 1.0 / proj),
        shape((SLAB, FBLK), f32),
        [VMEM] * cycle + [HBM],
        vmem=16,
        flops=10 ** 10,
        moved=10 ** 6,
    )(*parts, factors)
    inverses = [inverse] + [swapped(inverse, "dp", s) for s in range(1, cycle)]
    copies = {0: [inverse], 1: [factors], 2: [gathered[2]]}
    highs, lows, far = {}, {}, []
    for s in range(cycle):
        extra = copies.get(s, far)
        copied = s in (1, 2)
        highs[s], lows[s], *again = call(
            functools.partial(queries_kernel, each, cycle if s == late else 0),
            [shape((feat, queries), bf16)] * 2 + [shape(factors.shape, bf16)] * copied,
            [VMEM, VMEM] + [HBM if s == 0 else VMEM] * len(extra),
            vmem=24,
            flops=2 * feat * tokens * queries,
            moved=6 * feat * queries,
        )(gathered[s], parts[s], *extra)
        if s == 1:
            gathered[late] = lax.ppermute(again[0], "dp", [(1, 2), (2, 1)])
        if s == 2:
            far = [lax.ppermute(again[0], "dp", [(1, 0), (2, 3)])]
    handed = list(inverses)
    handed[late] = call(
        functools.partial(hand_kernel, 1),
        shape((SLAB, FBLK), f32),
        [VMEM] + [HBM] * (cycle - 2),
        vmem=16,
        moved=8 * SLAB * FBLK,
    )(inverses[late], *[highs[s] for s in range(1, cycle) if s != late])
    peers = [swapped(slab, "rep", 1) for slab in handed]

    half_rows = train_rows // lax.axis_size("mp")
    pieces, order = [], []
    for chosen in ([s for s in range(cycle) if s != late], [late]):
        count = len(chosen)
        outgoing, kept = call(
            functools.partial(scores_kernel, cycle, count),
            [shape((half_rows, count * queries), bf16)] * 2,
            [VMEM] * (2 * cycle + 2 * count + 1),
            [pltpu.VMEM((feat, count * queries), bf16)],
            vmem=24,
            flops=2 * train_rows * feat * count * queries,
            moved=8 * feat * queries * count,
        )(*inverses, *peers, *[highs[s] for s in chosen], *[lows[s] for s in chosen], train_grads)
        pieces += [kept, swapped(outgoing, "mp", 1)]
        order += chosen
    total = call(
        functools.partial(total_kernel, order),
        shape((half_rows, cycle * queries), bf16),
        [VMEM] * len(pieces),
        vmem=16,
        flops=half_rows * cycle * queries,
        moved=6 * half_rows * cycle * queries,
    )(*pieces)
    return total.reshape(half_rows, cycle, 1, queries)


def doc_matrix(lengths_row, count):
    ends = jnp.cumsum(lengths_row)
    starts = ends - lengths_row
    place = jnp.arange(count, dtype=jnp.int32)
    inside = (place[None, :] >= starts[:, None]) & (place[None, :] < ends[:, None])
    return inside.astype(jnp.bfloat16)


def solve_block(factor, rhs):
    return jax.scipy.linalg.cho_solve((factor, True), rhs)


def general(query_ids, query_delta, doc_lengths, vocab_factor, output_factor, train_grads):
    model_count = lax.axis_size("mp")
    model_index = lax.axis_index("mp")
    vocab_rows = vocab_factor.shape[0]
    local_ids = query_ids - model_index * vocab_rows
    owned = (local_ids >= 0) & (local_ids < vocab_rows)
    looked = vocab_factor[jnp.clip(local_ids, 0, vocab_rows - 1)].astype(jnp.float32)
    vocab_part = jnp.where(owned[:, None], looked, jnp.zeros_like(looked))
    output_part = jnp.dot(query_delta, output_factor, preferred_element_type=jnp.float32)
    input_side, output_side = lax.psum((vocab_part, output_part), "mp")
    proj = output_side.shape[1]
    rows_each = proj // model_count
    mine = lax.dynamic_slice_in_dim(output_side, model_index * rows_each, rows_each, 1)
    token_count = query_ids.shape[0]
    token_grads = (
        (mine[:, :, None] * input_side[:, None, :])
        .reshape(token_count, rows_each * proj)
        .astype(jnp.bfloat16)
    )
    query_grads = jnp.dot(
        doc_matrix(doc_lengths[0], token_count), token_grads, preferred_element_type=jnp.float32
    )
    train_rows, feat_dev = train_grads.shape
    nblocks = feat_dev // FBLK
    tiled = train_grads.reshape(train_rows, nblocks, FBLK)
    local_gram = jnp.einsum("tbi,tbj->bij", tiled, tiled, preferred_element_type=jnp.float32)
    total_gram = lax.psum(local_gram, "dp")
    fisher = total_gram / (train_rows * lax.axis_size("dp"))
    shift_amount = damping * (jnp.trace(fisher, axis1=1, axis2=2) / FBLK)
    damped = fisher + shift_amount[:, None, None] * jnp.eye(FBLK, dtype=jnp.float32)[None]
    factor = jnp.linalg.cholesky(damped)
    queries = query_grads.shape[0]
    rhs = jnp.transpose(query_grads.reshape(queries, nblocks, FBLK), (1, 2, 0))
    solved = jax.vmap(solve_block)(factor, rhs)
    pre = (jnp.transpose(solved, (2, 0, 1)).reshape(queries, feat_dev) / proj).astype(jnp.bfloat16)
    cycle = lax.axis_size("dp")
    everyone = lax.all_gather(pre, "dp", axis=0, tiled=True)
    scores = lax.dot_general(
        train_grads, everyone, (((1,), (1,)), ((), ())), preferred_element_type=jnp.float32
    )
    scores = scores.astype(jnp.bfloat16).reshape(train_rows, cycle, queries)
    summed = lax.psum_scatter(scores, "mp", scatter_dimension=0, tiled=True)
    return summed[:, :, None, :]


def per_device(query_ids, query_delta, doc_lengths, vocab_factor, output_factor, train_grads):
    owners = lax.axis_size("dp") * lax.axis_size("rep")
    fits = (
        train_grads.shape[1] == 2 * FBLK * owners
        and lax.axis_size("dp") == 4
        and lax.axis_size("mp") == 2
        and lax.axis_size("rep") == 2
        and doc_lengths.shape[1] == FBLK
        and vocab_factor.shape[0] % FBLK == 0
    )
    body = split_over_blocks if fits else general
    return body(query_ids, query_delta, doc_lengths, vocab_factor, output_factor, train_grads)


def solution(mesh):
    placed = (
        P(("groups", "dp", "rep")),
        P(("groups", "dp", "rep"), "mp"),
        P(("groups", "dp", "rep"), None),
        P("mp", None),
        P("mp", None),
        P(("groups", "dp"), "mp"),
    )
    return jax.shard_map(
        per_device,
        mesh=mesh,
        in_specs=placed,
        out_specs=P(("groups", "dp", "mp"), None, "rep", None),
        check_vma=False,
    )
```

```python
import functools
import jax
import jax.numpy as jnp
from jax import lax
from jax.experimental import pallas as pl
from jax.experimental.pallas import tpu as pltpu
from jax.sharding import PartitionSpec as P

FBLK = 128
SLAB = FBLK + 8
PANEL = 8
ROWS = 16

damping = 0.1

VMEM = pl.BlockSpec(memory_space=pltpu.VMEM)
SMEM = pl.BlockSpec(memory_space=pltpu.SMEM)
HBM = pl.BlockSpec(memory_space=pl.ANY)


def call(kernel, outs, in_specs, scratch=(), vmem=48, flops=0, moved=0):
    return pl.pallas_call(
        kernel,
        out_shape=outs,
        in_specs=in_specs,
        scratch_shapes=list(scratch),
        compiler_params=pltpu.CompilerParams(vmem_limit_bytes=vmem << 20),
        cost_estimate=pl.CostEstimate(flops=flops, bytes_accessed=moved, transcendentals=0),
    )


def swapped(shard, axis, by):
    return lax.ppermute(shard, axis, [(i, i ^ by) for i in range(lax.axis_size(axis))])


def square(dim):
    return lax.broadcasted_iota(jnp.int32, (FBLK, FBLK), dim)


def halves(value):
    high = value.astype(jnp.bfloat16)
    return high, (value - high.astype(jnp.float32)).astype(jnp.bfloat16)


def pack(first, second, spare=None):
    row, col = square(0), square(1)
    body = jnp.where(row >= col, first, second)
    diagonal = jnp.sum(jnp.where(row == col, second, 0.0), axis=0, keepdims=True)
    place = lax.broadcasted_iota(jnp.int32, (8, FBLK), 0)
    tail = jnp.where(place == 0, diagonal, 0.0)
    if spare is not None:
        tail = jnp.where(place == 1, spare, tail)
    return body, tail


def unpack(body, diagonal):
    row, col = square(0), square(1)
    turned = body.T
    first = jnp.where(row >= col, body, turned)
    second = jnp.where(row < col, body, jnp.where(row > col, turned, diagonal))
    return first, second


def grams(lengths, train, slabs):
    cycle = len(slabs)
    mine, half = lax.axis_index("dp"), lax.axis_index("rep")
    spare = lengths[...].astype(jnp.float32)
    for shift, slab in enumerate(slabs):
        owner = half * cycle + (mine ^ shift)
        start = pl.multiple_of(owner * (2 * FBLK), 2 * FBLK)
        part = train[:, pl.ds(start, 2 * FBLK)]
        gram = lax.dot_general(part, part, (((0,), (0,)), ((), ())), preferred_element_type=jnp.float32)
        body, tail = pack(gram[:FBLK, :FBLK], gram[FBLK:, FBLK:], spare)
        slab[pl.ds(0, FBLK), :] = body
        slab[pl.ds(FBLK, 8), :] = tail


def thirds(value):
    high = value.astype(jnp.bfloat16)
    rest = value - high.astype(jnp.float32)
    middle = rest.astype(jnp.bfloat16)
    return high, middle, (rest - middle.astype(jnp.float32)).astype(jnp.bfloat16)


def at_rows(panel, first):
    pair = 2 * PANEL
    blank = jnp.zeros((PANEL, FBLK), jnp.float32)
    panel = panel.astype(jnp.float32)
    piece = jnp.concatenate([panel, blank] if first % pair == 0 else [blank, panel], axis=0).astype(jnp.bfloat16)
    before = first // pair * pair
    pieces = [jnp.zeros((before, FBLK), jnp.bfloat16), piece, jnp.zeros((FBLK - before - pair, FBLK), jnp.bfloat16)]
    return jnp.concatenate([piece for piece in pieces if piece.shape[0]], axis=0)


def product(left, right, first):
    high, middle, low = thirds(left)
    right_high, right_middle, right_low = (at_rows(part, first) for part in thirds(right))
    both = jnp.concatenate([right_high, right_middle], axis=1)
    large = jnp.dot(
        jnp.concatenate([high, middle], axis=1), jnp.concatenate([both, both], axis=0),
        preferred_element_type=jnp.float32,
    )
    small = jnp.dot(
        jnp.concatenate([high, low], axis=1), jnp.concatenate([right_low, right_high], axis=0),
        preferred_element_type=jnp.float32,
    )
    return large[:, :FBLK] + (large[:, FBLK:] + small)


def eliminated(panel, first):
    lane = lax.broadcasted_iota(jnp.int32, (PANEL, FBLK), 1)
    sublane = lax.broadcasted_iota(jnp.int32, (PANEL, FBLK), 0)
    within = (lane >= first) & (lane < first + PANEL)
    count = range(PANEL)

    def across(value, row):
        return jnp.broadcast_to(value[row:row + 1, :], (PANEL, FBLK))

    columns = [jnp.broadcast_to(panel[:, first + j:first + j + 1], (PANEL, FBLK)) for j in count]
    pivots = [[across(columns[j], i) if j >= i else None for j in count] for i in count]
    rest = jnp.where(within, jnp.where(lane == first + sublane, 1.0, 0.0), panel)
    lines = [across(rest, i) for i in count]
    for i in count:
        scale = 1.0 / pivots[i][i]
        scaled = lines[i] * scale
        shares = [pivots[i][j] * scale if j > i else None for j in count]
        for m in range(i + 1, PANEL):
            lines[m] = lines[m] - pivots[i][m] * scaled
            for j in range(m, PANEL):
                pivots[m][j] = pivots[m][j] - shares[m] * pivots[i][j]
        lines[i] = scaled
        pivots[i] = shares
    for i in reversed(count):
        for m in range(i):
            lines[m] = lines[m] - pivots[m][i] * lines[i]
    result = lines[0]
    for i in range(1, PANEL):
        result = jnp.where(sublane == i, lines[i], result)
    return result


def inverted(blocks):
    lane = square(1)
    for first in range(0, FBLK, PANEL):
        within = (lane >= first) & (lane < first + PANEL)
        panels = [eliminated(block[first:first + PANEL, :], first) for block in blocks]
        updates = [product(block, panel, first) for block, panel in zip(blocks, panels)]
        rests = [jnp.where(within, 0.0, block) - update for block, update in zip(blocks, updates)]
        blocks = [
            jnp.concatenate(
                [part for part in (rest[:first], panel, rest[first + PANEL:]) if part.shape[0]], axis=0
            )
            for rest, panel in zip(rests, panels)
        ]
    return blocks


def factor_kernel(examples, scale, *refs):
    slabs, out = refs[:-2], refs[-1]
    body = slabs[0][pl.ds(0, FBLK), :]
    diagonal = slabs[0][pl.ds(FBLK, 1), :]
    for slab in slabs[1:]:
        body = body + slab[pl.ds(0, FBLK), :]
        diagonal = diagonal + slab[pl.ds(FBLK, 1), :]
    same = square(0) == square(1)
    damped = []
    for gram in unpack(body, diagonal):
        fisher = gram / examples
        trace = jnp.sum(jnp.sum(jnp.where(same, fisher, 0.0), axis=0, keepdims=True), axis=1, keepdims=True)
        damped.append(fisher + jnp.where(same, damping * (trace / FBLK), 0.0))
    first, second = inverted(damped)
    body, tail = pack(first * scale, second * scale)
    out[pl.ds(0, FBLK), :] = body
    out[pl.ds(FBLK, 8), :] = tail


def first_kernel(id_rows_hbm, delta_hbm, table_hbm, factor_hbm, lengths_hbm, train_hbm, sent, own, *refs):
    slabs, refs = refs[:-12], refs[-12:]
    id_rows, starts, rolls, start_of, roll_of, delta, table, factor, lengths, train, looked, sems = refs
    model = lax.axis_index("mp")
    proj, vocab_rows = table.shape
    tokens = delta.shape[0]
    each = proj // lax.axis_size("mp")
    groups = tokens // FBLK
    get_ids, get_factor, get_lengths, get_train = (
        pltpu.make_async_copy(source, target, sems.at[0, index])
        for index, (source, target) in enumerate((
            (id_rows_hbm, id_rows), (factor_hbm, factor), (lengths_hbm, lengths), (train_hbm, train),
        ))
    )
    get_table = [
        pltpu.make_async_copy(table_hbm.at[rows], table.at[rows], sems.at[1, index])
        for index in range(proj // ROWS) for rows in (pl.ds(index * ROWS, ROWS),)
    ]

    def get_delta(g):
        rows = pl.ds(pl.multiple_of(g * FBLK, FBLK), FBLK)
        return pltpu.make_async_copy(delta_hbm.at[rows], delta.at[rows], sems.at[2, g])

    for copy in (get_ids, get_lengths, get_train, *get_table, get_factor, *(get_delta(g) for g in range(groups))):
        copy.start()
    get_ids.wait()
    local = id_rows[...] - model * vocab_rows
    owned = (local >= 0) & (local < vocab_rows)
    local = jnp.where(owned, local, 0)
    low = FBLK - 1
    starts[...] = local & ~low
    rolls[...] = (lax.broadcasted_iota(jnp.int32, local.shape, 1) - local) & low
    fetches = [pltpu.make_async_copy(starts, start_of, sems.at[0, 4]), pltpu.make_async_copy(rolls, roll_of, sems.at[0, 5])]
    for fetch in fetches:
        fetch.start()
    get_lengths.wait()
    get_train.wait()
    grams(lengths, train, slabs)
    for fetch in fetches:
        fetch.wait()
    starts[...] = owned.astype(jnp.int32)
    for copy in get_table:
        copy.wait()
    get_factor.wait()
    lanes = lax.broadcasted_iota(jnp.int32, (ROWS, FBLK), 1)

    def group(g, carry):
        columns = pl.ds(pl.multiple_of(g * FBLK, FBLK), FBLK)
        get_delta(g).wait()
        output = lax.dot_general(
            delta[columns, :], factor[...], (((1,), (1,)), ((), ())), preferred_element_type=jnp.float32
        )
        looked[:, columns] = output.T
        gathered = [jnp.zeros((ROWS, FBLK), jnp.bfloat16) for _ in range(proj // ROWS)]
        for j in range(FBLK):
            start, by, here = pl.multiple_of(start_of[g, j], FBLK), roll_of[g, j], lanes == j
            for index in range(proj // ROWS):
                block = table[pl.ds(index * ROWS, ROWS), pl.ds(start, FBLK)]
                gathered[index] = jnp.where(here, pltpu.roll(block, by, 1), gathered[index])
        held = starts[pl.ds(g, 1), :].astype(jnp.float32)
        for index, value in enumerate(gathered):
            value = (value.astype(jnp.float32) * held).astype(jnp.bfloat16)
            rows = pl.ds(2 * each + index * ROWS, ROWS)
            sent[rows, columns] = value
            own[rows, columns] = value
        return carry

    lax.fori_loop(0, groups, group, 0)
    mine = looked[pl.ds(pl.multiple_of(model * each, each), each), :]
    other = looked[pl.ds(pl.multiple_of((1 - model) * each, each), each), :]
    for target, value in ((own, mine), (sent, other)):
        high, rest = halves(value)
        target[pl.ds(0, each), :] = high
        target[pl.ds(each, each), :] = rest


def merge_kernel(each, own, got, out):
    def value(ref):
        return ref[pl.ds(0, each), :].astype(jnp.float32) + ref[pl.ds(each, each), :].astype(jnp.float32)

    high, low = halves(value(own) + value(got))
    out[pl.ds(0, each), :] = high
    out[pl.ds(each, each), :] = low
    rows = pl.ds(2 * each, out.shape[0] - 2 * each)
    out[rows, :] = own[rows, :] + got[rows, :]


def queries_kernel(each, ends_of, factors, slab, *refs):
    far, refs = (refs[0], refs[1:]) if ends_of else (None, refs)
    high_out, low_out = refs[-2:]
    if len(refs) == 4:
        source, high_out, low_out, copy = refs
        copy[...] = source[...]
    tokens = factors.shape[1]
    proj = factors.shape[0] - 2 * each
    queries = high_out.shape[1]
    mine = lax.axis_index("dp")

    def part(first, count):
        value = factors[pl.ds(first, count), :].astype(jnp.float32)
        if ends_of:
            at_end = (mine == 0) | (mine == ends_of - 1)
            value = jnp.where(at_end, far[pl.ds(first, count), :].astype(jnp.float32), value)
        return value

    lengths = slab[pl.ds(FBLK + 1, 1), :]
    upto = jnp.where(square(0) <= square(1), 1.0, 0.0).astype(jnp.bfloat16)
    ends = lax.dot_general(
        jnp.broadcast_to(lengths, (8, queries)).astype(jnp.bfloat16), upto, (((1,), (0,)), ((), ())),
        preferred_element_type=jnp.float32,
    )[:1]
    starts = ends - lengths
    place = lax.broadcasted_iota(jnp.int32, (tokens, queries), 0).astype(jnp.float32)
    inside = jnp.where((place >= starts) & (place < ends), 1.0, 0.0).astype(jnp.bfloat16)
    output = part(0, each) + part(each, each)
    inputs = part(2 * each, proj)
    step = 8
    for start in range(0, each, step):
        grads = jnp.concatenate(
            [(inputs * output[r:r + 1, :]).astype(jnp.bfloat16) for r in range(start, start + step)], axis=0
        )
        summed = jnp.dot(grads, inside, preferred_element_type=jnp.float32)
        high, low = halves(summed)
        high_out[pl.ds(start * proj, step * proj), :] = high
        low_out[pl.ds(start * proj, step * proj), :] = low


def hand_kernel(count, *refs):
    for source, copy in zip(refs[:count], refs[-count:]):
        copy[...] = source[...]


def stack_kernel(count, *refs):
    for index, source in enumerate(refs[:count]):
        refs[-1][index] = source[...]


def scores_kernel(cycle, count, *refs):
    own, peers, refs = refs[:cycle], [refs[cycle].at[index] for index in range(cycle)], refs[cycle + 1:]
    highs, lows = refs[:count], refs[count:2 * count]
    train, sent, kept, pre = refs[2 * count:]
    mine, rep, model = lax.axis_index("dp"), lax.axis_index("rep"), lax.axis_index("mp")
    for half, slabs in ((rep, own), (1 - rep, peers)):
        for shift in range(cycle):
            owner = half * cycle + (mine ^ shift)
            slab = slabs[shift]
            blocks = unpack(slab[pl.ds(0, FBLK), :], slab[pl.ds(FBLK, 1), :])
            for index, block in enumerate(blocks):
                rows = pl.ds(pl.multiple_of(owner * (2 * FBLK) + index * FBLK, FBLK), FBLK)
                high, low = halves(block)
                right_high = jnp.concatenate([ref[rows, :] for ref in highs], axis=1)
                right_low = jnp.concatenate([ref[rows, :] for ref in lows], axis=1)
                solved = jnp.dot(
                    jnp.concatenate([high, high, low], axis=1),
                    jnp.concatenate([right_high, right_low, right_high], axis=0),
                    preferred_element_type=jnp.float32,
                )
                pre[rows, :] = solved.astype(jnp.bfloat16)
    half_rows = sent.shape[0]
    for out, which in ((sent, 1 - model), (kept, model)):
        rows = pl.ds(pl.multiple_of(which * half_rows, half_rows), half_rows)
        out[...] = jnp.dot(train[rows, :], pre[...], preferred_element_type=jnp.float32).astype(jnp.bfloat16)


def total_kernel(order, *refs):
    pieces, out = refs[:-1], refs[-1]
    mine, cycle = lax.axis_index("dp"), len(order)
    sums = {}
    for kept, got in zip(pieces[::2], pieces[1::2]):
        both = kept[...].astype(jnp.float32) + got[...].astype(jnp.float32)
        for index in range(both.shape[1] // FBLK):
            sums[order[len(sums)]] = both[:, index * FBLK:(index + 1) * FBLK]
    placed = []
    for source in range(cycle):
        shift = mine ^ source
        value = sums[0]
        for index in range(1, cycle):
            value = jnp.where(shift == index, sums[index], value)
        placed.append(value)
    out[...] = jnp.concatenate(placed, axis=1).astype(jnp.bfloat16)


def shape(dims, dtype):
    return jax.ShapeDtypeStruct(dims, dtype)


def split_over_blocks(query_ids, query_delta, doc_lengths, vocab_factor, output_factor, train_grads):
    cycle = lax.axis_size("dp")
    tokens, width = query_delta.shape
    proj = output_factor.shape[1]
    each = proj // lax.axis_size("mp")
    vocab_rows = vocab_factor.shape[0]
    train_rows, feat = train_grads.shape
    queries = doc_lengths.shape[1]
    bf16, f32 = jnp.bfloat16, jnp.float32

    sent, own, *slabs = call(
        first_kernel,
        [shape((2 * each + proj, tokens), bf16)] * 2 + [shape((SLAB, FBLK), f32)] * cycle,
        [HBM] * 6,
        [
            pltpu.VMEM((tokens // FBLK, FBLK), jnp.int32),
            pltpu.VMEM((tokens // FBLK, FBLK), jnp.int32),
            pltpu.VMEM((tokens // FBLK, FBLK), jnp.int32),
            pltpu.SMEM((tokens // FBLK, FBLK), jnp.int32),
            pltpu.SMEM((tokens // FBLK, FBLK), jnp.int32),
            pltpu.VMEM((tokens, width), bf16),
            pltpu.VMEM((proj, vocab_rows), bf16),
            pltpu.VMEM((proj, width), bf16),
            pltpu.VMEM((1, queries), jnp.int32),
            pltpu.VMEM((train_rows, feat), bf16),
            pltpu.VMEM((proj, tokens), f32),
            pltpu.SemaphoreType.DMA((3, 8)),
        ],
        vmem=62,
        flops=2 * tokens * width * proj,
        moved=2 * (tokens * width + proj * vocab_rows) * 2,
    )(
        query_ids.reshape(tokens // FBLK, FBLK), query_delta, vocab_factor.T, output_factor.T,
        doc_lengths, train_grads,
    )
    got = swapped(sent, "mp", 1)
    own, kept = call(
        functools.partial(hand_kernel, 2),
        [shape(own.shape, bf16), shape((SLAB, FBLK), f32)],
        [VMEM, VMEM],
        vmem=16,
        moved=4 * own.size,
    )(own, slabs[0])
    parts = [kept] + [swapped(slabs[s], "dp", s) for s in range(1, cycle)]

    factors = call(
        functools.partial(merge_kernel, each),
        shape(sent.shape, bf16),
        [VMEM, VMEM],
        vmem=16,
        flops=tokens * each,
        moved=8 * tokens * each * 4,
    )(own, got)
    late = cycle - 1
    gathered = [factors] + [swapped(factors, "dp", s) if s != late else None for s in range(1, cycle)]

    inverse = call(
        functools.partial(factor_kernel, train_rows * cycle, 1.0 / proj),
        shape((SLAB, FBLK), f32),
        [VMEM] * cycle + [HBM],
        vmem=16,
        flops=10 ** 10,
        moved=10 ** 6,
    )(*parts, factors)
    inverses = [inverse] + [swapped(inverse, "dp", s) for s in range(1, cycle)]
    copies = {0: [inverse], 1: [factors], 2: [gathered[2]]}
    highs, lows, far = {}, {}, []
    for s in range(cycle):
        extra = copies.get(s, far)
        copied = s in (1, 2)
        highs[s], lows[s], *again = call(
            functools.partial(queries_kernel, each, cycle if s == late else 0),
            [shape((feat, queries), bf16)] * 2 + [shape(factors.shape, bf16)] * copied,
            [VMEM, VMEM] + [HBM if s == 0 else VMEM] * len(extra),
            vmem=24,
            flops=2 * feat * tokens * queries,
            moved=6 * feat * queries,
        )(gathered[s], parts[s], *extra)
        if s == 1:
            gathered[late] = lax.ppermute(again[0], "dp", [(1, 2), (2, 1)])
        if s == 2:
            far = [lax.ppermute(again[0], "dp", [(1, 0), (2, 3)])]
    stacked = call(
        functools.partial(stack_kernel, cycle),
        shape((cycle, SLAB, FBLK), f32),
        [VMEM] * cycle + [HBM] * (cycle - 2),
        vmem=16,
        moved=8 * cycle * SLAB * FBLK,
    )(*inverses, *[highs[s] for s in range(1, cycle) if s != late])
    peers = swapped(stacked, "rep", 1)

    half_rows = train_rows // lax.axis_size("mp")
    pieces, order = [], []
    for chosen in ([s for s in range(cycle) if s != late], [late]):
        count = len(chosen)
        outgoing, kept = call(
            functools.partial(scores_kernel, cycle, count),
            [shape((half_rows, count * queries), bf16)] * 2,
            [VMEM] * (cycle + 2 * count + 2),
            [pltpu.VMEM((feat, count * queries), bf16)],
            vmem=24,
            flops=2 * train_rows * feat * count * queries,
            moved=8 * feat * queries * count,
        )(*inverses, peers, *[highs[s] for s in chosen], *[lows[s] for s in chosen], train_grads)
        pieces += [kept, swapped(outgoing, "mp", 1)]
        order += chosen
    total = call(
        functools.partial(total_kernel, order),
        shape((half_rows, cycle * queries), bf16),
        [VMEM] * len(pieces),
        vmem=16,
        flops=half_rows * cycle * queries,
        moved=6 * half_rows * cycle * queries,
    )(*pieces)
    return total.reshape(half_rows, cycle, 1, queries)


def doc_matrix(lengths_row, count):
    ends = jnp.cumsum(lengths_row)
    starts = ends - lengths_row
    place = jnp.arange(count, dtype=jnp.int32)
    inside = (place[None, :] >= starts[:, None]) & (place[None, :] < ends[:, None])
    return inside.astype(jnp.bfloat16)


def solve_block(factor, rhs):
    return jax.scipy.linalg.cho_solve((factor, True), rhs)


def general(query_ids, query_delta, doc_lengths, vocab_factor, output_factor, train_grads):
    model_count = lax.axis_size("mp")
    model_index = lax.axis_index("mp")
    vocab_rows = vocab_factor.shape[0]
    local_ids = query_ids - model_index * vocab_rows
    owned = (local_ids >= 0) & (local_ids < vocab_rows)
    looked = vocab_factor[jnp.clip(local_ids, 0, vocab_rows - 1)].astype(jnp.float32)
    vocab_part = jnp.where(owned[:, None], looked, jnp.zeros_like(looked))
    output_part = jnp.dot(query_delta, output_factor, preferred_element_type=jnp.float32)
    input_side, output_side = lax.psum((vocab_part, output_part), "mp")
    proj = output_side.shape[1]
    rows_each = proj // model_count
    mine = lax.dynamic_slice_in_dim(output_side, model_index * rows_each, rows_each, 1)
    token_count = query_ids.shape[0]
    token_grads = (
        (mine[:, :, None] * input_side[:, None, :])
        .reshape(token_count, rows_each * proj)
        .astype(jnp.bfloat16)
    )
    query_grads = jnp.dot(
        doc_matrix(doc_lengths[0], token_count), token_grads, preferred_element_type=jnp.float32
    )
    train_rows, feat_dev = train_grads.shape
    nblocks = feat_dev // FBLK
    tiled = train_grads.reshape(train_rows, nblocks, FBLK)
    local_gram = jnp.einsum("tbi,tbj->bij", tiled, tiled, preferred_element_type=jnp.float32)
    total_gram = lax.psum(local_gram, "dp")
    fisher = total_gram / (train_rows * lax.axis_size("dp"))
    shift_amount = damping * (jnp.trace(fisher, axis1=1, axis2=2) / FBLK)
    damped = fisher + shift_amount[:, None, None] * jnp.eye(FBLK, dtype=jnp.float32)[None]
    factor = jnp.linalg.cholesky(damped)
    queries = query_grads.shape[0]
    rhs = jnp.transpose(query_grads.reshape(queries, nblocks, FBLK), (1, 2, 0))
    solved = jax.vmap(solve_block)(factor, rhs)
    pre = (jnp.transpose(solved, (2, 0, 1)).reshape(queries, feat_dev) / proj).astype(jnp.bfloat16)
    cycle = lax.axis_size("dp")
    everyone = lax.all_gather(pre, "dp", axis=0, tiled=True)
    scores = lax.dot_general(
        train_grads, everyone, (((1,), (1,)), ((), ())), preferred_element_type=jnp.float32
    )
    scores = scores.astype(jnp.bfloat16).reshape(train_rows, cycle, queries)
    summed = lax.psum_scatter(scores, "mp", scatter_dimension=0, tiled=True)
    return summed[:, :, None, :]


def per_device(query_ids, query_delta, doc_lengths, vocab_factor, output_factor, train_grads):
    owners = lax.axis_size("dp") * lax.axis_size("rep")
    fits = (
        train_grads.shape[1] == 2 * FBLK * owners
        and lax.axis_size("dp") == 4
        and lax.axis_size("mp") == 2
        and lax.axis_size("rep") == 2
        and doc_lengths.shape[1] == FBLK
        and vocab_factor.shape[0] % FBLK == 0
    )
    body = split_over_blocks if fits else general
    return body(query_ids, query_delta, doc_lengths, vocab_factor, output_factor, train_grads)


def solution(mesh):
    placed = (
        P(("groups", "dp", "rep")),
        P(("groups", "dp", "rep"), "mp"),
        P(("groups", "dp", "rep"), None),
        P("mp", None),
        P("mp", None),
        P(("groups", "dp"), "mp"),
    )
    return jax.shard_map(
        per_device,
        mesh=mesh,
        in_specs=placed,
        out_specs=P(("groups", "dp", "mp"), None, "rep", None),
        check_vma=False,
    )
```

```python
import functools
import jax
import jax.numpy as jnp
from jax import lax
from jax.experimental import pallas as pl
from jax.experimental.pallas import tpu as pltpu
from jax.sharding import PartitionSpec as P

FBLK = 128
SLAB = FBLK + 8
PANEL = 8
ROWS = 16

damping = 0.1

VMEM = pl.BlockSpec(memory_space=pltpu.VMEM)
SMEM = pl.BlockSpec(memory_space=pltpu.SMEM)
HBM = pl.BlockSpec(memory_space=pl.ANY)


def call(kernel, outs, in_specs, scratch=(), vmem=48, flops=0, moved=0):
    return pl.pallas_call(
        kernel,
        out_shape=outs,
        in_specs=in_specs,
        scratch_shapes=list(scratch),
        compiler_params=pltpu.CompilerParams(vmem_limit_bytes=vmem << 20),
        cost_estimate=pl.CostEstimate(flops=flops, bytes_accessed=moved, transcendentals=0),
    )


def swapped(shard, axis, by):
    return lax.ppermute(shard, axis, [(i, i ^ by) for i in range(lax.axis_size(axis))])


def square(dim):
    return lax.broadcasted_iota(jnp.int32, (FBLK, FBLK), dim)


def halves(value):
    high = value.astype(jnp.bfloat16)
    return high, (value - high.astype(jnp.float32)).astype(jnp.bfloat16)


def pack(first, second, spare=None):
    row, col = square(0), square(1)
    body = jnp.where(row >= col, first, second)
    diagonal = jnp.sum(jnp.where(row == col, second, 0.0), axis=0, keepdims=True)
    place = lax.broadcasted_iota(jnp.int32, (8, FBLK), 0)
    tail = jnp.where(place == 0, diagonal, 0.0)
    if spare is not None:
        tail = jnp.where(place == 1, spare, tail)
    return body, tail


def unpack(body, diagonal):
    row, col = square(0), square(1)
    turned = body.T
    first = jnp.where(row >= col, body, turned)
    second = jnp.where(row < col, body, jnp.where(row > col, turned, diagonal))
    return first, second


def grams(lengths, train, slabs):
    cycle = len(slabs)
    mine, half = lax.axis_index("dp"), lax.axis_index("rep")
    spare = lengths[...].astype(jnp.float32)
    for shift, slab in enumerate(slabs):
        owner = half * cycle + (mine ^ shift)
        start = pl.multiple_of(owner * (2 * FBLK), 2 * FBLK)
        part = train[:, pl.ds(start, 2 * FBLK)]
        gram = lax.dot_general(part, part, (((0,), (0,)), ((), ())), preferred_element_type=jnp.float32)
        body, tail = pack(gram[:FBLK, :FBLK], gram[FBLK:, FBLK:], spare)
        slab[pl.ds(0, FBLK), :] = body
        slab[pl.ds(FBLK, 8), :] = tail


def thirds(value):
    high = value.astype(jnp.bfloat16)
    rest = value - high.astype(jnp.float32)
    middle = rest.astype(jnp.bfloat16)
    return high, middle, (rest - middle.astype(jnp.float32)).astype(jnp.bfloat16)


def at_rows(panel, first):
    pair = 2 * PANEL
    blank = jnp.zeros((PANEL, FBLK), jnp.float32)
    panel = panel.astype(jnp.float32)
    piece = jnp.concatenate([panel, blank] if first % pair == 0 else [blank, panel], axis=0).astype(jnp.bfloat16)
    before = first // pair * pair
    pieces = [jnp.zeros((before, FBLK), jnp.bfloat16), piece, jnp.zeros((FBLK - before - pair, FBLK), jnp.bfloat16)]
    return jnp.concatenate([piece for piece in pieces if piece.shape[0]], axis=0)


def product(left, right, first):
    high, middle, low = thirds(left)
    right_high, right_middle, right_low = (at_rows(part, first) for part in thirds(right))
    both = jnp.concatenate([right_high, right_middle], axis=1)
    large = jnp.dot(
        jnp.concatenate([high, middle], axis=1), jnp.concatenate([both, both], axis=0),
        preferred_element_type=jnp.float32,
    )
    small = jnp.dot(
        jnp.concatenate([high, low], axis=1), jnp.concatenate([right_low, right_high], axis=0),
        preferred_element_type=jnp.float32,
    )
    return large[:, :FBLK] + (large[:, FBLK:] + small)


def eliminated(panel, first):
    lane = lax.broadcasted_iota(jnp.int32, (PANEL, FBLK), 1)
    sublane = lax.broadcasted_iota(jnp.int32, (PANEL, FBLK), 0)
    within = (lane >= first) & (lane < first + PANEL)
    count = range(PANEL)

    def across(value, row):
        return jnp.broadcast_to(value[row:row + 1, :], (PANEL, FBLK))

    columns = [jnp.broadcast_to(panel[:, first + j:first + j + 1], (PANEL, FBLK)) for j in count]
    pivots = [[across(columns[j], i) if j >= i else None for j in count] for i in count]
    rest = jnp.where(within, jnp.where(lane == first + sublane, 1.0, 0.0), panel)
    lines = [across(rest, i) for i in count]
    for i in count:
        scale = 1.0 / pivots[i][i]
        scaled = lines[i] * scale
        shares = [pivots[i][j] * scale if j > i else None for j in count]
        for m in range(i + 1, PANEL):
            lines[m] = lines[m] - pivots[i][m] * scaled
            for j in range(m, PANEL):
                pivots[m][j] = pivots[m][j] - shares[m] * pivots[i][j]
        lines[i] = scaled
        pivots[i] = shares
    for i in reversed(count):
        for m in range(i):
            lines[m] = lines[m] - pivots[m][i] * lines[i]
    result = lines[0]
    for i in range(1, PANEL):
        result = jnp.where(sublane == i, lines[i], result)
    return result


def inverted(blocks):
    lane = square(1)
    for first in range(0, FBLK, PANEL):
        within = (lane >= first) & (lane < first + PANEL)
        panels = [eliminated(block[first:first + PANEL, :], first) for block in blocks]
        updates = [product(block, panel, first) for block, panel in zip(blocks, panels)]
        rests = [jnp.where(within, 0.0, block) - update for block, update in zip(blocks, updates)]
        blocks = [
            jnp.concatenate(
                [part for part in (rest[:first], panel, rest[first + PANEL:]) if part.shape[0]], axis=0
            )
            for rest, panel in zip(rests, panels)
        ]
    return blocks


def factor_kernel(examples, scale, *refs):
    slabs, out = refs[:-2], refs[-1]
    body = slabs[0][pl.ds(0, FBLK), :]
    diagonal = slabs[0][pl.ds(FBLK, 1), :]
    for slab in slabs[1:]:
        body = body + slab[pl.ds(0, FBLK), :]
        diagonal = diagonal + slab[pl.ds(FBLK, 1), :]
    same = square(0) == square(1)
    damped = []
    for gram in unpack(body, diagonal):
        fisher = gram / examples
        trace = jnp.sum(jnp.sum(jnp.where(same, fisher, 0.0), axis=0, keepdims=True), axis=1, keepdims=True)
        damped.append(fisher + jnp.where(same, damping * (trace / FBLK), 0.0))
    first, second = inverted(damped)
    body, tail = pack(first * scale, second * scale)
    out[pl.ds(0, FBLK), :] = body
    out[pl.ds(FBLK, 8), :] = tail


def first_kernel(id_rows_hbm, delta_hbm, table_hbm, factor_hbm, lengths_hbm, train_hbm, sent, own, *refs):
    slabs, refs = refs[:-12], refs[-12:]
    id_rows, starts, rolls, start_of, roll_of, delta, table, factor, lengths, train, looked, sems = refs
    model = lax.axis_index("mp")
    proj, vocab_rows = table.shape
    tokens = delta.shape[0]
    each = proj // lax.axis_size("mp")
    groups = tokens // FBLK
    get_ids, get_factor, get_lengths, get_train = (
        pltpu.make_async_copy(source, target, sems.at[0, index])
        for index, (source, target) in enumerate((
            (id_rows_hbm, id_rows), (factor_hbm, factor), (lengths_hbm, lengths), (train_hbm, train),
        ))
    )
    get_table = [
        pltpu.make_async_copy(table_hbm.at[rows], table.at[rows], sems.at[1, index])
        for index in range(proj // ROWS) for rows in (pl.ds(index * ROWS, ROWS),)
    ]

    def get_delta(g):
        rows = pl.ds(pl.multiple_of(g * FBLK, FBLK), FBLK)
        return pltpu.make_async_copy(delta_hbm.at[rows], delta.at[rows], sems.at[2, g])

    for copy in (get_ids, get_lengths, get_train, *get_table, get_factor, *(get_delta(g) for g in range(groups))):
        copy.start()
    get_ids.wait()
    local = id_rows[...] - model * vocab_rows
    owned = (local >= 0) & (local < vocab_rows)
    local = jnp.where(owned, local, 0)
    low = FBLK - 1
    starts[...] = local & ~low
    rolls[...] = (lax.broadcasted_iota(jnp.int32, local.shape, 1) - local) & low
    fetches = [pltpu.make_async_copy(starts, start_of, sems.at[0, 4]), pltpu.make_async_copy(rolls, roll_of, sems.at[0, 5])]
    for fetch in fetches:
        fetch.start()
    get_lengths.wait()
    get_train.wait()
    grams(lengths, train, slabs)
    for fetch in fetches:
        fetch.wait()
    starts[...] = owned.astype(jnp.int32)
    for copy in get_table:
        copy.wait()
    get_factor.wait()
    lanes = lax.broadcasted_iota(jnp.int32, (ROWS, FBLK), 1)

    def group(g, carry):
        columns = pl.ds(pl.multiple_of(g * FBLK, FBLK), FBLK)
        get_delta(g).wait()
        output = lax.dot_general(
            delta[columns, :], factor[...], (((1,), (1,)), ((), ())), preferred_element_type=jnp.float32
        )
        looked[:, columns] = output.T
        gathered = [jnp.zeros((ROWS, FBLK), jnp.bfloat16) for _ in range(proj // ROWS)]
        for j in range(FBLK):
            start, by, here = pl.multiple_of(start_of[g, j], FBLK), roll_of[g, j], lanes == j
            for index in range(proj // ROWS):
                block = table[pl.ds(index * ROWS, ROWS), pl.ds(start, FBLK)]
                gathered[index] = jnp.where(here, pltpu.roll(block, by, 1), gathered[index])
        held = starts[pl.ds(g, 1), :].astype(jnp.float32)
        for index, value in enumerate(gathered):
            value = (value.astype(jnp.float32) * held).astype(jnp.bfloat16)
            rows = pl.ds(2 * each + index * ROWS, ROWS)
            sent[rows, columns] = value
            own[rows, columns] = value
        return carry

    lax.fori_loop(0, groups, group, 0)
    mine = looked[pl.ds(pl.multiple_of(model * each, each), each), :]
    other = looked[pl.ds(pl.multiple_of((1 - model) * each, each), each), :]
    for target, value in ((own, mine), (sent, other)):
        high, rest = halves(value)
        target[pl.ds(0, each), :] = high
        target[pl.ds(each, each), :] = rest


def merge_kernel(each, own, got, out):
    def value(ref):
        return ref[pl.ds(0, each), :].astype(jnp.float32) + ref[pl.ds(each, each), :].astype(jnp.float32)

    high, low = halves(value(own) + value(got))
    out[pl.ds(0, each), :] = high
    out[pl.ds(each, each), :] = low
    rows = pl.ds(2 * each, out.shape[0] - 2 * each)
    out[rows, :] = own[rows, :] + got[rows, :]


def queries_kernel(each, ends_of, factors, slab, *refs):
    far, refs = (refs[0], refs[1:]) if ends_of else (None, refs)
    high_out, low_out = refs[-2:]
    if len(refs) == 4:
        source, high_out, low_out, copy = refs
        copy[...] = source[...]
    tokens = factors.shape[1]
    proj = factors.shape[0] - 2 * each
    queries = high_out.shape[1]
    mine = lax.axis_index("dp")

    def part(first, count):
        value = factors[pl.ds(first, count), :].astype(jnp.float32)
        if ends_of:
            at_end = (mine == 0) | (mine == ends_of - 1)
            value = jnp.where(at_end, far[pl.ds(first, count), :].astype(jnp.float32), value)
        return value

    lengths = slab[pl.ds(FBLK + 1, 1), :]
    upto = jnp.where(square(0) <= square(1), 1.0, 0.0).astype(jnp.bfloat16)
    ends = lax.dot_general(
        jnp.broadcast_to(lengths, (8, queries)).astype(jnp.bfloat16), upto, (((1,), (0,)), ((), ())),
        preferred_element_type=jnp.float32,
    )[:1]
    starts = ends - lengths
    place = lax.broadcasted_iota(jnp.int32, (tokens, queries), 0).astype(jnp.float32)
    inside = jnp.where((place >= starts) & (place < ends), 1.0, 0.0).astype(jnp.bfloat16)
    output = part(0, each) + part(each, each)
    inputs = part(2 * each, proj)
    step = 8
    for start in range(0, each, step):
        grads = jnp.concatenate(
            [(inputs * output[r:r + 1, :]).astype(jnp.bfloat16) for r in range(start, start + step)], axis=0
        )
        summed = jnp.dot(grads, inside, preferred_element_type=jnp.float32)
        high, low = halves(summed)
        high_out[pl.ds(start * proj, step * proj), :] = high
        low_out[pl.ds(start * proj, step * proj), :] = low


def hand_kernel(count, *refs):
    for source, copy in zip(refs[:count], refs[-count:]):
        copy[...] = source[...]


def scores_kernel(cycle, count, *refs):
    own, peers = refs[:cycle], refs[cycle:2 * cycle]
    highs, lows = refs[2 * cycle:2 * cycle + count], refs[2 * cycle + count:2 * cycle + 2 * count]
    train, sent, kept, pre = refs[2 * cycle + 2 * count:]
    mine, rep, model = lax.axis_index("dp"), lax.axis_index("rep"), lax.axis_index("mp")
    for half, slabs in ((rep, own), (1 - rep, peers)):
        for shift in range(cycle):
            owner = half * cycle + (mine ^ shift)
            slab = slabs[shift]
            blocks = unpack(slab[pl.ds(0, FBLK), :], slab[pl.ds(FBLK, 1), :])
            for index, block in enumerate(blocks):
                rows = pl.ds(pl.multiple_of(owner * (2 * FBLK) + index * FBLK, FBLK), FBLK)
                high, low = halves(block)
                right_high = jnp.concatenate([ref[rows, :] for ref in highs], axis=1)
                right_low = jnp.concatenate([ref[rows, :] for ref in lows], axis=1)
                solved = jnp.dot(
                    jnp.concatenate([high, high, low], axis=1),
                    jnp.concatenate([right_high, right_low, right_high], axis=0),
                    preferred_element_type=jnp.float32,
                )
                pre[rows, :] = solved.astype(jnp.bfloat16)
    half_rows = sent.shape[0]
    for out, which in ((sent, 1 - model), (kept, model)):
        rows = pl.ds(pl.multiple_of(which * half_rows, half_rows), half_rows)
        out[...] = jnp.dot(train[rows, :], pre[...], preferred_element_type=jnp.float32).astype(jnp.bfloat16)


def total_kernel(order, *refs):
    pieces, out = refs[:-1], refs[-1]
    mine, cycle = lax.axis_index("dp"), len(order)
    sums = {}
    for kept, got in zip(pieces[::2], pieces[1::2]):
        both = kept[...].astype(jnp.float32) + got[...].astype(jnp.float32)
        for index in range(both.shape[1] // FBLK):
            sums[order[len(sums)]] = both[:, index * FBLK:(index + 1) * FBLK]
    placed = []
    for source in range(cycle):
        shift = mine ^ source
        value = sums[0]
        for index in range(1, cycle):
            value = jnp.where(shift == index, sums[index], value)
        placed.append(value)
    out[...] = jnp.concatenate(placed, axis=1).astype(jnp.bfloat16)


def shape(dims, dtype):
    return jax.ShapeDtypeStruct(dims, dtype)


def split_over_blocks(query_ids, query_delta, doc_lengths, vocab_factor, output_factor, train_grads):
    cycle = lax.axis_size("dp")
    tokens, width = query_delta.shape
    proj = output_factor.shape[1]
    each = proj // lax.axis_size("mp")
    vocab_rows = vocab_factor.shape[0]
    train_rows, feat = train_grads.shape
    queries = doc_lengths.shape[1]
    bf16, f32 = jnp.bfloat16, jnp.float32

    sent, own, *slabs = call(
        first_kernel,
        [shape((2 * each + proj, tokens), bf16)] * 2 + [shape((SLAB, FBLK), f32)] * cycle,
        [HBM] * 6,
        [
            pltpu.VMEM((tokens // FBLK, FBLK), jnp.int32),
            pltpu.VMEM((tokens // FBLK, FBLK), jnp.int32),
            pltpu.VMEM((tokens // FBLK, FBLK), jnp.int32),
            pltpu.SMEM((tokens // FBLK, FBLK), jnp.int32),
            pltpu.SMEM((tokens // FBLK, FBLK), jnp.int32),
            pltpu.VMEM((tokens, width), bf16),
            pltpu.VMEM((proj, vocab_rows), bf16),
            pltpu.VMEM((proj, width), bf16),
            pltpu.VMEM((1, queries), jnp.int32),
            pltpu.VMEM((train_rows, feat), bf16),
            pltpu.VMEM((proj, tokens), f32),
            pltpu.SemaphoreType.DMA((3, 8)),
        ],
        vmem=62,
        flops=2 * tokens * width * proj,
        moved=2 * (tokens * width + proj * vocab_rows) * 2,
    )(
        query_ids.reshape(tokens // FBLK, FBLK), query_delta, vocab_factor.T, output_factor.T,
        doc_lengths, train_grads,
    )
    got = swapped(sent, "mp", 1)
    own, kept = call(
        functools.partial(hand_kernel, 2),
        [shape(own.shape, bf16), shape((SLAB, FBLK), f32)],
        [VMEM, VMEM],
        vmem=16,
        moved=4 * own.size,
    )(own, slabs[0])
    parts = [kept] + [swapped(slabs[s], "dp", s) for s in range(1, cycle)]

    factors = call(
        functools.partial(merge_kernel, each),
        shape(sent.shape, bf16),
        [VMEM, VMEM],
        vmem=16,
        flops=tokens * each,
        moved=8 * tokens * each * 4,
    )(own, got)
    late = cycle - 1
    gathered = [factors] + [swapped(factors, "dp", s) if s != late else None for s in range(1, cycle)]

    inverse = call(
        functools.partial(factor_kernel, train_rows * cycle, 1.0 / proj),
        shape((SLAB, FBLK), f32),
        [VMEM] * cycle + [HBM],
        vmem=16,
        flops=10 ** 10,
        moved=10 ** 6,
    )(*parts, factors)
    inverses = [inverse] + [swapped(inverse, "dp", s) for s in range(1, cycle)]
    copies = {0: [inverse], 1: [factors], 2: [gathered[2]]}
    highs, lows, far = {}, {}, []
    for s in range(cycle):
        extra = copies.get(s, far)
        copied = s in (1, 2)
        highs[s], lows[s], *again = call(
            functools.partial(queries_kernel, each, cycle if s == late else 0),
            [shape((feat, queries), bf16)] * 2 + [shape(factors.shape, bf16)] * copied,
            [VMEM, VMEM] + [HBM if s == 0 else VMEM] * len(extra),
            vmem=24,
            flops=2 * feat * tokens * queries,
            moved=6 * feat * queries,
        )(gathered[s], parts[s], *extra)
        if s == 1:
            gathered[late] = lax.ppermute(again[0], "dp", [(1, 2), (2, 1)])
        if s == 2:
            far = [lax.ppermute(again[0], "dp", [(1, 0), (2, 3)])]
    handed = list(inverses)
    handed[0], handed[late] = call(
        functools.partial(hand_kernel, 2),
        [shape((SLAB, FBLK), f32)] * 2,
        [VMEM] * 2 + [HBM] * (cycle - 2),
        vmem=16,
        moved=16 * SLAB * FBLK,
    )(inverse, inverses[late], *[highs[s] for s in range(1, cycle) if s != late])
    peers = [swapped(slab, "rep", 1) for slab in handed]

    half_rows = train_rows // lax.axis_size("mp")
    pieces, order = [], []
    for chosen in ([s for s in range(cycle) if s != late], [late]):
        count = len(chosen)
        outgoing, kept = call(
            functools.partial(scores_kernel, cycle, count),
            [shape((half_rows, count * queries), bf16)] * 2,
            [VMEM] * (2 * cycle + 2 * count + 1),
            [pltpu.VMEM((feat, count * queries), bf16)],
            vmem=24,
            flops=2 * train_rows * feat * count * queries,
            moved=8 * feat * queries * count,
        )(*inverses, *peers, *[highs[s] for s in chosen], *[lows[s] for s in chosen], train_grads)
        pieces += [kept, swapped(outgoing, "mp", 1)]
        order += chosen
    total = call(
        functools.partial(total_kernel, order),
        shape((half_rows, cycle * queries), bf16),
        [VMEM] * len(pieces),
        vmem=16,
        flops=half_rows * cycle * queries,
        moved=6 * half_rows * cycle * queries,
    )(*pieces)
    return total.reshape(half_rows, cycle, 1, queries)


def doc_matrix(lengths_row, count):
    ends = jnp.cumsum(lengths_row)
    starts = ends - lengths_row
    place = jnp.arange(count, dtype=jnp.int32)
    inside = (place[None, :] >= starts[:, None]) & (place[None, :] < ends[:, None])
    return inside.astype(jnp.bfloat16)


def solve_block(factor, rhs):
    return jax.scipy.linalg.cho_solve((factor, True), rhs)


def general(query_ids, query_delta, doc_lengths, vocab_factor, output_factor, train_grads):
    model_count = lax.axis_size("mp")
    model_index = lax.axis_index("mp")
    vocab_rows = vocab_factor.shape[0]
    local_ids = query_ids - model_index * vocab_rows
    owned = (local_ids >= 0) & (local_ids < vocab_rows)
    looked = vocab_factor[jnp.clip(local_ids, 0, vocab_rows - 1)].astype(jnp.float32)
    vocab_part = jnp.where(owned[:, None], looked, jnp.zeros_like(looked))
    output_part = jnp.dot(query_delta, output_factor, preferred_element_type=jnp.float32)
    input_side, output_side = lax.psum((vocab_part, output_part), "mp")
    proj = output_side.shape[1]
    rows_each = proj // model_count
    mine = lax.dynamic_slice_in_dim(output_side, model_index * rows_each, rows_each, 1)
    token_count = query_ids.shape[0]
    token_grads = (
        (mine[:, :, None] * input_side[:, None, :])
        .reshape(token_count, rows_each * proj)
        .astype(jnp.bfloat16)
    )
    query_grads = jnp.dot(
        doc_matrix(doc_lengths[0], token_count), token_grads, preferred_element_type=jnp.float32
    )
    train_rows, feat_dev = train_grads.shape
    nblocks = feat_dev // FBLK
    tiled = train_grads.reshape(train_rows, nblocks, FBLK)
    local_gram = jnp.einsum("tbi,tbj->bij", tiled, tiled, preferred_element_type=jnp.float32)
    total_gram = lax.psum(local_gram, "dp")
    fisher = total_gram / (train_rows * lax.axis_size("dp"))
    shift_amount = damping * (jnp.trace(fisher, axis1=1, axis2=2) / FBLK)
    damped = fisher + shift_amount[:, None, None] * jnp.eye(FBLK, dtype=jnp.float32)[None]
    factor = jnp.linalg.cholesky(damped)
    queries = query_grads.shape[0]
    rhs = jnp.transpose(query_grads.reshape(queries, nblocks, FBLK), (1, 2, 0))
    solved = jax.vmap(solve_block)(factor, rhs)
    pre = (jnp.transpose(solved, (2, 0, 1)).reshape(queries, feat_dev) / proj).astype(jnp.bfloat16)
    cycle = lax.axis_size("dp")
    everyone = lax.all_gather(pre, "dp", axis=0, tiled=True)
    scores = lax.dot_general(
        train_grads, everyone, (((1,), (1,)), ((), ())), preferred_element_type=jnp.float32
    )
    scores = scores.astype(jnp.bfloat16).reshape(train_rows, cycle, queries)
    summed = lax.psum_scatter(scores, "mp", scatter_dimension=0, tiled=True)
    return summed[:, :, None, :]


def per_device(query_ids, query_delta, doc_lengths, vocab_factor, output_factor, train_grads):
    owners = lax.axis_size("dp") * lax.axis_size("rep")
    fits = (
        train_grads.shape[1] == 2 * FBLK * owners
        and lax.axis_size("dp") == 4
        and lax.axis_size("mp") == 2
        and lax.axis_size("rep") == 2
        and doc_lengths.shape[1] == FBLK
        and vocab_factor.shape[0] % FBLK == 0
    )
    body = split_over_blocks if fits else general
    return body(query_ids, query_delta, doc_lengths, vocab_factor, output_factor, train_grads)


def solution(mesh):
    placed = (
        P(("groups", "dp", "rep")),
        P(("groups", "dp", "rep"), "mp"),
        P(("groups", "dp", "rep"), None),
        P("mp", None),
        P("mp", None),
        P(("groups", "dp"), "mp"),
    )
    return jax.shard_map(
        per_device,
        mesh=mesh,
        in_specs=placed,
        out_specs=P(("groups", "dp", "mp"), None, "rep", None),
        check_vma=False,
    )
```

```python
import functools
import jax
import jax.numpy as jnp
from jax import lax
from jax.experimental import pallas as pl
from jax.experimental.pallas import tpu as pltpu
from jax.sharding import PartitionSpec as P

FBLK = 128
SLAB = FBLK + 8
PANEL = 8
ROWS = 16

damping = 0.1

VMEM = pl.BlockSpec(memory_space=pltpu.VMEM)
SMEM = pl.BlockSpec(memory_space=pltpu.SMEM)
HBM = pl.BlockSpec(memory_space=pl.ANY)


def call(kernel, outs, in_specs, scratch=(), vmem=48, flops=0, moved=0):
    return pl.pallas_call(
        kernel,
        out_shape=outs,
        in_specs=in_specs,
        scratch_shapes=list(scratch),
        compiler_params=pltpu.CompilerParams(vmem_limit_bytes=vmem << 20),
        cost_estimate=pl.CostEstimate(flops=flops, bytes_accessed=moved, transcendentals=0),
    )


def swapped(shard, axis, by):
    return lax.ppermute(shard, axis, [(i, i ^ by) for i in range(lax.axis_size(axis))])


def square(dim):
    return lax.broadcasted_iota(jnp.int32, (FBLK, FBLK), dim)


def halves(value):
    high = value.astype(jnp.bfloat16)
    return high, (value - high.astype(jnp.float32)).astype(jnp.bfloat16)


def pack(first, second, spare=None):
    row, col = square(0), square(1)
    body = jnp.where(row >= col, first, second)
    diagonal = jnp.sum(jnp.where(row == col, second, 0.0), axis=0, keepdims=True)
    place = lax.broadcasted_iota(jnp.int32, (8, FBLK), 0)
    tail = jnp.where(place == 0, diagonal, 0.0)
    if spare is not None:
        tail = jnp.where(place == 1, spare, tail)
    return body, tail


def unpack(body, diagonal):
    row, col = square(0), square(1)
    turned = body.T
    first = jnp.where(row >= col, body, turned)
    second = jnp.where(row < col, body, jnp.where(row > col, turned, diagonal))
    return first, second


def grams(lengths, train, slabs):
    cycle = len(slabs)
    mine, half = lax.axis_index("dp"), lax.axis_index("rep")
    spare = lengths[...].astype(jnp.float32)
    for shift, slab in enumerate(slabs):
        owner = half * cycle + (mine ^ shift)
        start = pl.multiple_of(owner * (2 * FBLK), 2 * FBLK)
        part = train[:, pl.ds(start, 2 * FBLK)]
        gram = lax.dot_general(part, part, (((0,), (0,)), ((), ())), preferred_element_type=jnp.float32)
        body, tail = pack(gram[:FBLK, :FBLK], gram[FBLK:, FBLK:], spare)
        slab[pl.ds(0, FBLK), :] = body
        slab[pl.ds(FBLK, 8), :] = tail


def thirds(value):
    high = value.astype(jnp.bfloat16)
    rest = value - high.astype(jnp.float32)
    middle = rest.astype(jnp.bfloat16)
    return high, middle, (rest - middle.astype(jnp.float32)).astype(jnp.bfloat16)


def at_rows(panel, first):
    pair = 2 * PANEL
    blank = jnp.zeros((PANEL, FBLK), jnp.float32)
    panel = panel.astype(jnp.float32)
    piece = jnp.concatenate([panel, blank] if first % pair == 0 else [blank, panel], axis=0).astype(jnp.bfloat16)
    before = first // pair * pair
    pieces = [jnp.zeros((before, FBLK), jnp.bfloat16), piece, jnp.zeros((FBLK - before - pair, FBLK), jnp.bfloat16)]
    return jnp.concatenate([piece for piece in pieces if piece.shape[0]], axis=0)


def product(left, right, first):
    high, middle, low = thirds(left)
    right_high, right_middle, right_low = (at_rows(part, first) for part in thirds(right))
    both = jnp.concatenate([right_high, right_middle], axis=1)
    large = jnp.dot(
        jnp.concatenate([high, middle], axis=1), jnp.concatenate([both, both], axis=0),
        preferred_element_type=jnp.float32,
    )
    small = jnp.dot(
        jnp.concatenate([high, low], axis=1), jnp.concatenate([right_low, right_high], axis=0),
        preferred_element_type=jnp.float32,
    )
    return large[:, :FBLK] + (large[:, FBLK:] + small)


def eliminated(panel, first):
    lane = lax.broadcasted_iota(jnp.int32, (PANEL, FBLK), 1)
    sublane = lax.broadcasted_iota(jnp.int32, (PANEL, FBLK), 0)
    within = (lane >= first) & (lane < first + PANEL)
    count = range(PANEL)

    def across(value, row):
        return jnp.broadcast_to(value[row:row + 1, :], (PANEL, FBLK))

    columns = [jnp.broadcast_to(panel[:, first + j:first + j + 1], (PANEL, FBLK)) for j in count]
    pivots = [[across(columns[j], i) if j >= i else None for j in count] for i in count]
    rest = jnp.where(within, jnp.where(lane == first + sublane, 1.0, 0.0), panel)
    lines = [across(rest, i) for i in count]
    for i in count:
        scale = 1.0 / pivots[i][i]
        scaled = lines[i] * scale
        shares = [pivots[i][j] * scale if j > i else None for j in count]
        for m in range(i + 1, PANEL):
            lines[m] = lines[m] - pivots[i][m] * scaled
            for j in range(m, PANEL):
                pivots[m][j] = pivots[m][j] - shares[m] * pivots[i][j]
        lines[i] = scaled
        pivots[i] = shares
    for i in reversed(count):
        for m in range(i):
            lines[m] = lines[m] - pivots[m][i] * lines[i]
    result = lines[0]
    for i in range(1, PANEL):
        result = jnp.where(sublane == i, lines[i], result)
    return result


def inverted(blocks):
    lane = square(1)
    for first in range(0, FBLK, PANEL):
        within = (lane >= first) & (lane < first + PANEL)
        panels = [eliminated(block[first:first + PANEL, :], first) for block in blocks]
        updates = [product(block, panel, first) for block, panel in zip(blocks, panels)]
        rests = [jnp.where(within, 0.0, block) - update for block, update in zip(blocks, updates)]
        blocks = [
            jnp.concatenate(
                [part for part in (rest[:first], panel, rest[first + PANEL:]) if part.shape[0]], axis=0
            )
            for rest, panel in zip(rests, panels)
        ]
    return blocks


def factor_kernel(examples, scale, *refs):
    slabs, out = refs[:-2], refs[-1]
    body = slabs[0][pl.ds(0, FBLK), :]
    diagonal = slabs[0][pl.ds(FBLK, 1), :]
    for slab in slabs[1:]:
        body = body + slab[pl.ds(0, FBLK), :]
        diagonal = diagonal + slab[pl.ds(FBLK, 1), :]
    same = square(0) == square(1)
    damped = []
    for gram in unpack(body, diagonal):
        fisher = gram / examples
        trace = jnp.sum(jnp.sum(jnp.where(same, fisher, 0.0), axis=0, keepdims=True), axis=1, keepdims=True)
        damped.append(fisher + jnp.where(same, damping * (trace / FBLK), 0.0))
    first, second = inverted(damped)
    body, tail = pack(first * scale, second * scale)
    out[pl.ds(0, FBLK), :] = body
    out[pl.ds(FBLK, 8), :] = tail


def first_kernel(id_rows_hbm, delta_hbm, table_hbm, factor_hbm, lengths_hbm, train_hbm, sent, own, *refs):
    slabs, refs = refs[:-12], refs[-12:]
    id_rows, starts, rolls, start_of, roll_of, delta, table, factor, lengths, train, looked, sems = refs
    model = lax.axis_index("mp")
    proj, vocab_rows = table.shape
    tokens = delta.shape[0]
    each = proj // lax.axis_size("mp")
    groups = tokens // FBLK
    get_ids, get_factor, get_lengths, get_train = (
        pltpu.make_async_copy(source, target, sems.at[0, index])
        for index, (source, target) in enumerate((
            (id_rows_hbm, id_rows), (factor_hbm, factor), (lengths_hbm, lengths), (train_hbm, train),
        ))
    )
    get_table = [
        pltpu.make_async_copy(table_hbm.at[rows], table.at[rows], sems.at[1, index])
        for index in range(proj // ROWS) for rows in (pl.ds(index * ROWS, ROWS),)
    ]

    def get_delta(g):
        rows = pl.ds(pl.multiple_of(g * FBLK, FBLK), FBLK)
        return pltpu.make_async_copy(delta_hbm.at[rows], delta.at[rows], sems.at[2, g])

    for copy in (get_ids, get_lengths, get_train, *get_table, get_factor, *(get_delta(g) for g in range(groups))):
        copy.start()
    get_ids.wait()
    local = id_rows[...] - model * vocab_rows
    owned = (local >= 0) & (local < vocab_rows)
    local = jnp.where(owned, local, 0)
    low = FBLK - 1
    starts[...] = local & ~low
    rolls[...] = (lax.broadcasted_iota(jnp.int32, local.shape, 1) - local) & low
    fetches = [pltpu.make_async_copy(starts, start_of, sems.at[0, 4]), pltpu.make_async_copy(rolls, roll_of, sems.at[0, 5])]
    for fetch in fetches:
        fetch.start()
    get_lengths.wait()
    get_train.wait()
    grams(lengths, train, slabs)
    for fetch in fetches:
        fetch.wait()
    starts[...] = owned.astype(jnp.int32)
    for copy in get_table:
        copy.wait()
    get_factor.wait()
    lanes = lax.broadcasted_iota(jnp.int32, (ROWS, FBLK), 1)

    def group(g, carry):
        columns = pl.ds(pl.multiple_of(g * FBLK, FBLK), FBLK)
        get_delta(g).wait()
        output = lax.dot_general(
            delta[columns, :], factor[...], (((1,), (1,)), ((), ())), preferred_element_type=jnp.float32
        )
        looked[:, columns] = output.T
        gathered = [jnp.zeros((ROWS, FBLK), jnp.bfloat16) for _ in range(proj // ROWS)]
        for j in range(FBLK):
            start, by, here = pl.multiple_of(start_of[g, j], FBLK), roll_of[g, j], lanes == j
            for index in range(proj // ROWS):
                block = table[pl.ds(index * ROWS, ROWS), pl.ds(start, FBLK)]
                gathered[index] = jnp.where(here, pltpu.roll(block, by, 1), gathered[index])
        held = starts[pl.ds(g, 1), :].astype(jnp.float32)
        for index, value in enumerate(gathered):
            value = (value.astype(jnp.float32) * held).astype(jnp.bfloat16)
            rows = pl.ds(2 * each + index * ROWS, ROWS)
            sent[rows, columns] = value
            own[rows, columns] = value
        return carry

    lax.fori_loop(0, groups, group, 0)
    mine = looked[pl.ds(pl.multiple_of(model * each, each), each), :]
    other = looked[pl.ds(pl.multiple_of((1 - model) * each, each), each), :]
    for target, value in ((own, mine), (sent, other)):
        high, rest = halves(value)
        target[pl.ds(0, each), :] = high
        target[pl.ds(each, each), :] = rest


def merge_kernel(each, own, got, out):
    def value(ref):
        return ref[pl.ds(0, each), :].astype(jnp.float32) + ref[pl.ds(each, each), :].astype(jnp.float32)

    high, low = halves(value(own) + value(got))
    out[pl.ds(0, each), :] = high
    out[pl.ds(each, each), :] = low
    rows = pl.ds(2 * each, out.shape[0] - 2 * each)
    out[rows, :] = own[rows, :] + got[rows, :]


def queries_kernel(each, ends_of, factors, slab, *refs):
    far, refs = (refs[0], refs[1:]) if ends_of else (None, refs)
    high_out, low_out = refs[-2:]
    if len(refs) == 4:
        source, high_out, low_out, copy = refs
        copy[...] = source[...]
    tokens = factors.shape[1]
    proj = factors.shape[0] - 2 * each
    queries = high_out.shape[1]
    mine = lax.axis_index("dp")

    def part(first, count):
        value = factors[pl.ds(first, count), :].astype(jnp.float32)
        if ends_of:
            at_end = (mine == 0) | (mine == ends_of - 1)
            value = jnp.where(at_end, far[pl.ds(first, count), :].astype(jnp.float32), value)
        return value

    lengths = slab[pl.ds(FBLK + 1, 1), :]
    upto = jnp.where(square(0) <= square(1), 1.0, 0.0).astype(jnp.bfloat16)
    ends = lax.dot_general(
        jnp.broadcast_to(lengths, (8, queries)).astype(jnp.bfloat16), upto, (((1,), (0,)), ((), ())),
        preferred_element_type=jnp.float32,
    )[:1]
    starts = ends - lengths
    place = lax.broadcasted_iota(jnp.int32, (tokens, queries), 0).astype(jnp.float32)
    inside = jnp.where((place >= starts) & (place < ends), 1.0, 0.0).astype(jnp.bfloat16)
    output = part(0, each) + part(each, each)
    inputs = part(2 * each, proj)
    step = 8
    for start in range(0, each, step):
        grads = jnp.concatenate(
            [(inputs * output[r:r + 1, :]).astype(jnp.bfloat16) for r in range(start, start + step)], axis=0
        )
        summed = jnp.dot(grads, inside, preferred_element_type=jnp.float32)
        high, low = halves(summed)
        high_out[pl.ds(start * proj, step * proj), :] = high
        low_out[pl.ds(start * proj, step * proj), :] = low


def hand_kernel(count, *refs):
    for source, copy in zip(refs[:count], refs[-count:]):
        copy[...] = source[...]


def scores_kernel(cycle, count, *refs):
    own, peers = refs[:cycle], refs[cycle:2 * cycle]
    highs, lows = refs[2 * cycle:2 * cycle + count], refs[2 * cycle + count:2 * cycle + 2 * count]
    train, sent, kept, pre = refs[2 * cycle + 2 * count:]
    mine, rep, model = lax.axis_index("dp"), lax.axis_index("rep"), lax.axis_index("mp")
    for half, slabs in ((rep, own), (1 - rep, peers)):
        for shift in range(cycle):
            owner = half * cycle + (mine ^ shift)
            slab = slabs[shift]
            blocks = unpack(slab[pl.ds(0, FBLK), :], slab[pl.ds(FBLK, 1), :])
            for index, block in enumerate(blocks):
                rows = pl.ds(pl.multiple_of(owner * (2 * FBLK) + index * FBLK, FBLK), FBLK)
                high, low = halves(block)
                right_high = jnp.concatenate([ref[rows, :] for ref in highs], axis=1)
                right_low = jnp.concatenate([ref[rows, :] for ref in lows], axis=1)
                solved = jnp.dot(
                    jnp.concatenate([high, high, low], axis=1),
                    jnp.concatenate([right_high, right_low, right_high], axis=0),
                    preferred_element_type=jnp.float32,
                )
                pre[rows, :] = solved.astype(jnp.bfloat16)
    half_rows = sent.shape[0]
    for out, which in ((sent, 1 - model), (kept, model)):
        rows = pl.ds(pl.multiple_of(which * half_rows, half_rows), half_rows)
        out[...] = jnp.dot(train[rows, :], pre[...], preferred_element_type=jnp.float32).astype(jnp.bfloat16)


def total_kernel(order, *refs):
    pieces, out = refs[:-1], refs[-1]
    mine, cycle = lax.axis_index("dp"), len(order)
    sums = {}
    for kept, got in zip(pieces[::2], pieces[1::2]):
        both = kept[...].astype(jnp.float32) + got[...].astype(jnp.float32)
        for index in range(both.shape[1] // FBLK):
            sums[order[len(sums)]] = both[:, index * FBLK:(index + 1) * FBLK]
    placed = []
    for source in range(cycle):
        shift = mine ^ source
        value = sums[0]
        for index in range(1, cycle):
            value = jnp.where(shift == index, sums[index], value)
        placed.append(value)
    out[...] = jnp.concatenate(placed, axis=1).astype(jnp.bfloat16)


def shape(dims, dtype):
    return jax.ShapeDtypeStruct(dims, dtype)


def split_over_blocks(query_ids, query_delta, doc_lengths, vocab_factor, output_factor, train_grads):
    cycle = lax.axis_size("dp")
    tokens, width = query_delta.shape
    proj = output_factor.shape[1]
    each = proj // lax.axis_size("mp")
    vocab_rows = vocab_factor.shape[0]
    train_rows, feat = train_grads.shape
    queries = doc_lengths.shape[1]
    bf16, f32 = jnp.bfloat16, jnp.float32

    sent, own, *slabs = call(
        first_kernel,
        [shape((2 * each + proj, tokens), bf16)] * 2 + [shape((SLAB, FBLK), f32)] * cycle,
        [HBM] * 6,
        [
            pltpu.VMEM((tokens // FBLK, FBLK), jnp.int32),
            pltpu.VMEM((tokens // FBLK, FBLK), jnp.int32),
            pltpu.VMEM((tokens // FBLK, FBLK), jnp.int32),
            pltpu.SMEM((tokens // FBLK, FBLK), jnp.int32),
            pltpu.SMEM((tokens // FBLK, FBLK), jnp.int32),
            pltpu.VMEM((tokens, width), bf16),
            pltpu.VMEM((proj, vocab_rows), bf16),
            pltpu.VMEM((proj, width), bf16),
            pltpu.VMEM((1, queries), jnp.int32),
            pltpu.VMEM((train_rows, feat), bf16),
            pltpu.VMEM((proj, tokens), f32),
            pltpu.SemaphoreType.DMA((3, 8)),
        ],
        vmem=62,
        flops=2 * tokens * width * proj,
        moved=2 * (tokens * width + proj * vocab_rows) * 2,
    )(
        query_ids.reshape(tokens // FBLK, FBLK), query_delta, vocab_factor.T, output_factor.T,
        doc_lengths, train_grads,
    )
    got = swapped(sent, "mp", 1)
    own, kept = call(
        functools.partial(hand_kernel, 2),
        [shape(own.shape, bf16), shape((SLAB, FBLK), f32)],
        [VMEM, VMEM],
        vmem=16,
        moved=4 * own.size,
    )(own, slabs[0])
    parts = [kept] + [swapped(slabs[s], "dp", s) for s in range(1, cycle)]

    factors = call(
        functools.partial(merge_kernel, each),
        shape(sent.shape, bf16),
        [VMEM, VMEM],
        vmem=16,
        flops=tokens * each,
        moved=8 * tokens * each * 4,
    )(own, got)
    late = cycle - 1
    gathered = [factors] + [swapped(factors, "dp", s) if s != late else None for s in range(1, cycle)]

    inverse = call(
        functools.partial(factor_kernel, train_rows * cycle, 1.0 / proj),
        shape((SLAB, FBLK), f32),
        [VMEM] * cycle + [HBM],
        vmem=16,
        flops=10 ** 10,
        moved=10 ** 6,
    )(*parts, factors)
    inverses = [inverse] + [swapped(inverse, "dp", s) for s in range(1, cycle)]
    copies = {0: [inverse], 1: [factors], 2: [gathered[2]]}
    highs, lows, far = {}, {}, []
    for s in range(cycle):
        extra = copies.get(s, far)
        copied = s in (1, 2)
        highs[s], lows[s], *again = call(
            functools.partial(queries_kernel, each, cycle if s == late else 0),
            [shape((feat, queries), bf16)] * 2 + [shape(factors.shape, bf16)] * copied,
            [VMEM, VMEM] + [HBM if s == 0 else VMEM] * len(extra),
            vmem=24,
            flops=2 * feat * tokens * queries,
            moved=6 * feat * queries,
        )(gathered[s], parts[s], *extra)
        if s == 1:
            gathered[late] = lax.ppermute(again[0], "dp", [(1, 2), (2, 1)])
        if s == 2:
            far = [lax.ppermute(again[0], "dp", [(1, 0), (2, 3)])]
    handed = list(inverses)
    handed[late] = call(
        functools.partial(hand_kernel, 1),
        shape((SLAB, FBLK), f32),
        [VMEM] + [HBM] * (cycle - 1),
        vmem=16,
        moved=8 * SLAB * FBLK,
    )(inverses[late], *[highs[s] for s in range(cycle) if s != late])
    peers = [swapped(slab, "rep", 1) for slab in handed]

    half_rows = train_rows // lax.axis_size("mp")
    pieces, order = [], []
    for chosen in ([s for s in range(cycle) if s != late], [late]):
        count = len(chosen)
        outgoing, kept = call(
            functools.partial(scores_kernel, cycle, count),
            [shape((half_rows, count * queries), bf16)] * 2,
            [VMEM] * (2 * cycle + 2 * count + 1),
            [pltpu.VMEM((feat, count * queries), bf16)],
            vmem=24,
            flops=2 * train_rows * feat * count * queries,
            moved=8 * feat * queries * count,
        )(*inverses, *peers, *[highs[s] for s in chosen], *[lows[s] for s in chosen], train_grads)
        pieces += [kept, swapped(outgoing, "mp", 1)]
        order += chosen
    total = call(
        functools.partial(total_kernel, order),
        shape((half_rows, cycle * queries), bf16),
        [VMEM] * len(pieces),
        vmem=16,
        flops=half_rows * cycle * queries,
        moved=6 * half_rows * cycle * queries,
    )(*pieces)
    return total.reshape(half_rows, cycle, 1, queries)


def doc_matrix(lengths_row, count):
    ends = jnp.cumsum(lengths_row)
    starts = ends - lengths_row
    place = jnp.arange(count, dtype=jnp.int32)
    inside = (place[None, :] >= starts[:, None]) & (place[None, :] < ends[:, None])
    return inside.astype(jnp.bfloat16)


def solve_block(factor, rhs):
    return jax.scipy.linalg.cho_solve((factor, True), rhs)


def general(query_ids, query_delta, doc_lengths, vocab_factor, output_factor, train_grads):
    model_count = lax.axis_size("mp")
    model_index = lax.axis_index("mp")
    vocab_rows = vocab_factor.shape[0]
    local_ids = query_ids - model_index * vocab_rows
    owned = (local_ids >= 0) & (local_ids < vocab_rows)
    looked = vocab_factor[jnp.clip(local_ids, 0, vocab_rows - 1)].astype(jnp.float32)
    vocab_part = jnp.where(owned[:, None], looked, jnp.zeros_like(looked))
    output_part = jnp.dot(query_delta, output_factor, preferred_element_type=jnp.float32)
    input_side, output_side = lax.psum((vocab_part, output_part), "mp")
    proj = output_side.shape[1]
    rows_each = proj // model_count
    mine = lax.dynamic_slice_in_dim(output_side, model_index * rows_each, rows_each, 1)
    token_count = query_ids.shape[0]
    token_grads = (
        (mine[:, :, None] * input_side[:, None, :])
        .reshape(token_count, rows_each * proj)
        .astype(jnp.bfloat16)
    )
    query_grads = jnp.dot(
        doc_matrix(doc_lengths[0], token_count), token_grads, preferred_element_type=jnp.float32
    )
    train_rows, feat_dev = train_grads.shape
    nblocks = feat_dev // FBLK
    tiled = train_grads.reshape(train_rows, nblocks, FBLK)
    local_gram = jnp.einsum("tbi,tbj->bij", tiled, tiled, preferred_element_type=jnp.float32)
    total_gram = lax.psum(local_gram, "dp")
    fisher = total_gram / (train_rows * lax.axis_size("dp"))
    shift_amount = damping * (jnp.trace(fisher, axis1=1, axis2=2) / FBLK)
    damped = fisher + shift_amount[:, None, None] * jnp.eye(FBLK, dtype=jnp.float32)[None]
    factor = jnp.linalg.cholesky(damped)
    queries = query_grads.shape[0]
    rhs = jnp.transpose(query_grads.reshape(queries, nblocks, FBLK), (1, 2, 0))
    solved = jax.vmap(solve_block)(factor, rhs)
    pre = (jnp.transpose(solved, (2, 0, 1)).reshape(queries, feat_dev) / proj).astype(jnp.bfloat16)
    cycle = lax.axis_size("dp")
    everyone = lax.all_gather(pre, "dp", axis=0, tiled=True)
    scores = lax.dot_general(
        train_grads, everyone, (((1,), (1,)), ((), ())), preferred_element_type=jnp.float32
    )
    scores = scores.astype(jnp.bfloat16).reshape(train_rows, cycle, queries)
    summed = lax.psum_scatter(scores, "mp", scatter_dimension=0, tiled=True)
    return summed[:, :, None, :]


def per_device(query_ids, query_delta, doc_lengths, vocab_factor, output_factor, train_grads):
    owners = lax.axis_size("dp") * lax.axis_size("rep")
    fits = (
        train_grads.shape[1] == 2 * FBLK * owners
        and lax.axis_size("dp") == 4
        and lax.axis_size("mp") == 2
        and lax.axis_size("rep") == 2
        and doc_lengths.shape[1] == FBLK
        and vocab_factor.shape[0] % FBLK == 0
    )
    body = split_over_blocks if fits else general
    return body(query_ids, query_delta, doc_lengths, vocab_factor, output_factor, train_grads)


def solution(mesh):
    placed = (
        P(("groups", "dp", "rep")),
        P(("groups", "dp", "rep"), "mp"),
        P(("groups", "dp", "rep"), None),
        P("mp", None),
        P("mp", None),
        P(("groups", "dp"), "mp"),
    )
    return jax.shard_map(
        per_device,
        mesh=mesh,
        in_specs=placed,
        out_specs=P(("groups", "dp", "mp"), None, "rep", None),
        check_vma=False,
    )
```

```python
import functools
import jax
import jax.numpy as jnp
from jax import lax
from jax.experimental import pallas as pl
from jax.experimental.pallas import tpu as pltpu
from jax.sharding import PartitionSpec as P

FBLK = 128
SLAB = FBLK + 8
PANEL = 8
ROWS = 16

damping = 0.1

VMEM = pl.BlockSpec(memory_space=pltpu.VMEM)
SMEM = pl.BlockSpec(memory_space=pltpu.SMEM)
HBM = pl.BlockSpec(memory_space=pl.ANY)


def call(kernel, outs, in_specs, scratch=(), vmem=48, flops=0, moved=0):
    return pl.pallas_call(
        kernel,
        out_shape=outs,
        in_specs=in_specs,
        scratch_shapes=list(scratch),
        compiler_params=pltpu.CompilerParams(vmem_limit_bytes=vmem << 20),
        cost_estimate=pl.CostEstimate(flops=flops, bytes_accessed=moved, transcendentals=0),
    )


def swapped(shard, axis, by):
    return lax.ppermute(shard, axis, [(i, i ^ by) for i in range(lax.axis_size(axis))])


def square(dim):
    return lax.broadcasted_iota(jnp.int32, (FBLK, FBLK), dim)


def halves(value):
    high = value.astype(jnp.bfloat16)
    return high, (value - high.astype(jnp.float32)).astype(jnp.bfloat16)


def pack(first, second, spare=None):
    row, col = square(0), square(1)
    body = jnp.where(row >= col, first, second)
    diagonal = jnp.sum(jnp.where(row == col, second, 0.0), axis=0, keepdims=True)
    place = lax.broadcasted_iota(jnp.int32, (8, FBLK), 0)
    tail = jnp.where(place == 0, diagonal, 0.0)
    if spare is not None:
        tail = jnp.where(place == 1, spare, tail)
    return body, tail


def unpack(body, diagonal):
    row, col = square(0), square(1)
    turned = body.T
    first = jnp.where(row >= col, body, turned)
    second = jnp.where(row < col, body, jnp.where(row > col, turned, diagonal))
    return first, second


def grams(lengths, train, slabs):
    cycle = len(slabs)
    mine, half = lax.axis_index("dp"), lax.axis_index("rep")
    spare = lengths[...].astype(jnp.float32)
    for shift, slab in enumerate(slabs):
        owner = half * cycle + (mine ^ shift)
        start = pl.multiple_of(owner * (2 * FBLK), 2 * FBLK)
        part = train[:, pl.ds(start, 2 * FBLK)]
        gram = lax.dot_general(part, part, (((0,), (0,)), ((), ())), preferred_element_type=jnp.float32)
        body, tail = pack(gram[:FBLK, :FBLK], gram[FBLK:, FBLK:], spare)
        slab[pl.ds(0, FBLK), :] = body
        slab[pl.ds(FBLK, 8), :] = tail


def thirds(value):
    high = value.astype(jnp.bfloat16)
    rest = value - high.astype(jnp.float32)
    middle = rest.astype(jnp.bfloat16)
    return high, middle, (rest - middle.astype(jnp.float32)).astype(jnp.bfloat16)


def at_rows(panel, first):
    pair = 2 * PANEL
    blank = jnp.zeros((PANEL, FBLK), jnp.float32)
    panel = panel.astype(jnp.float32)
    piece = jnp.concatenate([panel, blank] if first % pair == 0 else [blank, panel], axis=0).astype(jnp.bfloat16)
    before = first // pair * pair
    pieces = [jnp.zeros((before, FBLK), jnp.bfloat16), piece, jnp.zeros((FBLK - before - pair, FBLK), jnp.bfloat16)]
    return jnp.concatenate([piece for piece in pieces if piece.shape[0]], axis=0)


def product(left, right, first):
    high, middle, low = thirds(left)
    right_high, right_middle, right_low = (at_rows(part, first) for part in thirds(right))
    both = jnp.concatenate([right_high, right_middle], axis=1)
    large = jnp.dot(
        jnp.concatenate([high, middle], axis=1), jnp.concatenate([both, both], axis=0),
        preferred_element_type=jnp.float32,
    )
    small = jnp.dot(
        jnp.concatenate([high, low], axis=1), jnp.concatenate([right_low, right_high], axis=0),
        preferred_element_type=jnp.float32,
    )
    return large[:, :FBLK] + (large[:, FBLK:] + small)


def eliminated(panel, first):
    lane = lax.broadcasted_iota(jnp.int32, (PANEL, FBLK), 1)
    sublane = lax.broadcasted_iota(jnp.int32, (PANEL, FBLK), 0)
    within = (lane >= first) & (lane < first + PANEL)
    count = range(PANEL)

    def across(value, row):
        return jnp.broadcast_to(value[row:row + 1, :], (PANEL, FBLK))

    columns = [jnp.broadcast_to(panel[:, first + j:first + j + 1], (PANEL, FBLK)) for j in count]
    pivots = [[across(columns[j], i) if j >= i else None for j in count] for i in count]
    rest = jnp.where(within, jnp.where(lane == first + sublane, 1.0, 0.0), panel)
    lines = [across(rest, i) for i in count]
    for i in count:
        scale = 1.0 / pivots[i][i]
        scaled = lines[i] * scale
        shares = [pivots[i][j] * scale if j > i else None for j in count]
        for m in range(i + 1, PANEL):
            lines[m] = lines[m] - pivots[i][m] * scaled
            for j in range(m, PANEL):
                pivots[m][j] = pivots[m][j] - shares[m] * pivots[i][j]
        lines[i] = scaled
        pivots[i] = shares
    for i in reversed(count):
        for m in range(i):
            lines[m] = lines[m] - pivots[m][i] * lines[i]
    result = lines[0]
    for i in range(1, PANEL):
        result = jnp.where(sublane == i, lines[i], result)
    return result


def inverted(blocks):
    lane = square(1)
    for first in range(0, FBLK, PANEL):
        within = (lane >= first) & (lane < first + PANEL)
        panels = [eliminated(block[first:first + PANEL, :], first) for block in blocks]
        updates = [product(block, panel, first) for block, panel in zip(blocks, panels)]
        rests = [jnp.where(within, 0.0, block) - update for block, update in zip(blocks, updates)]
        blocks = [
            jnp.concatenate(
                [part for part in (rest[:first], panel, rest[first + PANEL:]) if part.shape[0]], axis=0
            )
            for rest, panel in zip(rests, panels)
        ]
    return blocks


def factor_kernel(examples, scale, *refs):
    slabs, out = refs[:-2], refs[-1]
    body = slabs[0][pl.ds(0, FBLK), :]
    diagonal = slabs[0][pl.ds(FBLK, 1), :]
    for slab in slabs[1:]:
        body = body + slab[pl.ds(0, FBLK), :]
        diagonal = diagonal + slab[pl.ds(FBLK, 1), :]
    same = square(0) == square(1)
    damped = []
    for gram in unpack(body, diagonal):
        fisher = gram / examples
        trace = jnp.sum(jnp.sum(jnp.where(same, fisher, 0.0), axis=0, keepdims=True), axis=1, keepdims=True)
        damped.append(fisher + jnp.where(same, damping * (trace / FBLK), 0.0))
    first, second = inverted(damped)
    body, tail = pack(first * scale, second * scale)
    out[pl.ds(0, FBLK), :] = body
    out[pl.ds(FBLK, 8), :] = tail


def first_kernel(id_rows_hbm, delta_hbm, table_hbm, factor_hbm, lengths_hbm, train_hbm, sent, own, *refs):
    slabs, refs = refs[:-12], refs[-12:]
    id_rows, starts, rolls, start_of, roll_of, delta, table, factor, lengths, train, looked, sems = refs
    model = lax.axis_index("mp")
    proj, vocab_rows = table.shape
    tokens = delta.shape[0]
    each = proj // lax.axis_size("mp")
    groups = tokens // FBLK
    get_ids, get_factor, get_lengths, get_train = (
        pltpu.make_async_copy(source, target, sems.at[0, index])
        for index, (source, target) in enumerate((
            (id_rows_hbm, id_rows), (factor_hbm, factor), (lengths_hbm, lengths), (train_hbm, train),
        ))
    )
    get_table = [
        pltpu.make_async_copy(table_hbm.at[rows], table.at[rows], sems.at[1, index])
        for index in range(proj // ROWS) for rows in (pl.ds(index * ROWS, ROWS),)
    ]

    def get_delta(g):
        rows = pl.ds(pl.multiple_of(g * FBLK, FBLK), FBLK)
        return pltpu.make_async_copy(delta_hbm.at[rows], delta.at[rows], sems.at[2, g])

    for copy in (get_ids, get_lengths, get_train, *get_table, get_factor, *(get_delta(g) for g in range(groups))):
        copy.start()
    get_ids.wait()
    local = id_rows[...] - model * vocab_rows
    owned = (local >= 0) & (local < vocab_rows)
    local = jnp.where(owned, local, 0)
    low = FBLK - 1
    starts[...] = local & ~low
    rolls[...] = (lax.broadcasted_iota(jnp.int32, local.shape, 1) - local) & low
    fetches = [pltpu.make_async_copy(starts, start_of, sems.at[0, 4]), pltpu.make_async_copy(rolls, roll_of, sems.at[0, 5])]
    for fetch in fetches:
        fetch.start()
    get_lengths.wait()
    get_train.wait()
    grams(lengths, train, slabs)
    for fetch in fetches:
        fetch.wait()
    starts[...] = owned.astype(jnp.int32)
    for copy in get_table:
        copy.wait()
    get_factor.wait()
    lanes = lax.broadcasted_iota(jnp.int32, (ROWS, FBLK), 1)

    def group(g, carry):
        columns = pl.ds(pl.multiple_of(g * FBLK, FBLK), FBLK)
        get_delta(g).wait()
        output = lax.dot_general(
            delta[columns, :], factor[...], (((1,), (1,)), ((), ())), preferred_element_type=jnp.float32
        )
        looked[:, columns] = output.T
        gathered = [jnp.zeros((ROWS, FBLK), jnp.bfloat16) for _ in range(proj // ROWS)]
        for j in range(FBLK):
            start, by, here = pl.multiple_of(start_of[g, j], FBLK), roll_of[g, j], lanes == j
            for index in range(proj // ROWS):
                block = table[pl.ds(index * ROWS, ROWS), pl.ds(start, FBLK)]
                gathered[index] = jnp.where(here, pltpu.roll(block, by, 1), gathered[index])
        held = starts[pl.ds(g, 1), :].astype(jnp.float32)
        for index, value in enumerate(gathered):
            value = (value.astype(jnp.float32) * held).astype(jnp.bfloat16)
            rows = pl.ds(2 * each + index * ROWS, ROWS)
            sent[rows, columns] = value
            own[rows, columns] = value
        return carry

    lax.fori_loop(0, groups, group, 0)
    mine = looked[pl.ds(pl.multiple_of(model * each, each), each), :]
    other = looked[pl.ds(pl.multiple_of((1 - model) * each, each), each), :]
    for target, value in ((own, mine), (sent, other)):
        high, rest = halves(value)
        target[pl.ds(0, each), :] = high
        target[pl.ds(each, each), :] = rest


def merge_kernel(each, own, got, out):
    def value(ref):
        return ref[pl.ds(0, each), :].astype(jnp.float32) + ref[pl.ds(each, each), :].astype(jnp.float32)

    high, low = halves(value(own) + value(got))
    out[pl.ds(0, each), :] = high
    out[pl.ds(each, each), :] = low
    rows = pl.ds(2 * each, out.shape[0] - 2 * each)
    out[rows, :] = own[rows, :] + got[rows, :]


def queries_kernel(each, ends_of, factors, slab, *refs):
    far, refs = (refs[0], refs[1:]) if ends_of else (None, refs)
    high_out, low_out = refs[-2:]
    if len(refs) == 4:
        source, high_out, low_out, copy = refs
        copy[...] = source[...]
    tokens = factors.shape[1]
    proj = factors.shape[0] - 2 * each
    queries = high_out.shape[1]
    mine = lax.axis_index("dp")

    def part(first, count):
        value = factors[pl.ds(first, count), :].astype(jnp.float32)
        if ends_of:
            at_end = (mine == 0) | (mine == ends_of - 1)
            value = jnp.where(at_end, far[pl.ds(first, count), :].astype(jnp.float32), value)
        return value

    lengths = slab[pl.ds(FBLK + 1, 1), :]
    upto = jnp.where(square(0) <= square(1), 1.0, 0.0).astype(jnp.bfloat16)
    ends = lax.dot_general(
        jnp.broadcast_to(lengths, (8, queries)).astype(jnp.bfloat16), upto, (((1,), (0,)), ((), ())),
        preferred_element_type=jnp.float32,
    )[:1]
    starts = ends - lengths
    place = lax.broadcasted_iota(jnp.int32, (tokens, queries), 0).astype(jnp.float32)
    inside = jnp.where((place >= starts) & (place < ends), 1.0, 0.0).astype(jnp.bfloat16)
    output = part(0, each) + part(each, each)
    inputs = part(2 * each, proj)
    step = 8
    for start in range(0, each, step):
        grads = jnp.concatenate(
            [(inputs * output[r:r + 1, :]).astype(jnp.bfloat16) for r in range(start, start + step)], axis=0
        )
        summed = jnp.dot(grads, inside, preferred_element_type=jnp.float32)
        high, low = halves(summed)
        high_out[pl.ds(start * proj, step * proj), :] = high
        low_out[pl.ds(start * proj, step * proj), :] = low


def hand_kernel(count, *refs):
    for source, copy in zip(refs[:count], refs[-count:]):
        copy[...] = source[...]


def scores_kernel(cycle, count, *refs):
    own, peers = refs[:cycle], refs[cycle:2 * cycle]
    highs, lows = refs[2 * cycle:2 * cycle + count], refs[2 * cycle + count:2 * cycle + 2 * count]
    train, sent, pre = refs[2 * cycle + 2 * count:]
    mine, rep, model = lax.axis_index("dp"), lax.axis_index("rep"), lax.axis_index("mp")
    for half, slabs in ((rep, own), (1 - rep, peers)):
        for shift in range(cycle):
            owner = half * cycle + (mine ^ shift)
            slab = slabs[shift]
            blocks = unpack(slab[pl.ds(0, FBLK), :], slab[pl.ds(FBLK, 1), :])
            for index, block in enumerate(blocks):
                rows = pl.ds(pl.multiple_of(owner * (2 * FBLK) + index * FBLK, FBLK), FBLK)
                high, low = halves(block)
                right_high = jnp.concatenate([ref[rows, :] for ref in highs], axis=1)
                right_low = jnp.concatenate([ref[rows, :] for ref in lows], axis=1)
                solved = jnp.dot(
                    jnp.concatenate([high, high, low], axis=1),
                    jnp.concatenate([right_high, right_low, right_high], axis=0),
                    preferred_element_type=jnp.float32,
                )
                pre[rows, :] = solved.astype(jnp.bfloat16)
    half_rows = sent.shape[0]
    rows = pl.ds(pl.multiple_of((1 - model) * half_rows, half_rows), half_rows)
    sent[...] = jnp.dot(train[rows, :], pre[...], preferred_element_type=jnp.float32).astype(jnp.bfloat16)


def kept_kernel(train, pre, kept):
    half_rows = kept.shape[0]
    rows = pl.ds(pl.multiple_of(lax.axis_index("mp") * half_rows, half_rows), half_rows)
    kept[...] = jnp.dot(train[rows, :], pre[...], preferred_element_type=jnp.float32).astype(jnp.bfloat16)


def total_kernel(order, *refs):
    pieces, out = refs[:-1], refs[-1]
    mine, cycle = lax.axis_index("dp"), len(order)
    sums = {}
    for kept, got in zip(pieces[::2], pieces[1::2]):
        both = kept[...].astype(jnp.float32) + got[...].astype(jnp.float32)
        for index in range(both.shape[1] // FBLK):
            sums[order[len(sums)]] = both[:, index * FBLK:(index + 1) * FBLK]
    placed = []
    for source in range(cycle):
        shift = mine ^ source
        value = sums[0]
        for index in range(1, cycle):
            value = jnp.where(shift == index, sums[index], value)
        placed.append(value)
    out[...] = jnp.concatenate(placed, axis=1).astype(jnp.bfloat16)


def shape(dims, dtype):
    return jax.ShapeDtypeStruct(dims, dtype)


def split_over_blocks(query_ids, query_delta, doc_lengths, vocab_factor, output_factor, train_grads):
    cycle = lax.axis_size("dp")
    tokens, width = query_delta.shape
    proj = output_factor.shape[1]
    each = proj // lax.axis_size("mp")
    vocab_rows = vocab_factor.shape[0]
    train_rows, feat = train_grads.shape
    queries = doc_lengths.shape[1]
    bf16, f32 = jnp.bfloat16, jnp.float32

    sent, own, *slabs = call(
        first_kernel,
        [shape((2 * each + proj, tokens), bf16)] * 2 + [shape((SLAB, FBLK), f32)] * cycle,
        [HBM] * 6,
        [
            pltpu.VMEM((tokens // FBLK, FBLK), jnp.int32),
            pltpu.VMEM((tokens // FBLK, FBLK), jnp.int32),
            pltpu.VMEM((tokens // FBLK, FBLK), jnp.int32),
            pltpu.SMEM((tokens // FBLK, FBLK), jnp.int32),
            pltpu.SMEM((tokens // FBLK, FBLK), jnp.int32),
            pltpu.VMEM((tokens, width), bf16),
            pltpu.VMEM((proj, vocab_rows), bf16),
            pltpu.VMEM((proj, width), bf16),
            pltpu.VMEM((1, queries), jnp.int32),
            pltpu.VMEM((train_rows, feat), bf16),
            pltpu.VMEM((proj, tokens), f32),
            pltpu.SemaphoreType.DMA((3, 8)),
        ],
        vmem=62,
        flops=2 * tokens * width * proj,
        moved=2 * (tokens * width + proj * vocab_rows) * 2,
    )(
        query_ids.reshape(tokens // FBLK, FBLK), query_delta, vocab_factor.T, output_factor.T,
        doc_lengths, train_grads,
    )
    got = swapped(sent, "mp", 1)
    own, kept = call(
        functools.partial(hand_kernel, 2),
        [shape(own.shape, bf16), shape((SLAB, FBLK), f32)],
        [VMEM, VMEM],
        vmem=16,
        moved=4 * own.size,
    )(own, slabs[0])
    parts = [kept] + [swapped(slabs[s], "dp", s) for s in range(1, cycle)]

    factors = call(
        functools.partial(merge_kernel, each),
        shape(sent.shape, bf16),
        [VMEM, VMEM],
        vmem=16,
        flops=tokens * each,
        moved=8 * tokens * each * 4,
    )(own, got)
    late = cycle - 1
    gathered = [factors] + [swapped(factors, "dp", s) if s != late else None for s in range(1, cycle)]

    inverse = call(
        functools.partial(factor_kernel, train_rows * cycle, 1.0 / proj),
        shape((SLAB, FBLK), f32),
        [VMEM] * cycle + [HBM],
        vmem=16,
        flops=10 ** 10,
        moved=10 ** 6,
    )(*parts, factors)
    inverses = [inverse] + [swapped(inverse, "dp", s) for s in range(1, cycle)]
    copies = {0: [inverse], 1: [factors], 2: [gathered[2]]}
    highs, lows, far = {}, {}, []
    for s in range(cycle):
        extra = copies.get(s, far)
        copied = s in (1, 2)
        highs[s], lows[s], *again = call(
            functools.partial(queries_kernel, each, cycle if s == late else 0),
            [shape((feat, queries), bf16)] * 2 + [shape(factors.shape, bf16)] * copied,
            [VMEM, VMEM] + [HBM if s == 0 else VMEM] * len(extra),
            vmem=24,
            flops=2 * feat * tokens * queries,
            moved=6 * feat * queries,
        )(gathered[s], parts[s], *extra)
        if s == 1:
            gathered[late] = lax.ppermute(again[0], "dp", [(1, 2), (2, 1)])
        if s == 2:
            far = [lax.ppermute(again[0], "dp", [(1, 0), (2, 3)])]
    handed = list(inverses)
    handed[late] = call(
        functools.partial(hand_kernel, 1),
        shape((SLAB, FBLK), f32),
        [VMEM] + [HBM] * (cycle - 2),
        vmem=16,
        moved=8 * SLAB * FBLK,
    )(inverses[late], *[highs[s] for s in range(1, cycle) if s != late])
    peers = [swapped(slab, "rep", 1) for slab in handed]

    half_rows = train_rows // lax.axis_size("mp")
    pieces, order = [], []
    for chosen in ([s for s in range(cycle) if s != late], [late]):
        count = len(chosen)
        outgoing, solved = call(
            functools.partial(scores_kernel, cycle, count),
            [shape((half_rows, count * queries), bf16), shape((feat, count * queries), bf16)],
            [VMEM] * (2 * cycle + 2 * count + 1),
            vmem=24,
            flops=2 * train_rows * feat * count * queries,
            moved=8 * feat * queries * count,
        )(*inverses, *peers, *[highs[s] for s in chosen], *[lows[s] for s in chosen], train_grads)
        kept = call(
            kept_kernel,
            shape((half_rows, count * queries), bf16),
            [VMEM, VMEM],
            vmem=24,
            flops=train_rows * feat * count * queries,
            moved=2 * feat * (half_rows + count * queries),
        )(train_grads, solved)
        pieces += [kept, swapped(outgoing, "mp", 1)]
        order += chosen
    total = call(
        functools.partial(total_kernel, order),
        shape((half_rows, cycle * queries), bf16),
        [VMEM] * len(pieces),
        vmem=16,
        flops=half_rows * cycle * queries,
        moved=6 * half_rows * cycle * queries,
    )(*pieces)
    return total.reshape(half_rows, cycle, 1, queries)


def doc_matrix(lengths_row, count):
    ends = jnp.cumsum(lengths_row)
    starts = ends - lengths_row
    place = jnp.arange(count, dtype=jnp.int32)
    inside = (place[None, :] >= starts[:, None]) & (place[None, :] < ends[:, None])
    return inside.astype(jnp.bfloat16)


def solve_block(factor, rhs):
    return jax.scipy.linalg.cho_solve((factor, True), rhs)


def general(query_ids, query_delta, doc_lengths, vocab_factor, output_factor, train_grads):
    model_count = lax.axis_size("mp")
    model_index = lax.axis_index("mp")
    vocab_rows = vocab_factor.shape[0]
    local_ids = query_ids - model_index * vocab_rows
    owned = (local_ids >= 0) & (local_ids < vocab_rows)
    looked = vocab_factor[jnp.clip(local_ids, 0, vocab_rows - 1)].astype(jnp.float32)
    vocab_part = jnp.where(owned[:, None], looked, jnp.zeros_like(looked))
    output_part = jnp.dot(query_delta, output_factor, preferred_element_type=jnp.float32)
    input_side, output_side = lax.psum((vocab_part, output_part), "mp")
    proj = output_side.shape[1]
    rows_each = proj // model_count
    mine = lax.dynamic_slice_in_dim(output_side, model_index * rows_each, rows_each, 1)
    token_count = query_ids.shape[0]
    token_grads = (
        (mine[:, :, None] * input_side[:, None, :])
        .reshape(token_count, rows_each * proj)
        .astype(jnp.bfloat16)
    )
    query_grads = jnp.dot(
        doc_matrix(doc_lengths[0], token_count), token_grads, preferred_element_type=jnp.float32
    )
    train_rows, feat_dev = train_grads.shape
    nblocks = feat_dev // FBLK
    tiled = train_grads.reshape(train_rows, nblocks, FBLK)
    local_gram = jnp.einsum("tbi,tbj->bij", tiled, tiled, preferred_element_type=jnp.float32)
    total_gram = lax.psum(local_gram, "dp")
    fisher = total_gram / (train_rows * lax.axis_size("dp"))
    shift_amount = damping * (jnp.trace(fisher, axis1=1, axis2=2) / FBLK)
    damped = fisher + shift_amount[:, None, None] * jnp.eye(FBLK, dtype=jnp.float32)[None]
    factor = jnp.linalg.cholesky(damped)
    queries = query_grads.shape[0]
    rhs = jnp.transpose(query_grads.reshape(queries, nblocks, FBLK), (1, 2, 0))
    solved = jax.vmap(solve_block)(factor, rhs)
    pre = (jnp.transpose(solved, (2, 0, 1)).reshape(queries, feat_dev) / proj).astype(jnp.bfloat16)
    cycle = lax.axis_size("dp")
    everyone = lax.all_gather(pre, "dp", axis=0, tiled=True)
    scores = lax.dot_general(
        train_grads, everyone, (((1,), (1,)), ((), ())), preferred_element_type=jnp.float32
    )
    scores = scores.astype(jnp.bfloat16).reshape(train_rows, cycle, queries)
    summed = lax.psum_scatter(scores, "mp", scatter_dimension=0, tiled=True)
    return summed[:, :, None, :]


def per_device(query_ids, query_delta, doc_lengths, vocab_factor, output_factor, train_grads):
    owners = lax.axis_size("dp") * lax.axis_size("rep")
    fits = (
        train_grads.shape[1] == 2 * FBLK * owners
        and lax.axis_size("dp") == 4
        and lax.axis_size("mp") == 2
        and lax.axis_size("rep") == 2
        and doc_lengths.shape[1] == FBLK
        and vocab_factor.shape[0] % FBLK == 0
    )
    body = split_over_blocks if fits else general
    return body(query_ids, query_delta, doc_lengths, vocab_factor, output_factor, train_grads)


def solution(mesh):
    placed = (
        P(("groups", "dp", "rep")),
        P(("groups", "dp", "rep"), "mp"),
        P(("groups", "dp", "rep"), None),
        P("mp", None),
        P("mp", None),
        P(("groups", "dp"), "mp"),
    )
    return jax.shard_map(
        per_device,
        mesh=mesh,
        in_specs=placed,
        out_specs=P(("groups", "dp", "mp"), None, "rep", None),
        check_vma=False,
    )
```

```python
import functools
import jax
import jax.numpy as jnp
from jax import lax
from jax.experimental import pallas as pl
from jax.experimental.pallas import tpu as pltpu
from jax.sharding import PartitionSpec as P

FBLK = 128
SLAB = FBLK + 8
PANEL = 8
ROWS = 16

damping = 0.1

VMEM = pl.BlockSpec(memory_space=pltpu.VMEM)
SMEM = pl.BlockSpec(memory_space=pltpu.SMEM)
HBM = pl.BlockSpec(memory_space=pl.ANY)


def call(kernel, outs, in_specs, scratch=(), vmem=48, flops=0, moved=0):
    return pl.pallas_call(
        kernel,
        out_shape=outs,
        in_specs=in_specs,
        scratch_shapes=list(scratch),
        compiler_params=pltpu.CompilerParams(vmem_limit_bytes=vmem << 20),
        cost_estimate=pl.CostEstimate(flops=flops, bytes_accessed=moved, transcendentals=0),
    )


def swapped(shard, axis, by):
    return lax.ppermute(shard, axis, [(i, i ^ by) for i in range(lax.axis_size(axis))])


def square(dim):
    return lax.broadcasted_iota(jnp.int32, (FBLK, FBLK), dim)


def halves(value):
    high = value.astype(jnp.bfloat16)
    return high, (value - high.astype(jnp.float32)).astype(jnp.bfloat16)


def pack(first, second, spare=None):
    row, col = square(0), square(1)
    body = jnp.where(row >= col, first, second)
    diagonal = jnp.sum(jnp.where(row == col, second, 0.0), axis=0, keepdims=True)
    place = lax.broadcasted_iota(jnp.int32, (8, FBLK), 0)
    tail = jnp.where(place == 0, diagonal, 0.0)
    if spare is not None:
        tail = jnp.where(place == 1, spare, tail)
    return body, tail


def unpack(body, diagonal):
    row, col = square(0), square(1)
    turned = body.T
    first = jnp.where(row >= col, body, turned)
    second = jnp.where(row < col, body, jnp.where(row > col, turned, diagonal))
    return first, second


def grams(lengths, train, slabs):
    cycle = len(slabs)
    mine, half = lax.axis_index("dp"), lax.axis_index("rep")
    spare = lengths[...].astype(jnp.float32)
    for shift, slab in enumerate(slabs):
        owner = half * cycle + (mine ^ shift)
        start = pl.multiple_of(owner * (2 * FBLK), 2 * FBLK)
        part = train[:, pl.ds(start, 2 * FBLK)]
        gram = lax.dot_general(part, part, (((0,), (0,)), ((), ())), preferred_element_type=jnp.float32)
        body, tail = pack(gram[:FBLK, :FBLK], gram[FBLK:, FBLK:], spare)
        slab[pl.ds(0, FBLK), :] = body
        slab[pl.ds(FBLK, 8), :] = tail


def thirds(value):
    high = value.astype(jnp.bfloat16)
    rest = value - high.astype(jnp.float32)
    middle = rest.astype(jnp.bfloat16)
    return high, middle, (rest - middle.astype(jnp.float32)).astype(jnp.bfloat16)


def at_rows(panel, first):
    pair = 2 * PANEL
    blank = jnp.zeros((PANEL, FBLK), jnp.float32)
    panel = panel.astype(jnp.float32)
    piece = jnp.concatenate([panel, blank] if first % pair == 0 else [blank, panel], axis=0).astype(jnp.bfloat16)
    before = first // pair * pair
    pieces = [jnp.zeros((before, FBLK), jnp.bfloat16), piece, jnp.zeros((FBLK - before - pair, FBLK), jnp.bfloat16)]
    return jnp.concatenate([piece for piece in pieces if piece.shape[0]], axis=0)


def product(left, right, first):
    high, middle, low = thirds(left)
    right_high, right_middle, right_low = (at_rows(part, first) for part in thirds(right))
    both = jnp.concatenate([right_high, right_middle], axis=1)
    large = jnp.dot(
        jnp.concatenate([high, middle], axis=1), jnp.concatenate([both, both], axis=0),
        preferred_element_type=jnp.float32,
    )
    small = jnp.dot(
        jnp.concatenate([high, low], axis=1), jnp.concatenate([right_low, right_high], axis=0),
        preferred_element_type=jnp.float32,
    )
    return large[:, :FBLK] + (large[:, FBLK:] + small)


def eliminated(panel, first):
    lane = lax.broadcasted_iota(jnp.int32, (PANEL, FBLK), 1)
    sublane = lax.broadcasted_iota(jnp.int32, (PANEL, FBLK), 0)
    within = (lane >= first) & (lane < first + PANEL)
    count = range(PANEL)

    def across(value, row):
        return jnp.broadcast_to(value[row:row + 1, :], (PANEL, FBLK))

    columns = [jnp.broadcast_to(panel[:, first + j:first + j + 1], (PANEL, FBLK)) for j in count]
    pivots = [[across(columns[j], i) if j >= i else None for j in count] for i in count]
    rest = jnp.where(within, jnp.where(lane == first + sublane, 1.0, 0.0), panel)
    lines = [across(rest, i) for i in count]
    for i in count:
        scale = 1.0 / pivots[i][i]
        scaled = lines[i] * scale
        shares = [pivots[i][j] * scale if j > i else None for j in count]
        for m in range(i + 1, PANEL):
            lines[m] = lines[m] - pivots[i][m] * scaled
            for j in range(m, PANEL):
                pivots[m][j] = pivots[m][j] - shares[m] * pivots[i][j]
        lines[i] = scaled
        pivots[i] = shares
    for i in reversed(count):
        for m in range(i):
            lines[m] = lines[m] - pivots[m][i] * lines[i]
    result = lines[0]
    for i in range(1, PANEL):
        result = jnp.where(sublane == i, lines[i], result)
    return result


def inverted(blocks):
    lane = square(1)
    for first in range(0, FBLK, PANEL):
        within = (lane >= first) & (lane < first + PANEL)
        panels = [eliminated(block[first:first + PANEL, :], first) for block in blocks]
        updates = [product(block, panel, first) for block, panel in zip(blocks, panels)]
        rests = [jnp.where(within, 0.0, block) - update for block, update in zip(blocks, updates)]
        blocks = [
            jnp.concatenate(
                [part for part in (rest[:first], panel, rest[first + PANEL:]) if part.shape[0]], axis=0
            )
            for rest, panel in zip(rests, panels)
        ]
    return blocks


def factor_kernel(examples, scale, *refs):
    slabs, out = refs[:-2], refs[-1]
    body = slabs[0][pl.ds(0, FBLK), :]
    diagonal = slabs[0][pl.ds(FBLK, 1), :]
    for slab in slabs[1:]:
        body = body + slab[pl.ds(0, FBLK), :]
        diagonal = diagonal + slab[pl.ds(FBLK, 1), :]
    same = square(0) == square(1)
    damped = []
    for gram in unpack(body, diagonal):
        fisher = gram / examples
        trace = jnp.sum(jnp.sum(jnp.where(same, fisher, 0.0), axis=0, keepdims=True), axis=1, keepdims=True)
        damped.append(fisher + jnp.where(same, damping * (trace / FBLK), 0.0))
    first, second = inverted(damped)
    body, tail = pack(first * scale, second * scale)
    out[pl.ds(0, FBLK), :] = body
    out[pl.ds(FBLK, 8), :] = tail


def first_kernel(id_rows_hbm, delta_hbm, table_hbm, factor_hbm, lengths_hbm, train_hbm, sent, own, *refs):
    slabs, refs = refs[:-12], refs[-12:]
    id_rows, starts, rolls, start_of, roll_of, delta, table, factor, lengths, train, looked, sems = refs
    model = lax.axis_index("mp")
    proj, vocab_rows = table.shape
    tokens = delta.shape[0]
    each = proj // lax.axis_size("mp")
    groups = tokens // FBLK
    get_ids, get_factor, get_lengths, get_train = (
        pltpu.make_async_copy(source, target, sems.at[0, index])
        for index, (source, target) in enumerate((
            (id_rows_hbm, id_rows), (factor_hbm, factor), (lengths_hbm, lengths), (train_hbm, train),
        ))
    )
    get_table = [
        pltpu.make_async_copy(table_hbm.at[rows], table.at[rows], sems.at[1, index])
        for index in range(proj // ROWS) for rows in (pl.ds(index * ROWS, ROWS),)
    ]

    def get_delta(g):
        rows = pl.ds(pl.multiple_of(g * FBLK, FBLK), FBLK)
        return pltpu.make_async_copy(delta_hbm.at[rows], delta.at[rows], sems.at[2, g])

    for copy in (get_ids, get_lengths, get_train, *get_table, get_factor, *(get_delta(g) for g in range(groups))):
        copy.start()
    get_ids.wait()
    local = id_rows[...] - model * vocab_rows
    owned = (local >= 0) & (local < vocab_rows)
    local = jnp.where(owned, local, 0)
    low = FBLK - 1
    starts[...] = local & ~low
    rolls[...] = (lax.broadcasted_iota(jnp.int32, local.shape, 1) - local) & low
    fetches = [pltpu.make_async_copy(starts, start_of, sems.at[0, 4]), pltpu.make_async_copy(rolls, roll_of, sems.at[0, 5])]
    for fetch in fetches:
        fetch.start()
    get_lengths.wait()
    get_train.wait()
    grams(lengths, train, slabs)
    for fetch in fetches:
        fetch.wait()
    starts[...] = owned.astype(jnp.int32)
    for copy in get_table:
        copy.wait()
    get_factor.wait()
    lanes = lax.broadcasted_iota(jnp.int32, (ROWS, FBLK), 1)

    def group(g, carry):
        columns = pl.ds(pl.multiple_of(g * FBLK, FBLK), FBLK)
        get_delta(g).wait()
        output = lax.dot_general(
            delta[columns, :], factor[...], (((1,), (1,)), ((), ())), preferred_element_type=jnp.float32
        )
        looked[:, columns] = output.T
        gathered = [jnp.zeros((ROWS, FBLK), jnp.bfloat16) for _ in range(proj // ROWS)]
        for j in range(FBLK):
            start, by, here = pl.multiple_of(start_of[g, j], FBLK), roll_of[g, j], lanes == j
            for index in range(proj // ROWS):
                block = table[pl.ds(index * ROWS, ROWS), pl.ds(start, FBLK)]
                gathered[index] = jnp.where(here, pltpu.roll(block, by, 1), gathered[index])
        held = starts[pl.ds(g, 1), :].astype(jnp.float32)
        for index, value in enumerate(gathered):
            value = (value.astype(jnp.float32) * held).astype(jnp.bfloat16)
            rows = pl.ds(2 * each + index * ROWS, ROWS)
            sent[rows, columns] = value
            own[rows, columns] = value
        return carry

    lax.fori_loop(0, groups, group, 0)
    mine = looked[pl.ds(pl.multiple_of(model * each, each), each), :]
    other = looked[pl.ds(pl.multiple_of((1 - model) * each, each), each), :]
    for target, value in ((own, mine), (sent, other)):
        high, rest = halves(value)
        target[pl.ds(0, each), :] = high
        target[pl.ds(each, each), :] = rest


def merge_kernel(each, own, got, out):
    def value(ref):
        return ref[pl.ds(0, each), :].astype(jnp.float32) + ref[pl.ds(each, each), :].astype(jnp.float32)

    high, low = halves(value(own) + value(got))
    out[pl.ds(0, each), :] = high
    out[pl.ds(each, each), :] = low
    rows = pl.ds(2 * each, out.shape[0] - 2 * each)
    out[rows, :] = own[rows, :] + got[rows, :]


def queries_kernel(each, ends_of, factors, slab, *refs):
    far, refs = (refs[0], refs[1:]) if ends_of else (None, refs)
    high_out, low_out = refs[-2:]
    if len(refs) == 4:
        source, high_out, low_out, copy = refs
        copy[...] = source[...]
    tokens = factors.shape[1]
    proj = factors.shape[0] - 2 * each
    queries = high_out.shape[1]
    mine = lax.axis_index("dp")

    def part(first, count):
        value = factors[pl.ds(first, count), :].astype(jnp.float32)
        if ends_of:
            at_end = (mine == 0) | (mine == ends_of - 1)
            value = jnp.where(at_end, far[pl.ds(first, count), :].astype(jnp.float32), value)
        return value

    lengths = slab[pl.ds(FBLK + 1, 1), :]
    upto = jnp.where(square(0) <= square(1), 1.0, 0.0).astype(jnp.bfloat16)
    ends = lax.dot_general(
        jnp.broadcast_to(lengths, (8, queries)).astype(jnp.bfloat16), upto, (((1,), (0,)), ((), ())),
        preferred_element_type=jnp.float32,
    )[:1]
    starts = ends - lengths
    place = lax.broadcasted_iota(jnp.int32, (tokens, queries), 0).astype(jnp.float32)
    inside = jnp.where((place >= starts) & (place < ends), 1.0, 0.0).astype(jnp.bfloat16)
    output = part(0, each) + part(each, each)
    inputs = part(2 * each, proj)
    step = 16
    for start in range(0, each, step):
        grads = jnp.concatenate(
            [(inputs * output[r:r + 1, :]).astype(jnp.bfloat16) for r in range(start, start + step)], axis=0
        )
        summed = jnp.dot(grads, inside, preferred_element_type=jnp.float32)
        high, low = halves(summed)
        high_out[pl.ds(start * proj, step * proj), :] = high
        low_out[pl.ds(start * proj, step * proj), :] = low


def hand_kernel(count, *refs):
    for source, copy in zip(refs[:count], refs[-count:]):
        copy[...] = source[...]


def scores_kernel(cycle, count, *refs):
    own, peers = refs[:cycle], refs[cycle:2 * cycle]
    highs, lows = refs[2 * cycle:2 * cycle + count], refs[2 * cycle + count:2 * cycle + 2 * count]
    train, sent, pre = refs[2 * cycle + 2 * count:]
    mine, rep, model = lax.axis_index("dp"), lax.axis_index("rep"), lax.axis_index("mp")
    for half, slabs in ((rep, own), (1 - rep, peers)):
        for shift in range(cycle):
            owner = half * cycle + (mine ^ shift)
            slab = slabs[shift]
            blocks = unpack(slab[pl.ds(0, FBLK), :], slab[pl.ds(FBLK, 1), :])
            for index, block in enumerate(blocks):
                rows = pl.ds(pl.multiple_of(owner * (2 * FBLK) + index * FBLK, FBLK), FBLK)
                high, low = halves(block)
                right_high = jnp.concatenate([ref[rows, :] for ref in highs], axis=1)
                right_low = jnp.concatenate([ref[rows, :] for ref in lows], axis=1)
                solved = jnp.dot(
                    jnp.concatenate([high, high, low], axis=1),
                    jnp.concatenate([right_high, right_low, right_high], axis=0),
                    preferred_element_type=jnp.float32,
                )
                pre[rows, :] = solved.astype(jnp.bfloat16)
    half_rows = sent.shape[0]
    rows = pl.ds(pl.multiple_of((1 - model) * half_rows, half_rows), half_rows)
    sent[...] = jnp.dot(train[rows, :], pre[...], preferred_element_type=jnp.float32).astype(jnp.bfloat16)


def kept_kernel(train, pre, kept):
    half_rows = kept.shape[0]
    rows = pl.ds(pl.multiple_of(lax.axis_index("mp") * half_rows, half_rows), half_rows)
    kept[...] = jnp.dot(train[rows, :], pre[...], preferred_element_type=jnp.float32).astype(jnp.bfloat16)


def total_kernel(order, *refs):
    pieces, out = refs[:-1], refs[-1]
    mine, cycle = lax.axis_index("dp"), len(order)
    sums = {}
    for kept, got in zip(pieces[::2], pieces[1::2]):
        both = kept[...].astype(jnp.float32) + got[...].astype(jnp.float32)
        for index in range(both.shape[1] // FBLK):
            sums[order[len(sums)]] = both[:, index * FBLK:(index + 1) * FBLK]
    placed = []
    for source in range(cycle):
        shift = mine ^ source
        value = sums[0]
        for index in range(1, cycle):
            value = jnp.where(shift == index, sums[index], value)
        placed.append(value)
    out[...] = jnp.concatenate(placed, axis=1).astype(jnp.bfloat16)


def shape(dims, dtype):
    return jax.ShapeDtypeStruct(dims, dtype)


def split_over_blocks(query_ids, query_delta, doc_lengths, vocab_factor, output_factor, train_grads):
    cycle = lax.axis_size("dp")
    tokens, width = query_delta.shape
    proj = output_factor.shape[1]
    each = proj // lax.axis_size("mp")
    vocab_rows = vocab_factor.shape[0]
    train_rows, feat = train_grads.shape
    queries = doc_lengths.shape[1]
    bf16, f32 = jnp.bfloat16, jnp.float32

    sent, own, *slabs = call(
        first_kernel,
        [shape((2 * each + proj, tokens), bf16)] * 2 + [shape((SLAB, FBLK), f32)] * cycle,
        [HBM] * 6,
        [
            pltpu.VMEM((tokens // FBLK, FBLK), jnp.int32),
            pltpu.VMEM((tokens // FBLK, FBLK), jnp.int32),
            pltpu.VMEM((tokens // FBLK, FBLK), jnp.int32),
            pltpu.SMEM((tokens // FBLK, FBLK), jnp.int32),
            pltpu.SMEM((tokens // FBLK, FBLK), jnp.int32),
            pltpu.VMEM((tokens, width), bf16),
            pltpu.VMEM((proj, vocab_rows), bf16),
            pltpu.VMEM((proj, width), bf16),
            pltpu.VMEM((1, queries), jnp.int32),
            pltpu.VMEM((train_rows, feat), bf16),
            pltpu.VMEM((proj, tokens), f32),
            pltpu.SemaphoreType.DMA((3, 8)),
        ],
        vmem=62,
        flops=2 * tokens * width * proj,
        moved=2 * (tokens * width + proj * vocab_rows) * 2,
    )(
        query_ids.reshape(tokens // FBLK, FBLK), query_delta, vocab_factor.T, output_factor.T,
        doc_lengths, train_grads,
    )
    got = swapped(sent, "mp", 1)
    own, kept = call(
        functools.partial(hand_kernel, 2),
        [shape(own.shape, bf16), shape((SLAB, FBLK), f32)],
        [VMEM, VMEM],
        vmem=16,
        moved=4 * own.size,
    )(own, slabs[0])
    parts = [kept] + [swapped(slabs[s], "dp", s) for s in range(1, cycle)]

    factors = call(
        functools.partial(merge_kernel, each),
        shape(sent.shape, bf16),
        [VMEM, VMEM],
        vmem=16,
        flops=tokens * each,
        moved=8 * tokens * each * 4,
    )(own, got)
    late = cycle - 1
    gathered = [factors] + [swapped(factors, "dp", s) if s != late else None for s in range(1, cycle)]

    inverse = call(
        functools.partial(factor_kernel, train_rows * cycle, 1.0 / proj),
        shape((SLAB, FBLK), f32),
        [VMEM] * cycle + [HBM],
        vmem=16,
        flops=10 ** 10,
        moved=10 ** 6,
    )(*parts, factors)
    inverses = [inverse] + [swapped(inverse, "dp", s) for s in range(1, cycle)]
    copies = {0: [inverse], 1: [factors], 2: [gathered[2]]}
    highs, lows, far = {}, {}, []
    for s in range(cycle):
        extra = copies.get(s, far)
        copied = s in (1, 2)
        highs[s], lows[s], *again = call(
            functools.partial(queries_kernel, each, cycle if s == late else 0),
            [shape((feat, queries), bf16)] * 2 + [shape(factors.shape, bf16)] * copied,
            [VMEM, VMEM] + [HBM if s == 0 else VMEM] * len(extra),
            vmem=24,
            flops=2 * feat * tokens * queries,
            moved=6 * feat * queries,
        )(gathered[s], parts[s], *extra)
        if s == 1:
            gathered[late] = lax.ppermute(again[0], "dp", [(1, 2), (2, 1)])
        if s == 2:
            far = [lax.ppermute(again[0], "dp", [(1, 0), (2, 3)])]
    handed = list(inverses)
    handed[late] = call(
        functools.partial(hand_kernel, 1),
        shape((SLAB, FBLK), f32),
        [VMEM] + [HBM] * (cycle - 2),
        vmem=16,
        moved=8 * SLAB * FBLK,
    )(inverses[late], *[highs[s] for s in range(1, cycle) if s != late])
    peers = [swapped(slab, "rep", 1) for slab in handed]

    half_rows = train_rows // lax.axis_size("mp")
    pieces, order = [], []
    for chosen in ([s for s in range(cycle) if s != late], [late]):
        count = len(chosen)
        outgoing, solved = call(
            functools.partial(scores_kernel, cycle, count),
            [shape((half_rows, count * queries), bf16), shape((feat, count * queries), bf16)],
            [VMEM] * (2 * cycle + 2 * count + 1),
            vmem=24,
            flops=2 * train_rows * feat * count * queries,
            moved=8 * feat * queries * count,
        )(*inverses, *peers, *[highs[s] for s in chosen], *[lows[s] for s in chosen], train_grads)
        kept = call(
            kept_kernel,
            shape((half_rows, count * queries), bf16),
            [VMEM, VMEM],
            vmem=24,
            flops=train_rows * feat * count * queries,
            moved=2 * feat * (half_rows + count * queries),
        )(train_grads, solved)
        pieces += [kept, swapped(outgoing, "mp", 1)]
        order += chosen
    total = call(
        functools.partial(total_kernel, order),
        shape((half_rows, cycle * queries), bf16),
        [VMEM] * len(pieces),
        vmem=16,
        flops=half_rows * cycle * queries,
        moved=6 * half_rows * cycle * queries,
    )(*pieces)
    return total.reshape(half_rows, cycle, 1, queries)


def doc_matrix(lengths_row, count):
    ends = jnp.cumsum(lengths_row)
    starts = ends - lengths_row
    place = jnp.arange(count, dtype=jnp.int32)
    inside = (place[None, :] >= starts[:, None]) & (place[None, :] < ends[:, None])
    return inside.astype(jnp.bfloat16)


def solve_block(factor, rhs):
    return jax.scipy.linalg.cho_solve((factor, True), rhs)


def general(query_ids, query_delta, doc_lengths, vocab_factor, output_factor, train_grads):
    model_count = lax.axis_size("mp")
    model_index = lax.axis_index("mp")
    vocab_rows = vocab_factor.shape[0]
    local_ids = query_ids - model_index * vocab_rows
    owned = (local_ids >= 0) & (local_ids < vocab_rows)
    looked = vocab_factor[jnp.clip(local_ids, 0, vocab_rows - 1)].astype(jnp.float32)
    vocab_part = jnp.where(owned[:, None], looked, jnp.zeros_like(looked))
    output_part = jnp.dot(query_delta, output_factor, preferred_element_type=jnp.float32)
    input_side, output_side = lax.psum((vocab_part, output_part), "mp")
    proj = output_side.shape[1]
    rows_each = proj // model_count
    mine = lax.dynamic_slice_in_dim(output_side, model_index * rows_each, rows_each, 1)
    token_count = query_ids.shape[0]
    token_grads = (
        (mine[:, :, None] * input_side[:, None, :])
        .reshape(token_count, rows_each * proj)
        .astype(jnp.bfloat16)
    )
    query_grads = jnp.dot(
        doc_matrix(doc_lengths[0], token_count), token_grads, preferred_element_type=jnp.float32
    )
    train_rows, feat_dev = train_grads.shape
    nblocks = feat_dev // FBLK
    tiled = train_grads.reshape(train_rows, nblocks, FBLK)
    local_gram = jnp.einsum("tbi,tbj->bij", tiled, tiled, preferred_element_type=jnp.float32)
    total_gram = lax.psum(local_gram, "dp")
    fisher = total_gram / (train_rows * lax.axis_size("dp"))
    shift_amount = damping * (jnp.trace(fisher, axis1=1, axis2=2) / FBLK)
    damped = fisher + shift_amount[:, None, None] * jnp.eye(FBLK, dtype=jnp.float32)[None]
    factor = jnp.linalg.cholesky(damped)
    queries = query_grads.shape[0]
    rhs = jnp.transpose(query_grads.reshape(queries, nblocks, FBLK), (1, 2, 0))
    solved = jax.vmap(solve_block)(factor, rhs)
    pre = (jnp.transpose(solved, (2, 0, 1)).reshape(queries, feat_dev) / proj).astype(jnp.bfloat16)
    cycle = lax.axis_size("dp")
    everyone = lax.all_gather(pre, "dp", axis=0, tiled=True)
    scores = lax.dot_general(
        train_grads, everyone, (((1,), (1,)), ((), ())), preferred_element_type=jnp.float32
    )
    scores = scores.astype(jnp.bfloat16).reshape(train_rows, cycle, queries)
    summed = lax.psum_scatter(scores, "mp", scatter_dimension=0, tiled=True)
    return summed[:, :, None, :]


def per_device(query_ids, query_delta, doc_lengths, vocab_factor, output_factor, train_grads):
    owners = lax.axis_size("dp") * lax.axis_size("rep")
    fits = (
        train_grads.shape[1] == 2 * FBLK * owners
        and lax.axis_size("dp") == 4
        and lax.axis_size("mp") == 2
        and lax.axis_size("rep") == 2
        and doc_lengths.shape[1] == FBLK
        and vocab_factor.shape[0] % FBLK == 0
    )
    body = split_over_blocks if fits else general
    return body(query_ids, query_delta, doc_lengths, vocab_factor, output_factor, train_grads)


def solution(mesh):
    placed = (
        P(("groups", "dp", "rep")),
        P(("groups", "dp", "rep"), "mp"),
        P(("groups", "dp", "rep"), None),
        P("mp", None),
        P("mp", None),
        P(("groups", "dp"), "mp"),
    )
    return jax.shard_map(
        per_device,
        mesh=mesh,
        in_specs=placed,
        out_specs=P(("groups", "dp", "mp"), None, "rep", None),
        check_vma=False,
    )
```
